32 devices in a mesh: pb: 4 (over z), pa: 8 (over y, x, core).
Axes of the slice: x: 2, y: 2, z: 4, core: 2. Of those that a mesh axis runs over, the one named last changes fastest.
Arguments:
- query_states: bfloat16 [128, 32, 768], P(('pb', 'pa')), may hold values from -6 to 6
- passage_states: bfloat16 [1024, 180, 768], P(('pb', 'pa')), may hold values from -6 to 6
- head: bfloat16 [768, 128], replicated, may hold values from -0.21875 to 0.21875
- teacher: float32 [128, 32], P(('pb', 'pa')), may hold values from -8 to 8
- cand_owner: int32 [128, 32], P(('pb', 'pa')), may hold values from 0 to 31, all different within a row; in each aligned block of 4 rows (0 to 3, 4 to 7, ...) at most 4 rows name the same one
- cand_local: int32 [128, 32], P(('pb', 'pa')), may hold values from 0 to 31
- query_lengths: int32 [128], P(('pb', 'pa')), may hold values from 1 to 32, 3072 in all
- passage_lengths: int32 [1024], P(('pb', 'pa')), may hold values from 1 to 180, 122880 in all
Outputs:
- scores: float32 [128, 32], P(('pb', 'pa'))
- loss: float32 [], replicated
- head_grad: float32 [768, 128], replicated
The draws below stay inside these ranges and needn't reach their ends.
Inputs may be any that keep to these rules, and one draw needn't show every extreme that they name: `cand_owner`: each row names 32 different devices; among the rows of one device no device is named by more than 4 rows.
All inputs are finite; a program needn't handle non-finite values. No bound on the sum of `query_lengths` or of `passage_lengths` on one device may be relied on, other than what follows from the above.
Results may differ from the reference program's by a relative error of at most 0.0078.
Values may be sent and summed in bfloat16 or wider, within the bound.
A program may use at most 192 MiB of HBM per device.

```python
import math
import jax
import jax.numpy as jnp
import numpy as np
from jax import lax

H = 768
D = 128
QLEN = 32
PLEN = 180
K = 32
QDEV = 4
PDEV = 32
NQ = 128
NP = 1024
CAP = 4
DEVICES = 32


def with_ends(result, stream_key, least, largest):
    longest = result.shape.index(max(result.shape))
    spots = []
    for shift in (0, 1):
        where = [jax.random.randint(jax.random.fold_in(stream_key, axis), (), 0, length) for axis, length in enumerate(result.shape)]
        where[longest] = (where[longest] + shift) % result.shape[longest]
        spots.append(tuple(where))
    return result.at[spots[0]].set(least).at[spots[1]].set(largest)


def levels(stream_key, extent, shards, least, high):
    def one(position, parts):
        steps = jax.random.uniform(jax.random.fold_in(jax.random.fold_in(stream_key, 6), position), (parts,), jnp.float32, least / len(shards), high / len(shards))
        return jnp.repeat(jnp.exp(steps), extent[position] // parts).reshape((-1,) + (1,) * (len(extent) - position - 1))

    factor_of = one(*shards[0])
    for cut in shards[1:]:
        factor_of = factor_of * one(*cut)
    return factor_of


def length_profile(amount, total, reach, lean):
    loads = [(1 << 20) // math.isqrt(grade ** lean) + 1 for grade in range(2, amount + 1)]
    surplus, holding = total - reach - (amount - 1), [1] * (amount - 1)
    while surplus > 0:
        movable = [i for i in range(amount - 1) if holding[i] < reach]
        whole, left = sum([loads[i] for i in movable]), surplus
        for i in movable:
            more = min(reach - holding[i], max(1, left * loads[i] // whole), surplus)
            holding[i] = holding[i] + more
            surplus = surplus - more
    return np.array([reach] + holding)


def uneven_parts(key, count, total, most, slope):
    if count == 2:
        one = jax.random.randint(key, (), max(1, total - most), min(most, total - 1) + 1)
        return jnp.stack([one, total - one])
    lengths = jnp.asarray(length_profile(count, total, most, slope), jnp.int32)
    twos = (count - 1) // 2
    donor, receiver = lengths[1:1 + 2 * twos:2], lengths[2:2 + 2 * twos:2]
    slack = jnp.minimum(donor - 1, most - receiver)
    passed = jax.random.randint(jax.random.fold_in(key, 1), (twos,), 0, 1 << 20) % (slack + 1)
    lengths = lengths.at[1:1 + 2 * twos:2].set(donor - passed).at[2:2 + 2 * twos:2].set(receiver + passed)
    return lengths[jax.random.permutation(jax.random.fold_in(key, 2), count)]


def shared_out(own_key, own, number, rows, count, top, limit, skew):
    order = jax.random.permutation(own_key, count)
    heavy_load, usual = shares(count, rows * top, limit, skew, True), shares(count, rows * top, limit, skew, False)
    places = jnp.arange(count)

    def named(lengths, turn):
        used = int((lengths > 0).sum())
        fixed = max(1, used // 4)
        moved = fixed + (places - fixed + turn * (used - fixed)) % max(1, count - fixed)
        return jnp.zeros((count,), jnp.int32).at[order[jnp.where(places < fixed, places, moved)]].set(jnp.asarray(lengths, jnp.int32))

    lengths = jnp.where(number % 4 == 0, named(heavy_load, number // 4), named(usual, number - number // 4 - 1))
    mixed = jax.random.permutation(jax.random.fold_in(own, 3), count)
    donor, sink = mixed[0:count // 2 * 2:2], mixed[1:count // 2 * 2:2]
    margin = jnp.minimum(lengths[donor] - 1, limit - lengths[sink]) // 2
    margin = jnp.where((donor == order[0]) | (sink == order[0]) | (lengths[sink] == 0), 0, jnp.maximum(margin, 0))
    moved = jax.random.randint(jax.random.fold_in(own, 4), (count // 2,), 0, 1 << 20) % (margin + 1)
    lengths = lengths.at[donor].add(-moved).at[sink].add(moved)
    members = jnp.searchsorted(jnp.cumsum(lengths), jnp.arange(rows * top), side="right").astype(jnp.int32)
    table = members.reshape(top, rows).T
    table = table[jax.random.permutation(jax.random.fold_in(own, 1), rows)]
    turn = jax.random.randint(jax.random.fold_in(own, 2), (rows, 1), 0, top)
    return jnp.take_along_axis(table, (jnp.arange(top)[None, :] + turn) % top, axis=1)


def shares(amount, total, limit, lean, full):
    weights = [(1 << 20) // math.isqrt(standing ** lean) + 1 for standing in range(1, amount + 1)]
    largest = limit if full else min(limit, max(-(-total // amount), total * weights[0] // sum(weights)))
    least = 1 if total - largest >= amount - 1 else 0
    counts, spare = [largest] + [least] * (amount - 1), total - largest - least * (amount - 1)
    while spare > 0:
        candidates = [i for i in range(1, amount) if counts[i] < largest] or [i for i in range(1, amount) if counts[i] < limit]
        whole, budget = sum([weights[i] for i in candidates]), spare
        for i in candidates:
            more = min(limit - counts[i], max(1, budget * weights[i] // whole), spare)
            counts[i] = counts[i] + more
            spare = spare - more
    return np.array(counts)


def centred(key, extent, deviation, reach, split=(), kind=jnp.bfloat16):
    level = levels(key, extent, split, -0.22, 0.18) if split else 1.0
    values = jax.random.normal(key, extent, jnp.float32) * deviation * level
    return jnp.minimum(jnp.maximum(values, -reach), reach).astype(kind)


def setup_inputs(seed: int = 0) -> dict:
    key_of = jax.random.split(jax.random.key(seed), 9)
    query_states = centred(key_of[0], (NQ, QLEN, H), 1.0, 6.0, ((0, 32),))
    passage_states = centred(key_of[1], (NP, PLEN, H), 1.0, 6.0, ((0, 32),))
    head = centred(key_of[2], (H, D), H ** -0.5, 0.21875)
    teacher = centred(key_of[3], (NQ, K), 2.0, 8.0, ((0, 32),), jnp.float32)
    cand_owner_keys = jax.random.split(jax.random.fold_in(key_of[4], 1), NQ // QDEV)
    cand_owner_turns = jax.random.permutation(jax.random.fold_in(key_of[4], 3), NQ // QDEV)
    cand_owner = jax.vmap(lambda own, number: shared_out(jax.random.fold_in(key_of[4], 2), own, number, QDEV, DEVICES, K, CAP, 2))(cand_owner_keys, cand_owner_turns).reshape((NQ, K))
    cand_local = with_ends(jax.random.randint(key_of[5], (NQ, K), 0, PDEV), jax.random.fold_in(key_of[5], 1), 0, PDEV - 1).astype(jnp.int32)
    query_lengths = uneven_parts(key_of[6], NQ, NQ * QLEN * 3 // 4, QLEN, 2).astype(jnp.int32)
    passage_lengths = uneven_parts(key_of[7], NP, NP * PLEN * 2 // 3, PLEN, 2).astype(jnp.int32)
    return {"query_states": query_states, "passage_states": passage_states, "head": head, "teacher": teacher, "cand_owner": cand_owner, "cand_local": cand_local, "query_lengths": query_lengths, "passage_lengths": passage_lengths}


SOFTMAX_TEMP = 0.05
EPSILON = 1e-06

def embed(states, head):
    flat_states = states.reshape(-1, states.shape[-1])
    projected = jnp.dot(flat_states, head, preferred_element_type=jnp.float32)
    norm_value = jnp.sqrt(lax.optimization_barrier(jnp.sum(projected * projected, axis=-1, keepdims=True)) + EPSILON)
    unit_rows = projected / norm_value
    embedded = unit_rows.astype(jnp.bfloat16).reshape(states.shape[0], states.shape[1], -1)
    return (lax.optimization_barrier(embedded), unit_rows, norm_value)

def head_term(states, unit_rows, norm_value, grads):
    flat_states = states.reshape(unit_rows.shape[0], -1)
    along = grads.reshape(unit_rows.shape)
    radial = lax.optimization_barrier(jnp.sum(along * unit_rows, axis=-1, keepdims=True))
    grad_pre = ((along - unit_rows * radial) / norm_value).astype(jnp.bfloat16)
    return jnp.dot(flat_states.T, grad_pre, preferred_element_type=jnp.float32)

def pair_terms(query_rows, passage_rows, passage_token_mask):
    token_similarity = jnp.einsum('id,kjd->kij', query_rows.astype(jnp.float32), passage_rows.astype(jnp.float32))
    exponent_terms = jnp.exp(token_similarity / SOFTMAX_TEMP) * passage_token_mask[:, None, :]
    return (exponent_terms, lax.optimization_barrier(jnp.sum(exponent_terms, axis=-1)))

def distill(scores, teacher):
    student_exp = jnp.exp(scores)
    student_sum = lax.optimization_barrier(jnp.sum(student_exp, axis=-1, keepdims=True))
    teacher_exp = jnp.exp(teacher)
    teacher_sum = lax.optimization_barrier(jnp.sum(teacher_exp, axis=-1, keepdims=True))
    target = teacher_exp / teacher_sum
    divergence = lax.optimization_barrier(jnp.sum(target * (teacher - jnp.log(teacher_sum) - (scores - jnp.log(student_sum))), axis=-1))
    return (student_exp / student_sum - target, divergence)

def reference(query_states, passage_states, head, teacher, cand_owner, cand_local, query_lengths, passage_lengths):
    query_emb, query_unit, query_norm = embed(query_states, head)
    passage_emb, passage_unit, passage_norm = embed(passage_states, head)
    cand_ids = (cand_owner * PDEV + cand_local).astype(jnp.int32)
    query_token_mask = (jnp.arange(QLEN, dtype=jnp.int32)[None, :] < query_lengths[:, None]).astype(jnp.float32)
    passage_token_mask = (jnp.arange(PLEN, dtype=jnp.int32)[None, :] < passage_lengths[:, None]).astype(jnp.float32)

    def forward_one(inputs):
        query_rows, row_mask_vector, picked = inputs
        exponent_terms, exponent_total = pair_terms(query_rows, passage_emb[picked], passage_token_mask[picked])
        return lax.optimization_barrier(jnp.sum(row_mask_vector[None, :] * (SOFTMAX_TEMP * jnp.log(exponent_total)), axis=-1))
    scores = lax.map(forward_one, (query_emb, query_token_mask, cand_ids))
    weights, divergence = distill(scores, teacher)
    loss = jnp.sum(divergence) / NQ

    def backward_one(carry, inputs):
        query_rows, row_mask_vector, picked, weight_row = inputs
        passage_rows = passage_emb[picked]
        exponent_terms, exponent_total = pair_terms(query_rows, passage_rows, passage_token_mask[picked])
        share = ((weight_row[:, None] * row_mask_vector[None, :] / exponent_total)[:, :, None] * exponent_terms).astype(jnp.bfloat16)
        share = lax.optimization_barrier(share).astype(jnp.float32)
        query_part = jnp.einsum('kij,kjd->kid', share, passage_rows.astype(jnp.float32)).astype(jnp.bfloat16)
        passage_part = jnp.einsum('kij,id->kjd', share, query_rows.astype(jnp.float32)).astype(jnp.bfloat16)
        query_part, passage_part = lax.optimization_barrier((query_part, passage_part))
        carry = carry.at[picked].add(passage_part.astype(jnp.float32))
        return (carry, lax.optimization_barrier(jnp.sum(query_part.astype(jnp.float32), axis=0)))
    passage_grad, query_grad = lax.scan(backward_one, jnp.zeros((NP, PLEN, D), jnp.float32), (query_emb, query_token_mask, cand_ids, weights))
    head_grad = head_term(query_states, query_unit, query_norm, query_grad) + head_term(passage_states, passage_unit, passage_norm, passage_grad)
    return (scores, loss, head_grad)
```

```python
import functools

import jax
import jax.numpy as jnp
from jax import lax
from jax.experimental import pallas as pl
from jax.experimental.pallas import tpu as pltpu
from jax.sharding import PartitionSpec as P

MESH = pl.DeviceIdType.MESH
F32 = jnp.float32
BF16 = jnp.bfloat16
LANES = 128

SOFTMAX_TEMP = 0.05
EPSILON = 1e-06


def embed(states, head):
    flat_states = states.reshape(-1, states.shape[-1])
    projected = jnp.dot(flat_states, head, preferred_element_type=jnp.float32)
    norm_value = jnp.sqrt(jnp.sum(projected * projected, axis=-1, keepdims=True) + EPSILON)
    unit_rows = projected / norm_value
    embedded = unit_rows.astype(jnp.bfloat16).reshape(states.shape[0], states.shape[1], -1)
    return (embedded, unit_rows, norm_value)


def head_term(states, unit_rows, norm_value, grads):
    flat_states = states.reshape(unit_rows.shape[0], -1)
    along = grads.reshape(unit_rows.shape)
    radial = jnp.sum(along * unit_rows, axis=-1, keepdims=True)
    grad_pre = ((along - unit_rows * radial) / norm_value).astype(jnp.bfloat16)
    return lax.dot_general(
        flat_states, grad_pre, (((0,), (0,)), ((), ())), preferred_element_type=jnp.float32
    )


def length_mask(lengths, width_value):
    return (jnp.arange(width_value, dtype=jnp.int32)[None, :] < lengths[:, None]).astype(
        jnp.float32
    )


def pair_terms(query_rows, passage_rows, passage_token_mask):
    token_similarity = jnp.einsum(
        "sid,sjd->sij", query_rows, passage_rows, preferred_element_type=jnp.float32
    )
    exponent_terms = jnp.exp(token_similarity / SOFTMAX_TEMP) * passage_token_mask[:, None, :]
    return (exponent_terms, jnp.sum(exponent_terms, axis=-1))


def pair_scores(exponent_total, query_token_mask):
    return jnp.sum(query_token_mask * (SOFTMAX_TEMP * jnp.log(exponent_total)), axis=-1)


def pair_grads(exponent_terms, exponent_total, query_token_mask, weights, query_rows, passage_rows):
    share = (
        (weights[:, None] * query_token_mask / exponent_total)[:, :, None] * exponent_terms
    ).astype(jnp.bfloat16)
    query_part = jnp.einsum(
        "sij,sjd->sid", share, passage_rows, preferred_element_type=jnp.float32
    ).astype(jnp.bfloat16)
    passage_part = jnp.einsum(
        "sij,sid->sjd", share, query_rows, preferred_element_type=jnp.float32
    ).astype(jnp.bfloat16)
    return (query_part, passage_part)


def distill(scores, teacher):
    student_exp = jnp.exp(scores)
    student_sum = jnp.sum(student_exp, axis=-1, keepdims=True)
    teacher_exp = jnp.exp(teacher)
    teacher_sum = jnp.sum(teacher_exp, axis=-1, keepdims=True)
    target = teacher_exp / teacher_sum
    divergence = jnp.sum(
        target * (teacher - jnp.log(teacher_sum) - (scores - jnp.log(student_sum))), axis=-1
    )
    return (student_exp / student_sum - target, divergence)


def accumulate(parts, local_index, passages):
    onehot_rows = (local_index[:, None] == jnp.arange(passages, dtype=jnp.int32)[None, :]).astype(
        jnp.bfloat16
    )
    summed = jnp.einsum(
        "sp,sx->px",
        onehot_rows,
        parts.reshape(parts.shape[0], -1),
        preferred_element_type=jnp.float32,
    )
    return summed.reshape((passages,) + parts.shape[1:])


def slot_plan(owners, capacity, devices):
    hits = (owners[:, :, None] == jnp.arange(devices, dtype=jnp.int32)[None, None, :]).astype(
        jnp.int32
    )
    present = jnp.sum(hits, axis=1)
    earlier = jnp.cumsum(present, axis=0) - present
    rank_value = jnp.sum(hits * earlier[:, None, :], axis=2)
    return owners * capacity + rank_value


def on_device(
    query_states,
    passage_states,
    head,
    teacher,
    cand_owner,
    cand_local,
    query_lengths,
    passage_lengths,
):
    outer_size = lax.axis_size("pb")
    inner_size = lax.axis_size("pa")
    devices = outer_size * inner_size
    queries = query_states.shape[0]
    query_len = query_states.shape[1]
    passages = passage_states.shape[0]
    passage_len = passage_states.shape[1]
    candidates = cand_owner.shape[1]
    capacity = min(queries, max(2, 2 * queries * candidates // devices))
    slots = devices * capacity
    query_emb, query_unit, query_norm = embed(query_states, head)
    slot_index = slot_plan(cand_owner, capacity, devices)
    flat_slot = slot_index.reshape(-1)
    row_of = jnp.repeat(jnp.arange(queries, dtype=jnp.int32), candidates)
    slot_live = jnp.zeros((slots,), jnp.int32).at[flat_slot].set(1)
    slot_query = jnp.zeros((slots,), jnp.int32).at[flat_slot].set(row_of)
    slot_local = jnp.zeros((slots,), jnp.int32).at[flat_slot].set(cand_local.reshape(-1))
    passage_emb, passage_unit, passage_norm = embed(passage_states, head)
    sent_emb = query_emb.reshape(queries, -1)[slot_query]
    sent_len = query_lengths[slot_query] * slot_live
    got_emb, got_local, got_len = (
        lax.all_to_all(
            sent_emb.reshape(devices, capacity, -1),
            ("pb", "pa"),
            split_axis=0,
            concat_axis=0,
            tiled=True,
        ),
        lax.all_to_all(
            slot_local.reshape(devices, capacity),
            ("pb", "pa"),
            split_axis=0,
            concat_axis=0,
            tiled=True,
        ),
        lax.all_to_all(
            sent_len.reshape(devices, capacity),
            ("pb", "pa"),
            split_axis=0,
            concat_axis=0,
            tiled=True,
        ),
    )
    recv_emb = got_emb.reshape(slots, query_len, -1)
    recv_local = got_local.reshape(slots)
    recv_mask = length_mask(got_len.reshape(slots), query_len)
    passage_rows = passage_emb[recv_local]
    passage_token_mask = length_mask(passage_lengths[recv_local], passage_len)
    exponent_terms, exponent_total = pair_terms(recv_emb, passage_rows, passage_token_mask)
    slot_scores = pair_scores(exponent_total, recv_mask)
    returned_scores = lax.all_to_all(
        slot_scores.reshape(devices, capacity),
        ("pb", "pa"),
        split_axis=0,
        concat_axis=0,
        tiled=True,
    )
    scores = returned_scores.reshape(slots)[slot_index]
    weights, divergence = distill(scores, teacher)
    sent_weight = jnp.zeros((slots,), jnp.float32).at[flat_slot].set(weights.reshape(-1))
    recv_weight = lax.all_to_all(
        sent_weight.reshape(devices, capacity),
        ("pb", "pa"),
        split_axis=0,
        concat_axis=0,
        tiled=True,
    ).reshape(slots)
    query_part, passage_part = pair_grads(
        exponent_terms, exponent_total, recv_mask, recv_weight, recv_emb, passage_rows
    )
    passage_grad = accumulate(passage_part, recv_local, passages)
    returned_grads = lax.all_to_all(
        query_part.reshape(devices, capacity, -1),
        ("pb", "pa"),
        split_axis=0,
        concat_axis=0,
        tiled=True,
    )
    query_terms = returned_grads.reshape(slots, query_len, -1)[slot_index]
    query_grad = jnp.sum(query_terms.astype(jnp.float32), axis=1)
    local_grad = head_term(query_states, query_unit, query_norm, query_grad) + head_term(
        passage_states, passage_unit, passage_norm, passage_grad
    )
    head_grad, divergence_total = lax.psum((local_grad, jnp.sum(divergence)), ("pb", "pa"))
    loss = divergence_total / (queries * devices)
    return (scores, loss, head_grad)


def radices(size):
    found = []
    if (size.bit_length() - 1) % 2:
        found.append(2)
        size //= 2
    while size > 1:
        found.append(4)
        size //= 4
    return found


def exchange_stages(outer, inner):
    stages = []
    held = 1
    stride = 1
    for radix in radices(outer):
        stages.append(("pb", stride, radix, held))
        stride *= radix
        held *= radix
    inner_radices = radices(inner)
    strides = []
    stride = 1
    for radix in inner_radices:
        strides.append(stride)
        stride *= radix
    for radix, stride in zip(inner_radices[::-1], strides[::-1]):
        stages.append(("pa", stride, radix, held))
        held *= radix
    return stages


def rank_of(stages, coordinates):
    rank = 0
    for axis, stride, radix, held in stages:
        rank = rank + (coordinates[axis] // stride) % radix * held
    return rank


def here():
    return {"pb": lax.axis_index("pb"), "pa": lax.axis_index("pa")}


class Stage:
    def __init__(self, stage, at):
        self.axis, self.stride, self.radix, self.held = stage
        self.at = at
        self.digit = (at[self.axis] // self.stride) % self.radix

    def peers(self):
        found = []
        for step in range(1, self.radix):
            other = (self.digit + step) % self.radix
            place = dict(self.at)
            place[self.axis] = self.at[self.axis] + (other - self.digit) * self.stride
            found.append((step - 1, other, (place["pb"], place["pa"])))
        return found


def greet(stages):
    barrier = pltpu.get_barrier_semaphore()
    count = 0
    for stage in stages:
        for _, _, device in stage.peers():
            pl.semaphore_signal(barrier, inc=1, device_id=device, device_id_type=MESH)
            count += 1
    return barrier, count


def send(source, target, send_sem, recv_sem, device):
    copy = pltpu.make_async_remote_copy(
        src_ref=source,
        dst_ref=target,
        send_sem=send_sem,
        recv_sem=recv_sem,
        device_id=device,
        device_id_type=MESH,
    )
    copy.start()
    return copy


def gather_step(stage, rank, ref, unit, send_sems, recv_sems, base):
    first = rank // stage.held * stage.held * unit
    block = ref.at[pl.ds(first, stage.held * unit)]
    return [
        send(block, block, send_sems.at[base + slot], recv_sems.at[base + slot], device)
        for slot, _, device in stage.peers()
    ]


def reduce_step(stage, rank, ref, landing, unit, send_sems, recv_sems, base):
    span = stage.held * unit
    first = rank // (stage.held * stage.radix) * (stage.radix * span)
    return [
        send(
            ref.at[pl.ds(first + other * span, span)],
            landing.at[slot],
            send_sems.at[base + slot],
            recv_sems.at[base + slot],
            device,
        )
        for slot, other, device in stage.peers()
    ]


def finish(copies):
    for copy in copies:
        copy.wait()


def normal(pre):
    return lax.rsqrt(jnp.sum(pre * pre, axis=-1, keepdims=True) + EPSILON)


def embed_kernel(
    layout,
    chunk,
    query_ref,
    head_ref,
    meta_ref,
    states_ref,
    emb_ref,
    meta_all_ref,
    query_pre_ref,
    passage_emb_ref,
    passage_pre_ref,
    held_ref,
    load_sems,
    send_sems,
    recv_sems,
):
    at = here()
    stages = [Stage(stage, at) for stage in layout]
    rank = rank_of(layout, at)
    chunks = states_ref.shape[0] // chunk
    loads = []
    for index in range(chunks):
        part = pl.ds(index * chunk, chunk)
        load = pltpu.make_async_copy(states_ref.at[part], held_ref.at[part], load_sems.at[index])
        load.start()
        loads.append(load)
    barrier, count = greet(stages)
    queries = query_ref.shape[0]
    tokens = query_ref.shape[1]
    for index in range(queries):
        pre = jnp.dot(query_ref[index], head_ref[...], preferred_element_type=F32)
        query_pre_ref[index] = pre
        emb_ref[rank * queries + index] = (pre * normal(pre)).astype(BF16)
    meta_all_ref[rank] = meta_ref[...]
    pl.semaphore_wait(barrier, count)

    def project(index, carry):
        pre = jnp.dot(held_ref[index], head_ref[...], preferred_element_type=F32)
        passage_pre_ref[index] = pre.astype(BF16)
        passage_emb_ref[index] = (pre * normal(pre)).astype(BF16)
        return carry

    total = len(stages)
    base = 0
    done = 0
    for number, stage in enumerate(stages):
        flight = gather_step(stage, rank, emb_ref, queries, send_sems, recv_sems, base)
        base += stage.radix - 1
        flight += gather_step(stage, rank, meta_all_ref, 1, send_sems, recv_sems, base)
        base += stage.radix - 1
        until = chunks * (number + 1) // total
        for index in range(done, until):
            loads[index].wait()
            lax.fori_loop(index * chunk, (index + 1) * chunk, project, 0)
        done = until
        finish(flight)


def pair_kernel(
    layout,
    queries,
    table_ref,
    length_ref,
    emb_ref,
    passage_emb_ref,
    passage_pre_ref,
    query_pre_ref,
    target_ref,
    query_states_ref,
    states_ref,
    score_ref,
    loss_ref,
    head_grad_ref,
    held_ref,
    ratio_ref,
    column_ref,
    query_part_ref,
    sent_ref,
    running_ref,
    total_ref,
    head_part_ref,
    head_sum_ref,
    cross_ref,
    *rest,
):
    count = len(layout)
    landings = rest[:count]
    head_landings = rest[count : count + sum(1 for s in layout if s[0] == "pa")]
    load_sem, send_sems, recv_sems = rest[-3:]
    at = here()
    stages = [Stage(stage, at) for stage in layout]
    rank = rank_of(layout, at)
    load = pltpu.make_async_copy(states_ref, held_ref, load_sem)
    load.start()
    barrier, greeted = greet(stages)
    pairs, tokens, _ = emb_ref.shape
    passages, length, width = passage_emb_ref.shape

    def forward(pair, carry):
        local = table_ref[0, pair]
        rows = emb_ref[pair]
        sim = lax.dot_general(
            rows, passage_emb_ref[local], (((1,), (1,)), ((), ())), preferred_element_type=F32
        )
        column = lax.broadcasted_iota(jnp.int32, sim.shape, 1)
        exponent = jnp.where(column < length_ref[local], jnp.exp(sim / SOFTMAX_TEMP), 0.0)
        whole = jnp.sum(exponent, axis=-1, keepdims=True)
        live = lax.broadcasted_iota(jnp.int32, whole.shape, 0) < table_ref[1, pair]
        ratio_ref[pair] = (exponent * jnp.where(live, 1.0 / whole, 0.0)).astype(BF16)
        score = jnp.sum(
            jnp.where(live, SOFTMAX_TEMP * jnp.log(whole), 0.0), axis=0, keepdims=True
        )
        column_ref[pl.ds(pair, 1), :] = jnp.broadcast_to(score, (1, LANES))
        return carry

    lax.fori_loop(0, pairs, forward, 0, unroll=UNROLL)
    square = (LANES, LANES)
    diagonal = lax.broadcasted_iota(jnp.int32, square, 0) == lax.broadcasted_iota(
        jnp.int32, square, 1
    )
    score_ref[rank] = jnp.sum(
        jnp.where(diagonal, column_ref[...], 0.0), axis=0, keepdims=True
    )
    pl.semaphore_wait(barrier, greeted)

    def query_side(pair, carry):
        query_part_ref[pair] = jnp.dot(
            ratio_ref[pair], passage_emb_ref[table_ref[0, pair]], preferred_element_type=F32
        )
        return carry

    base = 0
    done = 0
    for number, stage in enumerate(stages):
        flight = gather_step(stage, rank, score_ref, 1, send_sems, recv_sems, base)
        base += stage.radix - 1
        until = pairs * (number + 1) // count
        lax.fori_loop(done, until, query_side, 0)
        done = until
        finish(flight)

    scores = score_ref[...].reshape(score_ref.shape[0], LANES)
    target = target_ref[...]
    student = jnp.exp(scores)
    student_sum = jnp.sum(student, axis=0, keepdims=True)
    share = jnp.exp(target)
    loss = jnp.sum(
        jnp.sum(share * (target - scores + jnp.log(student_sum)), axis=0, keepdims=True),
        axis=1,
        keepdims=True,
    )
    loss_ref[...] = jnp.broadcast_to(loss / pairs, loss_ref.shape)
    mine = lax.broadcasted_iota(jnp.int32, scores.shape, 0) == rank
    weight = jnp.sum(
        jnp.where(mine, student / student_sum - share, 0.0), axis=0, keepdims=True
    )
    upright = jnp.sum(
        jnp.where(diagonal, jnp.broadcast_to(weight, square), 0.0), axis=1, keepdims=True
    )
    column_ref[...] = jnp.broadcast_to(upright, square)

    def scale(pair, carry):
        sent_ref[pair] = (query_part_ref[pair] * column_ref[pl.ds(pair, 1), :]).astype(BF16)
        return carry

    lax.fori_loop(0, pairs, scale, 0, unroll=UNROLL)

    def reduce_start(number):
        stage = stages[number]
        return reduce_step(
            stage, rank, sent_ref, landings[number], queries, send_sems, recv_sems, bases[number]
        )

    def reduce_end(number, flight):
        finish(flight)
        stage = stages[number]
        landing = landings[number]
        first = rank // stage.held * stage.held * queries

        def add(index, carry):
            value = sent_ref[first + index].astype(F32)
            for slot in range(stage.radix - 1):
                value = value + landing[slot, index].astype(F32)
            if number:
                sent_ref[first + index] = value.astype(BF16)
            else:
                query_part_ref[index] = value
            return carry

        lax.fori_loop(0, stage.held * queries, add, 0, unroll=queries)

    bases = []
    for stage in stages:
        bases.append(base)
        base += stage.radix - 1

    flight = reduce_start(count - 1)

    def passage_side(place, carry):
        pair = table_ref[2, place]
        before = table_ref[2, jnp.maximum(place - 1, 0)]
        keep = jnp.where(table_ref[0, pair] == table_ref[0, before], 1.0, 0.0)
        part = lax.dot_general(
            ratio_ref[pair], emb_ref[pair], (((0,), (0,)), ((), ())), preferred_element_type=F32
        )
        grown = total_ref[...] * keep + part * column_ref[pl.ds(pair, 1), :]
        total_ref[...] = grown
        running_ref[place] = grown
        return carry

    def passage_head(index, carry):
        last = table_ref[3, index]
        keep = jnp.where(table_ref[0, table_ref[2, last]] == index, 1.0, 0.0)
        along = running_ref[last] * keep
        pre = passage_pre_ref[index].astype(F32)
        inverse = normal(pre)
        rows = pre * inverse
        radial = jnp.sum(along * rows, axis=-1, keepdims=True)
        grad = ((along - rows * radial) * inverse).astype(BF16)
        head_sum_ref[...] += lax.dot_general(
            grad, held_ref[index], (((0,), (0,)), ((), ())), preferred_element_type=F32
        )
        return carry

    total_ref[...] = jnp.zeros_like(total_ref)
    head_sum_ref[...] = jnp.zeros_like(head_sum_ref)
    load.wait()
    lax.fori_loop(0, pairs // 2, passage_side, 0)
    reduce_end(count - 1, flight)
    for number in range(count - 2, -1, -1):
        flight = reduce_start(number)
        if number == count - 2:
            lax.fori_loop(pairs // 2, pairs, passage_side, 0)
            lax.fori_loop(0, passages // 2, passage_head, 0)
        if number == 0:
            lax.fori_loop(passages // 2, passages, passage_head, 0)
        reduce_end(number, flight)

    for index in range(queries):
        along = query_part_ref[index]
        pre = query_pre_ref[index]
        inverse = normal(pre)
        rows = pre * inverse
        radial = jnp.sum(along * rows, axis=-1, keepdims=True)
        grad = ((along - rows * radial) * inverse).astype(BF16)
        head_sum_ref[...] += lax.dot_general(
            grad, query_states_ref[index], (((0,), (0,)), ((), ())), preferred_element_type=F32
        )

    chunks, rows_each, _ = head_part_ref.shape
    turned = jnp.transpose(head_sum_ref[...])
    for index in range(chunks):
        head_part_ref[index] = turned[index * rows_each : (index + 1) * rows_each].astype(BF16)

    outer_count = count - len(head_landings)
    outer_size = stages[outer_count].held
    chunk = rank // outer_size
    for number in range(count - 1, outer_count - 1, -1):
        stage = stages[number]
        landing = head_landings[number - outer_count]
        held = stage.held // outer_size
        first = chunk // (held * stage.radix) * (held * stage.radix)
        flight = [
            send(
                head_part_ref.at[pl.ds(first + other * held, held)],
                landing.at[slot],
                send_sems.at[base + slot],
                recv_sems.at[base + slot],
                device,
            )
            for slot, other, device in stage.peers()
        ]
        base += stage.radix - 1
        finish(flight)
        own = chunk // held * held
        for index in range(held):
            value = head_part_ref[own + index].astype(F32)
            for slot in range(stage.radix - 1):
                value = value + landing[slot, index].astype(F32)
            head_part_ref[own + index] = value.astype(BF16)

    place = 0
    for number in range(outer_count):
        stage = stages[number]
        cross_ref[place + stage.digit] = head_part_ref[chunk]
        flight = [
            send(
                cross_ref.at[place + stage.digit],
                cross_ref.at[place + stage.digit],
                send_sems.at[base + slot],
                recv_sems.at[base + slot],
                device,
            )
            for slot, _, device in stage.peers()
        ]
        base += stage.radix - 1
        finish(flight)
        value = cross_ref[place].astype(F32)
        for digit in range(1, stage.radix):
            value = value + cross_ref[place + digit].astype(F32)
        head_part_ref[chunk] = value.astype(BF16)
        place += stage.radix

    whole_ref = rest[-4]
    whole_ref[chunk] = head_part_ref[chunk]
    for number in range(outer_count, count):
        stage = stages[number]
        held = stage.held // outer_size
        block = whole_ref.at[pl.ds(chunk // held * held, held)]
        flight = [
            send(
                block, block, send_sems.at[base + slot], recv_sems.at[base + slot], device
            )
            for slot, _, device in stage.peers()
        ]
        base += stage.radix - 1
        finish(flight)
    for index in range(chunks):
        head_grad_ref[index * rows_each : (index + 1) * rows_each, :] = whole_ref[index].astype(F32)


UNROLL = 4


def on_device_dense(
    query_states,
    passage_states,
    head,
    teacher,
    cand_owner,
    cand_local,
    query_lengths,
    passage_lengths,
):
    outer = lax.axis_size("pb")
    inner = lax.axis_size("pa")
    devices = outer * inner
    queries, tokens, hidden = query_states.shape
    passages, length, _ = passage_states.shape
    width = head.shape[1]
    pairs = queries * devices
    layout = exchange_stages(outer, inner)
    rank = rank_of(layout, here())
    peers = sum(stage[2] - 1 for stage in layout)

    owner_rank = rank_of(layout, {"pb": cand_owner // inner, "pa": cand_owner % inner})
    hits = owner_rank[:, :, None] == jnp.arange(LANES, dtype=jnp.int32)[None, None, :]
    target = teacher - jnp.log(jnp.sum(jnp.exp(teacher), axis=-1, keepdims=True))
    code = (cand_local + passages * query_lengths[:, None]).astype(F32)
    meta = jnp.sum(
        jnp.where(hits[None], jnp.stack([target, code])[:, :, :, None], 0.0), axis=2
    ).reshape(2 * queries, LANES)

    vmem = pl.BlockSpec(memory_space=pltpu.VMEM)
    smem = pl.BlockSpec(memory_space=pltpu.SMEM)
    anywhere = pl.BlockSpec(memory_space=pl.ANY)
    chunk = 4 if passages % 4 == 0 else 1
    emb, meta_all, query_pre, passage_emb, passage_pre = pl.pallas_call(
        functools.partial(embed_kernel, layout, chunk),
        out_shape=[
            jax.ShapeDtypeStruct((pairs, tokens, width), BF16),
            jax.ShapeDtypeStruct((devices, 2 * queries, LANES), F32),
            jax.ShapeDtypeStruct((queries, tokens, width), F32),
            jax.ShapeDtypeStruct((passages, length, width), BF16),
            jax.ShapeDtypeStruct((passages, length, width), BF16),
        ],
        in_specs=[vmem, vmem, vmem, anywhere],
        out_specs=[vmem] * 5,
        scratch_shapes=[
            pltpu.VMEM(passage_states.shape, BF16),
            pltpu.SemaphoreType.DMA((passages // chunk,)),
            pltpu.SemaphoreType.DMA((2 * peers,)),
            pltpu.SemaphoreType.DMA((2 * peers,)),
        ],
        compiler_params=pltpu.CompilerParams(
            collective_id=0, has_side_effects=True, vmem_limit_bytes=40 * 2**20
        ),
    )(query_states, head, meta, passage_states)

    mine = (jnp.arange(LANES, dtype=jnp.int32) == rank).astype(F32)
    codes = jnp.sum(meta_all[:, queries:, :] * mine, axis=-1).astype(jnp.int32).reshape(pairs)
    local = codes % passages
    names = jnp.arange(pairs, dtype=jnp.int32)
    keys = local * pairs + names
    places = jnp.sum((keys[None, :] < keys[:, None]).astype(jnp.int32), axis=1)
    order = jnp.sum(
        jnp.where(places[:, None] == names[None, :], names[:, None], 0), axis=0
    )
    last = jnp.sum((local[None, :] <= names[:, None]).astype(jnp.int32), axis=1) - 1
    table = jnp.stack([local, codes // passages, order, jnp.maximum(last, 0)])
    target_all = meta_all[:, :queries, :devices].reshape(pairs, devices).T

    landings = [
        pltpu.VMEM((radix - 1, held * queries, tokens, width), BF16)
        for _, _, radix, held in layout
    ]
    chunks = inner
    rows_each = hidden // chunks
    head_landings = [
        pltpu.VMEM((radix - 1, held // outer, rows_each, width), BF16)
        for axis, _, radix, held in layout
        if axis == "pa"
    ]
    cross = sum(stage[2] for stage in layout if stage[0] == "pb")
    all_scores, loss, head_grad = pl.pallas_call(
        functools.partial(pair_kernel, layout, queries),
        out_shape=[
            jax.ShapeDtypeStruct((devices, 1, LANES), F32),
            jax.ShapeDtypeStruct((8, LANES), F32),
            jax.ShapeDtypeStruct((hidden, width), F32),
        ],
        in_specs=[smem, smem, vmem, vmem, vmem, vmem, vmem, vmem, anywhere],
        out_specs=[vmem] * 3,
        scratch_shapes=[
            pltpu.VMEM(passage_states.shape, BF16),
            pltpu.VMEM((pairs, tokens, length), BF16),
            pltpu.VMEM((LANES, LANES), F32),
            pltpu.VMEM((pairs, tokens, width), F32),
            pltpu.VMEM((pairs, tokens, width), BF16),
            pltpu.VMEM((pairs, length, width), F32),
            pltpu.VMEM((length, width), F32),
            pltpu.VMEM((chunks, rows_each, width), BF16),
            pltpu.VMEM((width, hidden), F32),
            pltpu.VMEM((cross, rows_each, width), BF16),
            *landings,
            *head_landings,
            pltpu.VMEM((chunks, rows_each, width), BF16),
            pltpu.SemaphoreType.DMA,
            pltpu.SemaphoreType.DMA((4 * peers,)),
            pltpu.SemaphoreType.DMA((4 * peers,)),
        ],
        compiler_params=pltpu.CompilerParams(
            collective_id=1, has_side_effects=True, vmem_limit_bytes=56 * 2**20
        ),
    )(
        table,
        passage_lengths,
        emb,
        passage_emb,
        passage_pre,
        query_pre,
        target_all,
        query_states,
        passage_states,
    )
    own = lax.dynamic_slice(
        all_scores.reshape(devices, pairs), (0, rank * queries), (devices, queries)
    )
    scores = jnp.sum(jnp.where(hits[:, :, :devices], own.T[:, None, :], 0.0), axis=2)
    return (scores, loss[0, 0], head_grad)


def suits_dense(mesh, arguments):
    outer, inner = mesh.shape["pb"], mesh.shape["pa"]
    devices = outer * inner
    queries = arguments[0].shape[0]
    hidden = arguments[0].shape[2]
    return (
        arguments[4].shape[1] == devices
        and queries == LANES
        and queries // devices == 4
        and outer & (outer - 1) == 0
        and inner & (inner - 1) == 0
        and hidden % (16 * inner) == 0
    )


def solution(mesh):
    def run(*arguments):
        body = on_device_dense if suits_dense(mesh, arguments) else on_device
        return placed(mesh, body)(*arguments)

    return run


def placed(mesh, body):
    return jax.shard_map(
        body,
        mesh=mesh,
        in_specs=(
            P(("pb", "pa"), None, None),
            P(("pb", "pa"), None, None),
            P(),
            P(("pb", "pa"), None),
            P(("pb", "pa"), None),
            P(("pb", "pa"), None),
            P(("pb", "pa")),
            P(("pb", "pa")),
        ),
        out_specs=(P(("pb", "pa"), None), P(), P()),
        check_vma=False,
    )
```

```python
import functools

import jax
import jax.numpy as jnp
from jax import lax
from jax.experimental import pallas as pl
from jax.experimental.pallas import tpu as pltpu
from jax.sharding import PartitionSpec as P

MESH = pl.DeviceIdType.MESH
F32 = jnp.float32
BF16 = jnp.bfloat16
LANES = 128

SOFTMAX_TEMP = 0.05
EPSILON = 1e-06


def embed(states, head):
    flat_states = states.reshape(-1, states.shape[-1])
    projected = jnp.dot(flat_states, head, preferred_element_type=jnp.float32)
    norm_value = jnp.sqrt(jnp.sum(projected * projected, axis=-1, keepdims=True) + EPSILON)
    unit_rows = projected / norm_value
    embedded = unit_rows.astype(jnp.bfloat16).reshape(states.shape[0], states.shape[1], -1)
    return (embedded, unit_rows, norm_value)


def head_term(states, unit_rows, norm_value, grads):
    flat_states = states.reshape(unit_rows.shape[0], -1)
    along = grads.reshape(unit_rows.shape)
    radial = jnp.sum(along * unit_rows, axis=-1, keepdims=True)
    grad_pre = ((along - unit_rows * radial) / norm_value).astype(jnp.bfloat16)
    return lax.dot_general(
        flat_states, grad_pre, (((0,), (0,)), ((), ())), preferred_element_type=jnp.float32
    )


def length_mask(lengths, width_value):
    return (jnp.arange(width_value, dtype=jnp.int32)[None, :] < lengths[:, None]).astype(
        jnp.float32
    )


def pair_terms(query_rows, passage_rows, passage_token_mask):
    token_similarity = jnp.einsum(
        "sid,sjd->sij", query_rows, passage_rows, preferred_element_type=jnp.float32
    )
    exponent_terms = jnp.exp(token_similarity / SOFTMAX_TEMP) * passage_token_mask[:, None, :]
    return (exponent_terms, jnp.sum(exponent_terms, axis=-1))


def pair_scores(exponent_total, query_token_mask):
    return jnp.sum(query_token_mask * (SOFTMAX_TEMP * jnp.log(exponent_total)), axis=-1)


def pair_grads(exponent_terms, exponent_total, query_token_mask, weights, query_rows, passage_rows):
    share = (
        (weights[:, None] * query_token_mask / exponent_total)[:, :, None] * exponent_terms
    ).astype(jnp.bfloat16)
    query_part = jnp.einsum(
        "sij,sjd->sid", share, passage_rows, preferred_element_type=jnp.float32
    ).astype(jnp.bfloat16)
    passage_part = jnp.einsum(
        "sij,sid->sjd", share, query_rows, preferred_element_type=jnp.float32
    ).astype(jnp.bfloat16)
    return (query_part, passage_part)


def distill(scores, teacher):
    student_exp = jnp.exp(scores)
    student_sum = jnp.sum(student_exp, axis=-1, keepdims=True)
    teacher_exp = jnp.exp(teacher)
    teacher_sum = jnp.sum(teacher_exp, axis=-1, keepdims=True)
    target = teacher_exp / teacher_sum
    divergence = jnp.sum(
        target * (teacher - jnp.log(teacher_sum) - (scores - jnp.log(student_sum))), axis=-1
    )
    return (student_exp / student_sum - target, divergence)


def accumulate(parts, local_index, passages):
    onehot_rows = (local_index[:, None] == jnp.arange(passages, dtype=jnp.int32)[None, :]).astype(
        jnp.bfloat16
    )
    summed = jnp.einsum(
        "sp,sx->px",
        onehot_rows,
        parts.reshape(parts.shape[0], -1),
        preferred_element_type=jnp.float32,
    )
    return summed.reshape((passages,) + parts.shape[1:])


def slot_plan(owners, capacity, devices):
    hits = (owners[:, :, None] == jnp.arange(devices, dtype=jnp.int32)[None, None, :]).astype(
        jnp.int32
    )
    present = jnp.sum(hits, axis=1)
    earlier = jnp.cumsum(present, axis=0) - present
    rank_value = jnp.sum(hits * earlier[:, None, :], axis=2)
    return owners * capacity + rank_value


def on_device(
    query_states,
    passage_states,
    head,
    teacher,
    cand_owner,
    cand_local,
    query_lengths,
    passage_lengths,
):
    outer_size = lax.axis_size("pb")
    inner_size = lax.axis_size("pa")
    devices = outer_size * inner_size
    queries = query_states.shape[0]
    query_len = query_states.shape[1]
    passages = passage_states.shape[0]
    passage_len = passage_states.shape[1]
    candidates = cand_owner.shape[1]
    capacity = min(queries, max(2, 2 * queries * candidates // devices))
    slots = devices * capacity
    query_emb, query_unit, query_norm = embed(query_states, head)
    slot_index = slot_plan(cand_owner, capacity, devices)
    flat_slot = slot_index.reshape(-1)
    row_of = jnp.repeat(jnp.arange(queries, dtype=jnp.int32), candidates)
    slot_live = jnp.zeros((slots,), jnp.int32).at[flat_slot].set(1)
    slot_query = jnp.zeros((slots,), jnp.int32).at[flat_slot].set(row_of)
    slot_local = jnp.zeros((slots,), jnp.int32).at[flat_slot].set(cand_local.reshape(-1))
    passage_emb, passage_unit, passage_norm = embed(passage_states, head)
    sent_emb = query_emb.reshape(queries, -1)[slot_query]
    sent_len = query_lengths[slot_query] * slot_live
    got_emb, got_local, got_len = (
        lax.all_to_all(
            sent_emb.reshape(devices, capacity, -1),
            ("pb", "pa"),
            split_axis=0,
            concat_axis=0,
            tiled=True,
        ),
        lax.all_to_all(
            slot_local.reshape(devices, capacity),
            ("pb", "pa"),
            split_axis=0,
            concat_axis=0,
            tiled=True,
        ),
        lax.all_to_all(
            sent_len.reshape(devices, capacity),
            ("pb", "pa"),
            split_axis=0,
            concat_axis=0,
            tiled=True,
        ),
    )
    recv_emb = got_emb.reshape(slots, query_len, -1)
    recv_local = got_local.reshape(slots)
    recv_mask = length_mask(got_len.reshape(slots), query_len)
    passage_rows = passage_emb[recv_local]
    passage_token_mask = length_mask(passage_lengths[recv_local], passage_len)
    exponent_terms, exponent_total = pair_terms(recv_emb, passage_rows, passage_token_mask)
    slot_scores = pair_scores(exponent_total, recv_mask)
    returned_scores = lax.all_to_all(
        slot_scores.reshape(devices, capacity),
        ("pb", "pa"),
        split_axis=0,
        concat_axis=0,
        tiled=True,
    )
    scores = returned_scores.reshape(slots)[slot_index]
    weights, divergence = distill(scores, teacher)
    sent_weight = jnp.zeros((slots,), jnp.float32).at[flat_slot].set(weights.reshape(-1))
    recv_weight = lax.all_to_all(
        sent_weight.reshape(devices, capacity),
        ("pb", "pa"),
        split_axis=0,
        concat_axis=0,
        tiled=True,
    ).reshape(slots)
    query_part, passage_part = pair_grads(
        exponent_terms, exponent_total, recv_mask, recv_weight, recv_emb, passage_rows
    )
    passage_grad = accumulate(passage_part, recv_local, passages)
    returned_grads = lax.all_to_all(
        query_part.reshape(devices, capacity, -1),
        ("pb", "pa"),
        split_axis=0,
        concat_axis=0,
        tiled=True,
    )
    query_terms = returned_grads.reshape(slots, query_len, -1)[slot_index]
    query_grad = jnp.sum(query_terms.astype(jnp.float32), axis=1)
    local_grad = head_term(query_states, query_unit, query_norm, query_grad) + head_term(
        passage_states, passage_unit, passage_norm, passage_grad
    )
    head_grad, divergence_total = lax.psum((local_grad, jnp.sum(divergence)), ("pb", "pa"))
    loss = divergence_total / (queries * devices)
    return (scores, loss, head_grad)


def radices(size):
    found = []
    if (size.bit_length() - 1) % 2:
        found.append(2)
        size //= 2
    while size > 1:
        found.append(4)
        size //= 4
    return found


def exchange_stages(outer, inner):
    stages = []
    held = 1
    stride = 1
    for radix in radices(outer):
        stages.append(("pb", stride, radix, held))
        stride *= radix
        held *= radix
    inner_radices = radices(inner)
    strides = []
    stride = 1
    for radix in inner_radices:
        strides.append(stride)
        stride *= radix
    for radix, stride in zip(inner_radices[::-1], strides[::-1]):
        stages.append(("pa", stride, radix, held))
        held *= radix
    return stages


def rank_of(stages, coordinates):
    rank = 0
    for axis, stride, radix, held in stages:
        rank = rank + (coordinates[axis] // stride) % radix * held
    return rank


def here():
    return {"pb": lax.axis_index("pb"), "pa": lax.axis_index("pa")}


class Stage:
    def __init__(self, stage, at):
        self.axis, self.stride, self.radix, self.held = stage
        self.at = at
        self.digit = (at[self.axis] // self.stride) % self.radix

    def peers(self):
        found = []
        for step in range(1, self.radix):
            other = (self.digit + step) % self.radix
            place = dict(self.at)
            place[self.axis] = self.at[self.axis] + (other - self.digit) * self.stride
            found.append((step - 1, other, (place["pb"], place["pa"])))
        return found


def greet(stages):
    barrier = pltpu.get_barrier_semaphore()
    count = 0
    for stage in stages:
        for _, _, device in stage.peers():
            pl.semaphore_signal(barrier, inc=1, device_id=device, device_id_type=MESH)
            count += 1
    return barrier, count


def send(source, target, send_sem, recv_sem, device):
    copy = pltpu.make_async_remote_copy(
        src_ref=source,
        dst_ref=target,
        send_sem=send_sem,
        recv_sem=recv_sem,
        device_id=device,
        device_id_type=MESH,
    )
    copy.start()
    return copy


def gather_step(stage, rank, ref, unit, send_sems, recv_sems, base):
    first = rank // stage.held * stage.held * unit
    block = ref.at[pl.ds(first, stage.held * unit)]
    return [
        send(block, block, send_sems.at[base + slot], recv_sems.at[base + slot], device)
        for slot, _, device in stage.peers()
    ]


def reduce_step(stage, rank, ref, landing, unit, send_sems, recv_sems, base):
    span = stage.held * unit
    first = rank // (stage.held * stage.radix) * (stage.radix * span)
    return [
        send(
            ref.at[pl.ds(first + other * span, span)],
            landing.at[slot],
            send_sems.at[base + slot],
            recv_sems.at[base + slot],
            device,
        )
        for slot, other, device in stage.peers()
    ]


def finish(copies):
    for copy in copies:
        copy.wait()


def normal(pre):
    return lax.rsqrt(jnp.sum(pre * pre, axis=-1, keepdims=True) + EPSILON)


def spread(values, lanes, columns):
    total = jnp.zeros((values.shape[0], LANES), values.dtype)
    for index in range(values.shape[1]):
        here_lane = lanes == columns[:, index : index + 1]
        total = total + jnp.where(here_lane, values[:, index : index + 1], 0)
    return total


def vector_rank(layout, owner, inner):
    bits = inner.bit_length() - 1
    parts = {"pb": owner >> bits, "pa": owner & (inner - 1)}
    rank = 0
    for axis, stride, radix, held in layout:
        digit = (parts[axis] >> (stride.bit_length() - 1)) & (radix - 1)
        rank = rank + digit * held
    return rank


def pair_row(pair, queries):
    return pair // queries * (2 * queries) + pair % queries


def step_kernel(
    layout,
    sizes,
    length_ref,
    query_length_ref,
    query_ref,
    head_ref,
    teacher_ref,
    owner_ref,
    local_ref,
    states_ref,
    score_ref,
    loss_ref,
    whole_ref,
    held_ref,
    pre_ref,
    query_pre_ref,
    passage_emb_ref,
    emb_ref,
    meta_ref,
    all_score_ref,
    turned_ref,
    table_ref,
    scalar_ref,
    ratio_ref,
    column_ref,
    query_part_ref,
    sent_ref,
    running_ref,
    total_ref,
    head_part_ref,
    head_sum_ref,
    cross_ref,
    *rest,
):
    outer, inner, parts = sizes
    count = len(layout)
    landings = rest[:count]
    head_landings = rest[count:-4]
    load_sems, table_sem, send_sems, recv_sems = rest[-4:]
    at = here()
    stages = [Stage(stage, at) for stage in layout]
    rank = rank_of(layout, at)
    length, passages, hidden = states_ref.shape
    queries, tokens, _ = query_ref.shape
    pairs = emb_ref.shape[0]
    width = head_ref.shape[1]
    rows = 2 * queries
    devices = pairs // queries
    step = length // parts
    span = step * passages

    loads = []
    for index in range(parts):
        part = pl.ds(index * step, step)
        load = pltpu.make_async_copy(states_ref.at[part], held_ref.at[part], load_sems.at[index])
        load.start()
        loads.append(load)
    barrier, greeted = greet(stages)

    for index in range(queries):
        pre = jnp.dot(query_ref[index], head_ref[...], preferred_element_type=F32)
        query_pre_ref[index] = pre
        emb_ref[rank * queries + index] = (pre * normal(pre)).astype(BF16)
    teacher = teacher_ref[...]
    target = teacher - jnp.log(jnp.sum(jnp.exp(teacher), axis=-1, keepdims=True))
    owner_rank = vector_rank(layout, owner_ref[...], inner)
    lanes = lax.broadcasted_iota(jnp.int32, (queries, LANES), 1)
    slot = lax.broadcasted_iota(jnp.int32, local_ref.shape, 0)
    code = local_ref[...]
    for index in range(queries):
        code = code + jnp.where(slot == index, query_length_ref[index] * passages, 0)
    meta_ref[rank, 0:queries, :] = spread(target, lanes, owner_rank)
    meta_ref[rank, queries:rows, :] = spread(code.astype(F32), lanes, owner_rank)
    pl.semaphore_wait(barrier, greeted)

    def project(index, carry):
        flat = held_ref[pl.ds(index * step, step)].reshape(span, hidden)
        pre_ref[pl.ds(pl.multiple_of(index * span, 8), span), :] = jnp.dot(
            flat, head_ref[...], preferred_element_type=F32
        )
        return carry

    def passage_pre(index):
        return pre_ref[pl.ds(index, length, stride=passages), :]

    def unit_rows(group, carry):
        for index in range(4):
            pre = passage_pre(group * 4 + index)
            passage_emb_ref[group * 4 + index] = (pre * normal(pre)).astype(BF16)
        return carry

    base = 0
    done = 0
    for number, stage in enumerate(stages):
        flight = gather_step(stage, rank, emb_ref, queries, send_sems, recv_sems, base)
        base += stage.radix - 1
        flight += gather_step(stage, rank, meta_ref, 1, send_sems, recv_sems, base)
        base += stage.radix - 1
        until = parts * (number + 1) // count
        for index in range(done, until):
            loads[index].wait()
            project(index, 0)
        done = until
        if number == count - 1:
            lax.fori_loop(0, passages // 4, unit_rows, 0)
        finish(flight)

    wide = devices * rows
    table = meta_ref[...].reshape(wide, LANES)
    turned = jnp.transpose(table)
    target = turned[:devices]
    column_code = jnp.sum(
        jnp.where(lax.broadcasted_iota(jnp.int32, table.shape, 1) == rank, table, 0.0),
        axis=1,
        keepdims=True,
    ).astype(jnp.int32)
    row_code = jnp.sum(
        jnp.where(lax.broadcasted_iota(jnp.int32, turned.shape, 0) == rank, turned, 0.0),
        axis=0,
        keepdims=True,
    ).astype(jnp.int32)
    low = passages.bit_length() - 1
    column_place = lax.broadcasted_iota(jnp.int32, (wide, 1), 0)
    row_place = lax.broadcasted_iota(jnp.int32, (1, wide), 1)
    column_valid = (column_place & (rows - 1)) >= queries
    row_valid = (row_place & (rows - 1)) >= queries
    column_local = jnp.where(column_valid, column_code & (passages - 1), passages)
    row_local = jnp.where(row_valid, row_code & (passages - 1), passages)
    column_key = column_local * wide + column_place
    row_key = row_local * wide + row_place
    place = jnp.sum((row_key < column_key).astype(jnp.int32), axis=1, keepdims=True)
    chosen = place == row_place
    pair_name = (column_place >> (rows.bit_length() - 1)) * queries + (
        column_place & (queries - 1)
    )
    table_ref[0:1, :] = row_code & (passages - 1)
    table_ref[1:2, :] = row_code >> low
    table_ref[2:3, :] = jnp.clip(
        jnp.sum(jnp.where(chosen, pair_name, 0), axis=0, keepdims=True), 0, pairs - 1
    )
    table_ref[3:4, :] = jnp.clip(
        jnp.sum((column_local <= row_place).astype(jnp.int32), axis=0, keepdims=True) - 1,
        0,
        pairs - 1,
    )
    table_ref[4:5, :] = jnp.sum(jnp.where(chosen, column_local, 0), axis=0, keepdims=True)
    to_scalar = pltpu.make_async_copy(table_ref, scalar_ref, table_sem)
    to_scalar.start()
    column_ref[...] = jnp.zeros_like(column_ref)
    to_scalar.wait()

    def local_of(pair):
        return scalar_ref[0, pair_row(pair, queries) + queries]

    def forward(group, carry):
        names = [group * queries + index for index in range(queries)]
        places = [local_of(name) for name in names]
        sim = jnp.concatenate(
            [
                lax.dot_general(
                    emb_ref[name],
                    passage_emb_ref[place],
                    (((1,), (1,)), ((), ())),
                    preferred_element_type=F32,
                )
                for name, place in zip(names, places)
            ],
            axis=0,
        )
        until = jnp.concatenate(
            [jnp.full((tokens, 1), length_ref[place], jnp.int32) for place in places], axis=0
        )
        alive = jnp.concatenate(
            [
                jnp.full((tokens, 1), scalar_ref[1, pair_row(name, queries) + queries], jnp.int32)
                for name in names
            ],
            axis=0,
        )
        exponent = jnp.where(
            lax.broadcasted_iota(jnp.int32, sim.shape, 1) < until, jnp.exp(sim / SOFTMAX_TEMP), 0.0
        )
        whole = jnp.sum(exponent, axis=-1, keepdims=True)
        live = (lax.broadcasted_iota(jnp.int32, whole.shape, 0) & (tokens - 1)) < alive
        ratio = (exponent * jnp.where(live, 1.0 / whole, 0.0)).astype(BF16)
        logs = jnp.where(live, SOFTMAX_TEMP * jnp.log(whole), 0.0)
        for index, name in enumerate(names):
            ratio_ref[name] = ratio[index * tokens : (index + 1) * tokens]
            column_ref[pl.ds(group * rows + index, 1), :] = jnp.broadcast_to(
                jnp.sum(logs[index * tokens : (index + 1) * tokens], axis=0, keepdims=True),
                (1, LANES),
            )
        return carry

    lax.fori_loop(0, devices, forward, 0, unroll=2)

    square = (LANES, LANES)
    diagonal = lax.broadcasted_iota(jnp.int32, square, 0) == lax.broadcasted_iota(
        jnp.int32, square, 1
    )
    blocks = wide // LANES
    all_score_ref[rank] = jnp.concatenate(
        [
            jnp.sum(
                jnp.where(diagonal, column_ref[block * LANES : (block + 1) * LANES], 0.0),
                axis=0,
                keepdims=True,
            )
            for block in range(blocks)
        ],
        axis=1,
    )

    def query_side(group, carry):
        names = [group * queries + index for index in range(queries)]
        found = [
            jnp.dot(ratio_ref[name], passage_emb_ref[local_of(name)], preferred_element_type=F32)
            for name in names
        ]
        for name, value in zip(names, found):
            query_part_ref[name] = value
        return carry

    done = 0
    for number, stage in enumerate(stages):
        flight = gather_step(stage, rank, all_score_ref, 1, send_sems, recv_sems, base)
        base += stage.radix - 1
        until = devices * (number + 1) // count
        lax.fori_loop(done, until, query_side, 0, unroll=2)
        done = until
        finish(flight)

    valid = (lax.broadcasted_iota(jnp.int32, (1, wide), 1) & (rows - 1)) < queries
    target = jnp.where(valid, target, 0.0)
    scores = jnp.where(valid, all_score_ref[...].reshape(devices, wide), 0.0)
    student = jnp.exp(scores)
    student_sum = jnp.sum(student, axis=0, keepdims=True)
    share = jnp.exp(target)
    mine = lax.broadcasted_iota(jnp.int32, scores.shape, 0) == rank
    weight = jnp.sum(
        jnp.where(mine, student / student_sum - share, 0.0), axis=0, keepdims=True
    )
    for block in range(blocks):
        upright = jnp.sum(
            jnp.where(
                diagonal,
                jnp.broadcast_to(weight[:, block * LANES : (block + 1) * LANES], square),
                0.0,
            ),
            axis=1,
            keepdims=True,
        )
        column_ref[block * LANES : (block + 1) * LANES] = jnp.broadcast_to(upright, square)

    def weight_of(pair):
        return column_ref[pl.ds(pair_row(pair, queries), 1), :]

    def scale(group, carry):
        for index in range(queries):
            pair = group * queries + index
            sent_ref[pair] = (query_part_ref[pair] * weight_of(pair)).astype(BF16)
        return carry

    lax.fori_loop(0, devices, scale, 0, unroll=2)

    bases = []
    for stage in stages:
        bases.append(base)
        base += stage.radix - 1

    def reduce_start(number):
        stage = stages[number]
        return reduce_step(
            stage, rank, sent_ref, landings[number], queries, send_sems, recv_sems, bases[number]
        )

    def reduce_end(number, flight):
        finish(flight)
        stage = stages[number]
        landing = landings[number]
        first = rank // stage.held * stage.held * queries

        def add(group, carry):
            for inner_index in range(queries):
                index = group * queries + inner_index
                value = sent_ref[first + index].astype(F32)
                for slot in range(stage.radix - 1):
                    value = value + landing[slot, index].astype(F32)
                if number:
                    sent_ref[first + index] = value.astype(BF16)
                else:
                    query_part_ref[index] = value
            return carry

        lax.fori_loop(0, stage.held, add, 0)

    def passage_side(group, carry):
        places = [group * 4 + index for index in range(4)]
        names = [scalar_ref[2, place] for place in places]
        found = [
            lax.dot_general(
                ratio_ref[name], emb_ref[name], (((0,), (0,)), ((), ())), preferred_element_type=F32
            )
            * weight_of(name)
            for name in names
        ]
        grown = total_ref[...]
        for place, value in zip(places, found):
            before = scalar_ref[4, jnp.maximum(place - 1, 0)]
            grown = grown * jnp.where(scalar_ref[4, place] == before, 1.0, 0.0) + value
            running_ref[place] = grown
        total_ref[...] = grown
        return carry

    def passage_grad(group, carry):
        for inner_index in range(4):
            index = group * 4 + inner_index
            last = scalar_ref[3, index]
            along = running_ref[last] * jnp.where(scalar_ref[4, last] == index, 1.0, 0.0)
            pre = passage_pre(index)
            inverse = normal(pre)
            unit = pre * inverse
            radial = jnp.sum(along * unit, axis=-1, keepdims=True)
            pre_ref[pl.ds(index, length, stride=passages), :] = (along - unit * radial) * inverse
        return carry

    def head_term(index, carry):
        head_sum_ref[...] += lax.dot_general(
            pre_ref[pl.ds(pl.multiple_of(index * span, 8), span), :].astype(BF16),
            held_ref[pl.ds(index * step, step)].reshape(span, hidden),
            (((0,), (0,)), ((), ())),
            preferred_element_type=F32,
        )
        return carry

    flight = reduce_start(count - 1)
    total_ref[...] = jnp.zeros_like(total_ref)
    head_sum_ref[...] = jnp.zeros_like(head_sum_ref)
    lax.fori_loop(0, pairs // 8, passage_side, 0)
    reduce_end(count - 1, flight)
    for number in range(count - 2, -1, -1):
        flight = reduce_start(number)
        if number == count - 2:
            lax.fori_loop(pairs // 8, pairs // 4, passage_side, 0)
            lax.fori_loop(0, passages // 4, passage_grad, 0)
        if number == 0:
            lax.fori_loop(0, parts, head_term, 0)
        reduce_end(number, flight)

    turned_ref[...] = jnp.zeros_like(turned_ref)
    turned_ref[:, 0:devices] = jnp.transpose(scores)
    own = turned_ref[pl.ds(pl.multiple_of(rank * rows, rows), rows), :][:queries]
    picked = jnp.zeros(owner_rank.shape, F32)
    for device in range(devices):
        picked = picked + jnp.where(owner_rank == device, own[:, device : device + 1], 0.0)
    score_ref[...] = picked
    loss = jnp.sum(
        jnp.sum(
            jnp.where(valid, share * (target - scores + jnp.log(student_sum)), 0.0),
            axis=0,
            keepdims=True,
        ),
        axis=1,
        keepdims=True,
    )
    loss_ref[...] = jnp.broadcast_to(loss / pairs, loss_ref.shape)

    for index in range(queries):
        along = query_part_ref[index]
        pre = query_pre_ref[index]
        inverse = normal(pre)
        unit = pre * inverse
        radial = jnp.sum(along * unit, axis=-1, keepdims=True)
        grad = ((along - unit * radial) * inverse).astype(BF16)
        head_sum_ref[...] += lax.dot_general(
            grad, query_ref[index], (((0,), (0,)), ((), ())), preferred_element_type=F32
        )

    chunks, rows_each, _ = head_part_ref.shape
    upright = jnp.transpose(head_sum_ref[...])
    for index in range(chunks):
        head_part_ref[index] = upright[index * rows_each : (index + 1) * rows_each].astype(BF16)

    outer_count = count - len(head_landings)
    chunk = rank // outer
    for number in range(count - 1, outer_count - 1, -1):
        stage = stages[number]
        landing = head_landings[number - outer_count]
        held = stage.held // outer
        first = chunk // (held * stage.radix) * (held * stage.radix)
        flight = [
            send(
                head_part_ref.at[pl.ds(first + other * held, held)],
                landing.at[slot],
                send_sems.at[base + slot],
                recv_sems.at[base + slot],
                device,
            )
            for slot, other, device in stage.peers()
        ]
        base += stage.radix - 1
        finish(flight)
        own = chunk // held * held
        for index in range(held):
            value = head_part_ref[own + index].astype(F32)
            for slot in range(stage.radix - 1):
                value = value + landing[slot, index].astype(F32)
            head_part_ref[own + index] = value.astype(BF16)

    place = 0
    for number in range(outer_count):
        stage = stages[number]
        cross_ref[place + stage.digit] = head_part_ref[chunk]
        flight = [
            send(
                cross_ref.at[place + stage.digit],
                cross_ref.at[place + stage.digit],
                send_sems.at[base + slot],
                recv_sems.at[base + slot],
                device,
            )
            for slot, _, device in stage.peers()
        ]
        base += stage.radix - 1
        finish(flight)
        value = cross_ref[place].astype(F32)
        for digit in range(1, stage.radix):
            value = value + cross_ref[place + digit].astype(F32)
        head_part_ref[chunk] = value.astype(BF16)
        place += stage.radix

    whole_ref[chunk] = head_part_ref[chunk]
    for number in range(outer_count, count):
        stage = stages[number]
        held = stage.held // outer
        block = whole_ref.at[pl.ds(chunk // held * held, held)]
        flight = [
            send(block, block, send_sems.at[base + slot], recv_sems.at[base + slot], device)
            for slot, _, device in stage.peers()
        ]
        base += stage.radix - 1
        finish(flight)


def on_device_dense(
    query_states,
    passage_states,
    head,
    teacher,
    cand_owner,
    cand_local,
    query_lengths,
    passage_lengths,
):
    outer = lax.axis_size("pb")
    inner = lax.axis_size("pa")
    devices = outer * inner
    queries, tokens, hidden = query_states.shape
    passages, length, _ = passage_states.shape
    width = head.shape[1]
    pairs = queries * devices
    wide = 2 * pairs
    layout = exchange_stages(outer, inner)
    peers = sum(stage[2] - 1 for stage in layout)
    parts = 10 if length % 10 == 0 else 1

    vmem = pl.BlockSpec(memory_space=pltpu.VMEM)
    smem = pl.BlockSpec(memory_space=pltpu.SMEM)
    anywhere = pl.BlockSpec(memory_space=pl.ANY)
    landings = [
        pltpu.VMEM((radix - 1, held * queries, tokens, width), BF16)
        for _, _, radix, held in layout
    ]
    chunks = inner
    rows_each = hidden // chunks
    head_landings = [
        pltpu.VMEM((radix - 1, held // outer, rows_each, width), BF16)
        for axis, _, radix, held in layout
        if axis == "pa"
    ]
    cross = sum(stage[2] for stage in layout if stage[0] == "pb")
    scores, loss, head_grad = pl.pallas_call(
        functools.partial(step_kernel, layout, (outer, inner, parts)),
        out_shape=[
            jax.ShapeDtypeStruct(teacher.shape, F32),
            jax.ShapeDtypeStruct((8, LANES), F32),
            jax.ShapeDtypeStruct((chunks, rows_each, width), BF16),
        ],
        in_specs=[smem, smem, vmem, vmem, vmem, vmem, vmem, anywhere],
        out_specs=[vmem] * 3,
        scratch_shapes=[
            pltpu.VMEM((length, passages, hidden), BF16),
            pltpu.VMEM(((length + 1) * passages, width), F32),
            pltpu.VMEM((queries, tokens, width), F32),
            pltpu.VMEM((passages, length, width), BF16),
            pltpu.VMEM((pairs, tokens, width), BF16),
            pltpu.VMEM((devices, 2 * queries, LANES), F32),
            pltpu.VMEM((devices, 1, wide), F32),
            pltpu.VMEM((wide, LANES), F32),
            pltpu.VMEM((8, wide), jnp.int32),
            pltpu.SMEM((8, wide), jnp.int32),
            pltpu.VMEM((pairs, tokens, length), BF16),
            pltpu.VMEM((wide, LANES), F32),
            pltpu.VMEM((pairs, tokens, width), F32),
            pltpu.VMEM((pairs, tokens, width), BF16),
            pltpu.VMEM((pairs, length, width), F32),
            pltpu.VMEM((length, width), F32),
            pltpu.VMEM((chunks, rows_each, width), BF16),
            pltpu.VMEM((width, hidden), F32),
            pltpu.VMEM((cross, rows_each, width), BF16),
            *landings,
            *head_landings,
            pltpu.SemaphoreType.DMA((parts,)),
            pltpu.SemaphoreType.DMA,
            pltpu.SemaphoreType.DMA((6 * peers,)),
            pltpu.SemaphoreType.DMA((6 * peers,)),
        ],
        compiler_params=pltpu.CompilerParams(
            collective_id=0, has_side_effects=True, vmem_limit_bytes=56 * 2**20
        ),
    )(
        passage_lengths,
        query_lengths,
        query_states,
        head,
        teacher,
        cand_owner,
        cand_local,
        jnp.transpose(passage_states, (1, 0, 2)),
    )
    return (scores, loss[0, 0], head_grad.astype(F32).reshape(hidden, width))


def suits_dense(mesh, arguments):
    outer, inner = mesh.shape["pb"], mesh.shape["pa"]
    devices = outer * inner
    queries = arguments[0].shape[0]
    hidden = arguments[0].shape[2]
    return (
        arguments[4].shape[1] == devices
        and queries == LANES
        and queries // devices == 4
        and outer & (outer - 1) == 0
        and inner & (inner - 1) == 0
        and hidden % (16 * inner) == 0
        and arguments[0].shape[1] == 32
        and arguments[1].shape[0] // devices in (16, 32, 64)
        and arguments[1].shape[1] * (arguments[1].shape[0] // devices) % 8 == 0
        and arguments[2].shape[1] == LANES
    )


def solution(mesh):
    def run(*arguments):
        body = on_device_dense if suits_dense(mesh, arguments) else on_device
        return placed(mesh, body)(*arguments)

    return run


def placed(mesh, body):
    return jax.shard_map(
        body,
        mesh=mesh,
        in_specs=(
            P(("pb", "pa"), None, None),
            P(("pb", "pa"), None, None),
            P(),
            P(("pb", "pa"), None),
            P(("pb", "pa"), None),
            P(("pb", "pa"), None),
            P(("pb", "pa")),
            P(("pb", "pa")),
        ),
        out_specs=(P(("pb", "pa"), None), P(), P()),
        check_vma=False,
    )
```

```python
import functools

import jax
import jax.numpy as jnp
from jax import lax
from jax.experimental import pallas as pl
from jax.experimental.pallas import tpu as pltpu
from jax.sharding import PartitionSpec as P

MESH = pl.DeviceIdType.MESH
F32 = jnp.float32
BF16 = jnp.bfloat16
LANES = 128

SOFTMAX_TEMP = 0.05
EPSILON = 1e-06


def embed(states, head):
    flat_states = states.reshape(-1, states.shape[-1])
    projected = jnp.dot(flat_states, head, preferred_element_type=jnp.float32)
    norm_value = jnp.sqrt(jnp.sum(projected * projected, axis=-1, keepdims=True) + EPSILON)
    unit_rows = projected / norm_value
    embedded = unit_rows.astype(jnp.bfloat16).reshape(states.shape[0], states.shape[1], -1)
    return (embedded, unit_rows, norm_value)


def head_term(states, unit_rows, norm_value, grads):
    flat_states = states.reshape(unit_rows.shape[0], -1)
    along = grads.reshape(unit_rows.shape)
    radial = jnp.sum(along * unit_rows, axis=-1, keepdims=True)
    grad_pre = ((along - unit_rows * radial) / norm_value).astype(jnp.bfloat16)
    return lax.dot_general(
        flat_states, grad_pre, (((0,), (0,)), ((), ())), preferred_element_type=jnp.float32
    )


def length_mask(lengths, width_value):
    return (jnp.arange(width_value, dtype=jnp.int32)[None, :] < lengths[:, None]).astype(
        jnp.float32
    )


def pair_terms(query_rows, passage_rows, passage_token_mask):
    token_similarity = jnp.einsum(
        "sid,sjd->sij", query_rows, passage_rows, preferred_element_type=jnp.float32
    )
    exponent_terms = jnp.exp(token_similarity / SOFTMAX_TEMP) * passage_token_mask[:, None, :]
    return (exponent_terms, jnp.sum(exponent_terms, axis=-1))


def pair_scores(exponent_total, query_token_mask):
    return jnp.sum(query_token_mask * (SOFTMAX_TEMP * jnp.log(exponent_total)), axis=-1)


def pair_grads(exponent_terms, exponent_total, query_token_mask, weights, query_rows, passage_rows):
    share = (
        (weights[:, None] * query_token_mask / exponent_total)[:, :, None] * exponent_terms
    ).astype(jnp.bfloat16)
    query_part = jnp.einsum(
        "sij,sjd->sid", share, passage_rows, preferred_element_type=jnp.float32
    ).astype(jnp.bfloat16)
    passage_part = jnp.einsum(
        "sij,sid->sjd", share, query_rows, preferred_element_type=jnp.float32
    ).astype(jnp.bfloat16)
    return (query_part, passage_part)


def distill(scores, teacher):
    student_exp = jnp.exp(scores)
    student_sum = jnp.sum(student_exp, axis=-1, keepdims=True)
    teacher_exp = jnp.exp(teacher)
    teacher_sum = jnp.sum(teacher_exp, axis=-1, keepdims=True)
    target = teacher_exp / teacher_sum
    divergence = jnp.sum(
        target * (teacher - jnp.log(teacher_sum) - (scores - jnp.log(student_sum))), axis=-1
    )
    return (student_exp / student_sum - target, divergence)


def accumulate(parts, local_index, passages):
    onehot_rows = (local_index[:, None] == jnp.arange(passages, dtype=jnp.int32)[None, :]).astype(
        jnp.bfloat16
    )
    summed = jnp.einsum(
        "sp,sx->px",
        onehot_rows,
        parts.reshape(parts.shape[0], -1),
        preferred_element_type=jnp.float32,
    )
    return summed.reshape((passages,) + parts.shape[1:])


def slot_plan(owners, capacity, devices):
    hits = (owners[:, :, None] == jnp.arange(devices, dtype=jnp.int32)[None, None, :]).astype(
        jnp.int32
    )
    present = jnp.sum(hits, axis=1)
    earlier = jnp.cumsum(present, axis=0) - present
    rank_value = jnp.sum(hits * earlier[:, None, :], axis=2)
    return owners * capacity + rank_value


def on_device(
    query_states,
    passage_states,
    head,
    teacher,
    cand_owner,
    cand_local,
    query_lengths,
    passage_lengths,
):
    outer_size = lax.axis_size("pb")
    inner_size = lax.axis_size("pa")
    devices = outer_size * inner_size
    queries = query_states.shape[0]
    query_len = query_states.shape[1]
    passages = passage_states.shape[0]
    passage_len = passage_states.shape[1]
    candidates = cand_owner.shape[1]
    capacity = min(queries, max(2, 2 * queries * candidates // devices))
    slots = devices * capacity
    query_emb, query_unit, query_norm = embed(query_states, head)
    slot_index = slot_plan(cand_owner, capacity, devices)
    flat_slot = slot_index.reshape(-1)
    row_of = jnp.repeat(jnp.arange(queries, dtype=jnp.int32), candidates)
    slot_live = jnp.zeros((slots,), jnp.int32).at[flat_slot].set(1)
    slot_query = jnp.zeros((slots,), jnp.int32).at[flat_slot].set(row_of)
    slot_local = jnp.zeros((slots,), jnp.int32).at[flat_slot].set(cand_local.reshape(-1))
    passage_emb, passage_unit, passage_norm = embed(passage_states, head)
    sent_emb = query_emb.reshape(queries, -1)[slot_query]
    sent_len = query_lengths[slot_query] * slot_live
    got_emb, got_local, got_len = (
        lax.all_to_all(
            sent_emb.reshape(devices, capacity, -1),
            ("pb", "pa"),
            split_axis=0,
            concat_axis=0,
            tiled=True,
        ),
        lax.all_to_all(
            slot_local.reshape(devices, capacity),
            ("pb", "pa"),
            split_axis=0,
            concat_axis=0,
            tiled=True,
        ),
        lax.all_to_all(
            sent_len.reshape(devices, capacity),
            ("pb", "pa"),
            split_axis=0,
            concat_axis=0,
            tiled=True,
        ),
    )
    recv_emb = got_emb.reshape(slots, query_len, -1)
    recv_local = got_local.reshape(slots)
    recv_mask = length_mask(got_len.reshape(slots), query_len)
    passage_rows = passage_emb[recv_local]
    passage_token_mask = length_mask(passage_lengths[recv_local], passage_len)
    exponent_terms, exponent_total = pair_terms(recv_emb, passage_rows, passage_token_mask)
    slot_scores = pair_scores(exponent_total, recv_mask)
    returned_scores = lax.all_to_all(
        slot_scores.reshape(devices, capacity),
        ("pb", "pa"),
        split_axis=0,
        concat_axis=0,
        tiled=True,
    )
    scores = returned_scores.reshape(slots)[slot_index]
    weights, divergence = distill(scores, teacher)
    sent_weight = jnp.zeros((slots,), jnp.float32).at[flat_slot].set(weights.reshape(-1))
    recv_weight = lax.all_to_all(
        sent_weight.reshape(devices, capacity),
        ("pb", "pa"),
        split_axis=0,
        concat_axis=0,
        tiled=True,
    ).reshape(slots)
    query_part, passage_part = pair_grads(
        exponent_terms, exponent_total, recv_mask, recv_weight, recv_emb, passage_rows
    )
    passage_grad = accumulate(passage_part, recv_local, passages)
    returned_grads = lax.all_to_all(
        query_part.reshape(devices, capacity, -1),
        ("pb", "pa"),
        split_axis=0,
        concat_axis=0,
        tiled=True,
    )
    query_terms = returned_grads.reshape(slots, query_len, -1)[slot_index]
    query_grad = jnp.sum(query_terms.astype(jnp.float32), axis=1)
    local_grad = head_term(query_states, query_unit, query_norm, query_grad) + head_term(
        passage_states, passage_unit, passage_norm, passage_grad
    )
    head_grad, divergence_total = lax.psum((local_grad, jnp.sum(divergence)), ("pb", "pa"))
    loss = divergence_total / (queries * devices)
    return (scores, loss, head_grad)


def radices(size):
    found = []
    if (size.bit_length() - 1) % 2:
        found.append(2)
        size //= 2
    while size > 1:
        found.append(4)
        size //= 4
    return found


def exchange_stages(outer, inner):
    stages = []
    held = 1
    stride = 1
    for radix in radices(outer):
        stages.append(("pb", stride, radix, held))
        stride *= radix
        held *= radix
    inner_radices = radices(inner)
    strides = []
    stride = 1
    for radix in inner_radices:
        strides.append(stride)
        stride *= radix
    for radix, stride in zip(inner_radices[::-1], strides[::-1]):
        stages.append(("pa", stride, radix, held))
        held *= radix
    return stages


def rank_of(stages, coordinates):
    rank = 0
    for axis, stride, radix, held in stages:
        rank = rank + (coordinates[axis] // stride) % radix * held
    return rank


def here():
    return {"pb": lax.axis_index("pb"), "pa": lax.axis_index("pa")}


class Stage:
    def __init__(self, stage, at):
        self.axis, self.stride, self.radix, self.held = stage
        self.at = at
        self.digit = (at[self.axis] // self.stride) % self.radix

    def peers(self):
        found = []
        for step in range(1, self.radix):
            other = (self.digit + step) % self.radix
            place = dict(self.at)
            place[self.axis] = self.at[self.axis] + (other - self.digit) * self.stride
            found.append((step - 1, other, (place["pb"], place["pa"])))
        return found


class Plane:
    def __init__(self, at, outer, inner):
        self.at = at
        self.held = outer
        self.radix = inner
        self.digit = at["pa"]

    def peers(self):
        found = []
        for step in range(1, self.radix):
            other = (self.digit + step) % self.radix
            found.append((step - 1, other, (self.at["pb"], other)))
        return found


def greet(stages):
    barrier = pltpu.get_barrier_semaphore()
    count = 0
    for stage in stages:
        for _, _, device in stage.peers():
            pl.semaphore_signal(barrier, inc=1, device_id=device, device_id_type=MESH)
            count += 1
    return barrier, count


def send(source, target, send_sem, recv_sem, device):
    copy = pltpu.make_async_remote_copy(
        src_ref=source,
        dst_ref=target,
        send_sem=send_sem,
        recv_sem=recv_sem,
        device_id=device,
        device_id_type=MESH,
    )
    copy.start()
    return copy


def gather_step(stage, rank, ref, unit, send_sems, recv_sems, base):
    first = rank // stage.held * stage.held * unit
    block = ref.at[pl.ds(first, stage.held * unit)]
    return [
        send(block, block, send_sems.at[base + slot], recv_sems.at[base + slot], device)
        for slot, _, device in stage.peers()
    ]


def reduce_step(stage, rank, ref, landing, unit, send_sems, recv_sems, base):
    span = stage.held * unit
    first = rank // (stage.held * stage.radix) * (stage.radix * span)
    return [
        send(
            ref.at[pl.ds(first + other * span, span)],
            landing.at[slot],
            send_sems.at[base + slot],
            recv_sems.at[base + slot],
            device,
        )
        for slot, other, device in stage.peers()
    ]


def finish(copies):
    for copy in copies:
        copy.wait()


def normal(pre):
    return lax.rsqrt(jnp.sum(pre * pre, axis=-1, keepdims=True) + EPSILON)


def spread(values, lanes, columns):
    total = jnp.zeros((values.shape[0], LANES), values.dtype)
    for index in range(values.shape[1]):
        here_lane = lanes == columns[:, index : index + 1]
        total = total + jnp.where(here_lane, values[:, index : index + 1], 0)
    return total


def vector_rank(layout, owner, inner):
    bits = inner.bit_length() - 1
    parts = {"pb": owner >> bits, "pa": owner & (inner - 1)}
    rank = 0
    for axis, stride, radix, held in layout:
        digit = (parts[axis] >> (stride.bit_length() - 1)) & (radix - 1)
        rank = rank + digit * held
    return rank


def pair_row(pair, queries):
    return pair // queries * (2 * queries) + pair % queries


def step_kernel(
    layout,
    sizes,
    length_ref,
    query_length_ref,
    query_ref,
    head_ref,
    teacher_ref,
    owner_ref,
    local_ref,
    states_ref,
    score_ref,
    loss_ref,
    whole_ref,
    held_ref,
    pre_ref,
    query_pre_ref,
    passage_emb_ref,
    emb_ref,
    meta_ref,
    all_score_ref,
    turned_ref,
    table_ref,
    scalar_ref,
    ratio_ref,
    column_ref,
    query_part_ref,
    sent_ref,
    running_ref,
    head_part_ref,
    head_sum_ref,
    cross_ref,
    *rest,
):
    outer, inner, parts = sizes
    count = len(layout)
    landings = rest[:count]
    head_landing = rest[count]
    load_sems, table_sem, send_sems, recv_sems = rest[-4:]
    at = here()
    stages = [Stage(stage, at) for stage in layout]
    rank = rank_of(layout, at)
    length, passages, hidden = states_ref.shape
    queries, tokens, _ = query_ref.shape
    pairs = emb_ref.shape[0]
    width = head_ref.shape[1]
    rows = 2 * queries
    devices = pairs // queries
    step = length // parts
    span = step * passages

    loads = []
    for index in range(parts):
        part = pl.ds(index * step, step)
        load = pltpu.make_async_copy(states_ref.at[part], held_ref.at[part], load_sems.at[index])
        load.start()
        loads.append(load)
    plane = Plane(at, outer, inner)
    outer_stages = [stage for stage in stages if stage.axis == "pb"]
    short_stages = outer_stages + [plane]
    barrier, greeted = greet(short_stages)

    for index in range(queries):
        pre = jnp.dot(query_ref[index], head_ref[...], preferred_element_type=F32)
        query_pre_ref[index] = pre
        emb_ref[rank * queries + index] = (pre * normal(pre)).astype(BF16)
    teacher = teacher_ref[...]
    target = teacher - jnp.log(jnp.sum(jnp.exp(teacher), axis=-1, keepdims=True))
    owner_rank = vector_rank(layout, owner_ref[...], inner)
    lanes = lax.broadcasted_iota(jnp.int32, (queries, LANES), 1)
    slot = lax.broadcasted_iota(jnp.int32, local_ref.shape, 0)
    code = local_ref[...]
    for index in range(queries):
        code = code + jnp.where(slot == index, query_length_ref[index] * passages, 0)
    meta_ref[rank, 0:queries, :] = spread(target, lanes, owner_rank)
    meta_ref[rank, queries:rows, :] = spread(code.astype(F32), lanes, owner_rank)
    pl.semaphore_wait(barrier, greeted)

    def project(index, carry):
        flat = held_ref[pl.ds(index * step, step)].reshape(span, hidden)
        pre_ref[pl.ds(pl.multiple_of(index * span, 8), span), :] = jnp.dot(
            flat, head_ref[...], preferred_element_type=F32
        )
        return carry

    def passage_pre(index):
        return pre_ref[pl.ds(index, length, stride=passages), :]

    def unit_rows(group, carry):
        for index in range(4):
            pre = passage_pre(group * 4 + index)
            passage_emb_ref[group * 4 + index] = (pre * normal(pre)).astype(BF16)
        return carry

    emb_bases = []
    base = 0
    for stage in stages:
        emb_bases.append(base)
        base += stage.radix - 1

    def gather_emb(number):
        return gather_step(
            stages[number], rank, emb_ref, queries, send_sems, recv_sems, emb_bases[number]
        )

    def project_until(first, until):
        for index in range(first, until):
            loads[index].wait()
            project(index, 0)

    done = 0
    flight = gather_emb(0)
    for number, stage in enumerate(short_stages):
        meta_flight = gather_step(stage, rank, meta_ref, 1, send_sems, recv_sems, base)
        base += stage.radix - 1
        until = parts * 2 * (number + 1) // (5 * len(short_stages))
        project_until(done, until)
        done = until
        finish(meta_flight)
    for number in range(1, count - 1):
        finish(flight)
        flight = gather_emb(number)
        until = parts * (number + 1) // (count - 1) if number < count - 2 else parts
        project_until(done, until)
        done = until
    project_until(done, parts)
    lax.fori_loop(0, passages // 4, unit_rows, 0, unroll=2)

    wide = devices * rows
    table = meta_ref[...].reshape(wide, LANES)
    turned = jnp.transpose(table)
    target = turned[:devices]
    column_code = jnp.sum(
        jnp.where(lax.broadcasted_iota(jnp.int32, table.shape, 1) == rank, table, 0.0),
        axis=1,
        keepdims=True,
    ).astype(jnp.int32)
    row_code = jnp.sum(
        jnp.where(lax.broadcasted_iota(jnp.int32, turned.shape, 0) == rank, turned, 0.0),
        axis=0,
        keepdims=True,
    ).astype(jnp.int32)
    low = passages.bit_length() - 1
    column_place = lax.broadcasted_iota(jnp.int32, (wide, 1), 0)
    row_place = lax.broadcasted_iota(jnp.int32, (1, wide), 1)
    column_valid = (column_place & (rows - 1)) >= queries
    row_valid = (row_place & (rows - 1)) >= queries
    column_local = jnp.where(column_valid, column_code & (passages - 1), passages)
    row_local = jnp.where(row_valid, row_code & (passages - 1), passages)
    column_key = column_local * wide + column_place
    row_key = row_local * wide + row_place
    place = jnp.sum((row_key < column_key).astype(jnp.int32), axis=1, keepdims=True)
    chosen = place == row_place
    pair_name = (column_place >> (rows.bit_length() - 1)) * queries + (
        column_place & (queries - 1)
    )
    table_ref[0:1, :] = row_code & (passages - 1)
    table_ref[1:2, :] = row_code >> low
    table_ref[2:3, :] = jnp.clip(
        jnp.sum(jnp.where(chosen, pair_name, 0), axis=0, keepdims=True), 0, pairs - 1
    )
    table_ref[3:4, :] = jnp.clip(
        jnp.sum((column_local <= row_place).astype(jnp.int32), axis=0, keepdims=True) - 1,
        0,
        pairs - 1,
    )
    table_ref[4:5, :] = jnp.sum(jnp.where(chosen, column_local, 0), axis=0, keepdims=True)
    to_scalar = pltpu.make_async_copy(table_ref, scalar_ref, table_sem)
    to_scalar.start()
    column_ref[...] = jnp.zeros_like(column_ref)
    to_scalar.wait()

    def local_of(pair):
        return scalar_ref[0, pair_row(pair, queries) + queries]

    def forward(group, carry):
        names = [group * queries + index for index in range(queries)]
        places = [local_of(name) for name in names]
        sim = jnp.concatenate(
            [
                lax.dot_general(
                    emb_ref[name],
                    passage_emb_ref[place],
                    (((1,), (1,)), ((), ())),
                    preferred_element_type=F32,
                )
                for name, place in zip(names, places)
            ],
            axis=0,
        )
        until = jnp.concatenate(
            [jnp.full((tokens, 1), length_ref[place], jnp.int32) for place in places], axis=0
        )
        alive = jnp.concatenate(
            [
                jnp.full((tokens, 1), scalar_ref[1, pair_row(name, queries) + queries], jnp.int32)
                for name in names
            ],
            axis=0,
        )
        exponent = jnp.where(
            lax.broadcasted_iota(jnp.int32, sim.shape, 1) < until, jnp.exp(sim * (1.0 / SOFTMAX_TEMP)), 0.0
        )
        whole = jnp.sum(exponent, axis=-1, keepdims=True)
        live = (lax.broadcasted_iota(jnp.int32, whole.shape, 0) & (tokens - 1)) < alive
        ratio = (exponent * jnp.where(live, 1.0 / whole, 0.0)).astype(BF16)
        logs = jnp.where(live, SOFTMAX_TEMP * jnp.log(whole), 0.0)
        for index, name in enumerate(names):
            ratio_ref[name] = ratio[index * tokens : (index + 1) * tokens]
            column_ref[pl.ds(group * rows + index, 1), :] = jnp.broadcast_to(
                jnp.sum(logs[index * tokens : (index + 1) * tokens], axis=0, keepdims=True),
                (1, LANES),
            )
        return carry

    finish(flight)
    flight = gather_emb(count - 1)
    top = stages[count - 1]
    near = rank // top.held * top.held

    def forward_near(group, carry):
        return forward(near + group, carry)

    def forward_far(group, carry):
        return forward((near + top.held + group) % devices, carry)

    lax.fori_loop(0, top.held, forward_near, 0, unroll=4)
    finish(flight)
    lax.fori_loop(0, devices - top.held, forward_far, 0, unroll=4)

    square = (LANES, LANES)
    diagonal = lax.broadcasted_iota(jnp.int32, square, 0) == lax.broadcasted_iota(
        jnp.int32, square, 1
    )
    blocks = wide // LANES
    all_score_ref[rank] = jnp.concatenate(
        [
            jnp.sum(
                jnp.where(diagonal, column_ref[block * LANES : (block + 1) * LANES], 0.0),
                axis=0,
                keepdims=True,
            )
            for block in range(blocks)
        ],
        axis=1,
    )

    def query_side(group, carry):
        names = [group * queries + index for index in range(queries)]
        found = [
            jnp.dot(ratio_ref[name], passage_emb_ref[local_of(name)], preferred_element_type=F32)
            for name in names
        ]
        for name, value in zip(names, found):
            query_part_ref[name] = value
        return carry

    done = 0
    for number, stage in enumerate(short_stages):
        flight = gather_step(stage, rank, all_score_ref, 1, send_sems, recv_sems, base)
        base += stage.radix - 1
        until = devices * (number + 1) // len(short_stages)
        lax.fori_loop(done, until, query_side, 0, unroll=2)
        done = until
        finish(flight)

    valid = (lax.broadcasted_iota(jnp.int32, (1, wide), 1) & (rows - 1)) < queries
    target = jnp.where(valid, target, 0.0)
    scores = jnp.where(valid, all_score_ref[...].reshape(devices, wide), 0.0)
    student = jnp.exp(scores)
    student_sum = jnp.sum(student, axis=0, keepdims=True)
    share = jnp.exp(target)
    mine = lax.broadcasted_iota(jnp.int32, scores.shape, 0) == rank
    weight = jnp.sum(
        jnp.where(mine, student / student_sum - share, 0.0), axis=0, keepdims=True
    )
    for block in range(blocks):
        upright = jnp.sum(
            jnp.where(
                diagonal,
                jnp.broadcast_to(weight[:, block * LANES : (block + 1) * LANES], square),
                0.0,
            ),
            axis=1,
            keepdims=True,
        )
        column_ref[block * LANES : (block + 1) * LANES] = jnp.broadcast_to(upright, square)

    def weight_of(pair):
        return column_ref[pl.ds(pair_row(pair, queries), 1), :]

    def scale(group, carry):
        for index in range(queries):
            pair = group * queries + index
            sent_ref[pair] = (query_part_ref[pair] * weight_of(pair)).astype(BF16)
        return carry

    lax.fori_loop(0, devices, scale, 0, unroll=2)

    bases = []
    for stage in stages:
        bases.append(base)
        base += stage.radix - 1

    def reduce_start(number):
        stage = stages[number]
        return reduce_step(
            stage, rank, sent_ref, landings[number], queries, send_sems, recv_sems, bases[number]
        )

    def reduce_end(number, flight):
        finish(flight)
        stage = stages[number]
        landing = landings[number]
        first = rank // stage.held * stage.held * queries

        def add(group, carry):
            for inner_index in range(queries):
                index = group * queries + inner_index
                value = sent_ref[first + index].astype(F32)
                for slot in range(stage.radix - 1):
                    value = value + landing[slot, index].astype(F32)
                if number:
                    sent_ref[first + index] = value.astype(BF16)
                else:
                    query_part_ref[index] = value
            return carry

        lax.fori_loop(0, stage.held, add, 0)

    def passage_side(group, carry):
        places = [group * 4 + index for index in range(4)]
        names = [scalar_ref[2, place] for place in places]
        found = [
            lax.dot_general(
                ratio_ref[name], emb_ref[name], (((0,), (0,)), ((), ())), preferred_element_type=F32
            )
            * weight_of(name)
            for name in names
        ]
        grown = carry
        for place, value in zip(places, found):
            before = scalar_ref[4, jnp.maximum(place - 1, 0)]
            grown = grown * jnp.where(scalar_ref[4, place] == before, 1.0, 0.0) + value
            running_ref[place] = grown
        return grown

    def passage_grad(group, carry):
        indices = [group * 4 + index for index in range(4)]
        found = []
        for index in indices:
            last = scalar_ref[3, index]
            along = running_ref[last] * jnp.where(scalar_ref[4, last] == index, 1.0, 0.0)
            pre = passage_pre(index)
            inverse = normal(pre)
            unit = pre * inverse
            radial = jnp.sum(along * unit, axis=-1, keepdims=True)
            found.append((along - unit * radial) * inverse)
        for index, value in zip(indices, found):
            pre_ref[pl.ds(index, length, stride=passages), :] = value
        return carry

    def head_term(index, carry):
        head_sum_ref[...] += lax.dot_general(
            pre_ref[pl.ds(pl.multiple_of(index * span, 8), span), :].astype(BF16),
            held_ref[pl.ds(index * step, step)].reshape(span, hidden),
            (((0,), (0,)), ((), ())),
            preferred_element_type=F32,
        )
        return carry

    flight = reduce_start(count - 1)
    head_sum_ref[...] = jnp.zeros_like(head_sum_ref)
    total = lax.fori_loop(
        0, pairs // 8, passage_side, jnp.zeros((length, width), F32), unroll=2
    )
    reduce_end(count - 1, flight)
    for number in range(count - 2, -1, -1):
        flight = reduce_start(number)
        if number == count - 2:
            lax.fori_loop(pairs // 8, pairs // 4, passage_side, total, unroll=2)
            lax.fori_loop(0, passages // 4, passage_grad, 0)
        if number == 0:
            lax.fori_loop(0, parts, head_term, 0)
        reduce_end(number, flight)

    for index in range(queries):
        along = query_part_ref[index]
        pre = query_pre_ref[index]
        inverse = normal(pre)
        unit = pre * inverse
        radial = jnp.sum(along * unit, axis=-1, keepdims=True)
        grad = ((along - unit * radial) * inverse).astype(BF16)
        head_sum_ref[...] += lax.dot_general(
            grad, query_ref[index], (((0,), (0,)), ((), ())), preferred_element_type=F32
        )

    chunks, rows_each, _ = head_part_ref.shape
    upright = jnp.transpose(head_sum_ref[...])
    for index in range(chunks):
        head_part_ref[index] = upright[index * rows_each : (index + 1) * rows_each].astype(BF16)

    chunk = at["pa"]
    flight = [
        send(
            head_part_ref.at[other],
            head_landing.at[slot],
            send_sems.at[base + slot],
            recv_sems.at[base + slot],
            device,
        )
        for slot, other, device in plane.peers()
    ]
    base += inner - 1

    turned_ref[...] = jnp.zeros_like(turned_ref)
    turned_ref[:, 0:devices] = jnp.transpose(scores)
    own = turned_ref[pl.ds(pl.multiple_of(rank * rows, rows), rows), :][:queries]
    picked = jnp.zeros(owner_rank.shape, F32)
    for device in range(devices):
        picked = picked + jnp.where(owner_rank == device, own[:, device : device + 1], 0.0)
    score_ref[...] = picked
    loss = jnp.sum(
        jnp.sum(
            jnp.where(valid, share * (target - scores + jnp.log(student_sum)), 0.0),
            axis=0,
            keepdims=True,
        ),
        axis=1,
        keepdims=True,
    )
    loss_ref[0, 0] = (loss / pairs)[0, 0]

    finish(flight)
    value = head_part_ref[chunk].astype(F32)
    for slot in range(inner - 1):
        value = value + head_landing[slot].astype(F32)

    place = 0
    for stage in outer_stages:
        cross_ref[place + stage.digit] = value.astype(BF16)
        part = cross_ref.at[place + stage.digit]
        flight = [
            send(part, part, send_sems.at[base + slot], recv_sems.at[base + slot], device)
            for slot, _, device in stage.peers()
        ]
        base += stage.radix - 1
        finish(flight)
        value = cross_ref[place].astype(F32)
        for digit in range(1, stage.radix):
            value = value + cross_ref[place + digit].astype(F32)
        place += stage.radix

    whole_ref[chunk] = value.astype(BF16)
    part = whole_ref.at[chunk]
    flight = [
        send(part, part, send_sems.at[base + slot], recv_sems.at[base + slot], device)
        for slot, _, device in plane.peers()
    ]
    finish(flight)


def on_device_dense(
    query_states,
    passage_states,
    head,
    teacher,
    cand_owner,
    cand_local,
    query_lengths,
    passage_lengths,
):
    outer = lax.axis_size("pb")
    inner = lax.axis_size("pa")
    devices = outer * inner
    queries, tokens, hidden = query_states.shape
    passages, length, _ = passage_states.shape
    width = head.shape[1]
    pairs = queries * devices
    wide = 2 * pairs
    layout = exchange_stages(outer, inner)
    peers = outer + inner
    parts = 10 if length % 10 == 0 else 1

    vmem = pl.BlockSpec(memory_space=pltpu.VMEM)
    smem = pl.BlockSpec(memory_space=pltpu.SMEM)
    anywhere = pl.BlockSpec(memory_space=pl.ANY)
    landings = [
        pltpu.VMEM((radix - 1, held * queries, tokens, width), BF16)
        for _, _, radix, held in layout
    ]
    chunks = inner
    rows_each = hidden // chunks
    cross = sum(stage[2] for stage in layout if stage[0] == "pb")
    scores, loss, head_grad = pl.pallas_call(
        functools.partial(step_kernel, layout, (outer, inner, parts)),
        out_shape=[
            jax.ShapeDtypeStruct(teacher.shape, F32),
            jax.ShapeDtypeStruct((1, 1), F32),
            jax.ShapeDtypeStruct((chunks, rows_each, width), BF16),
        ],
        in_specs=[smem, smem, vmem, vmem, vmem, vmem, vmem, anywhere],
        out_specs=[vmem, smem, vmem],
        scratch_shapes=[
            pltpu.VMEM((length, passages, hidden), BF16),
            pltpu.VMEM(((length + 1) * passages, width), F32),
            pltpu.VMEM((queries, tokens, width), F32),
            pltpu.VMEM((passages, length, width), BF16),
            pltpu.VMEM((pairs, tokens, width), BF16),
            pltpu.VMEM((devices, 2 * queries, LANES), F32),
            pltpu.VMEM((devices, 1, wide), F32),
            pltpu.VMEM((wide, LANES), F32),
            pltpu.VMEM((8, wide), jnp.int32),
            pltpu.SMEM((8, wide), jnp.int32),
            pltpu.VMEM((pairs, tokens, length), BF16),
            pltpu.VMEM((wide, LANES), F32),
            pltpu.VMEM((pairs, tokens, width), F32),
            pltpu.VMEM((pairs, tokens, width), BF16),
            pltpu.VMEM((pairs, length, width), F32),
            pltpu.VMEM((chunks, rows_each, width), BF16),
            pltpu.VMEM((width, hidden), F32),
            pltpu.VMEM((cross, rows_each, width), BF16),
            *landings,
            pltpu.VMEM((inner - 1, rows_each, width), BF16),
            pltpu.SemaphoreType.DMA((parts,)),
            pltpu.SemaphoreType.DMA,
            pltpu.SemaphoreType.DMA((6 * peers,)),
            pltpu.SemaphoreType.DMA((6 * peers,)),
        ],
        compiler_params=pltpu.CompilerParams(
            collective_id=0, has_side_effects=True, vmem_limit_bytes=56 * 2**20
        ),
    )(
        passage_lengths,
        query_lengths,
        query_states,
        head,
        teacher,
        cand_owner,
        cand_local,
        jnp.transpose(passage_states, (1, 0, 2)),
    )
    return (scores, loss.reshape(()), head_grad.astype(F32).reshape(hidden, width))


def suits_dense(mesh, arguments):
    outer, inner = mesh.shape["pb"], mesh.shape["pa"]
    devices = outer * inner
    queries = arguments[0].shape[0]
    hidden = arguments[0].shape[2]
    return (
        arguments[4].shape[1] == devices
        and queries == LANES
        and queries // devices == 4
        and outer & (outer - 1) == 0
        and inner & (inner - 1) == 0
        and hidden % (16 * inner) == 0
        and arguments[0].shape[1] == 32
        and arguments[1].shape[0] // devices in (16, 32, 64)
        and arguments[1].shape[1] * (arguments[1].shape[0] // devices) % 8 == 0
        and arguments[2].shape[1] == LANES
    )


def solution(mesh):
    def run(*arguments):
        body = on_device_dense if suits_dense(mesh, arguments) else on_device
        return placed(mesh, body)(*arguments)

    return run


def placed(mesh, body):
    return jax.shard_map(
        body,
        mesh=mesh,
        in_specs=(
            P(("pb", "pa"), None, None),
            P(("pb", "pa"), None, None),
            P(),
            P(("pb", "pa"), None),
            P(("pb", "pa"), None),
            P(("pb", "pa"), None),
            P(("pb", "pa")),
            P(("pb", "pa")),
        ),
        out_specs=(P(("pb", "pa"), None), P(), P()),
        check_vma=False,
    )
```

```python
import functools

import jax
import jax.numpy as jnp
from jax import lax
from jax.experimental import pallas as pl
from jax.experimental.pallas import tpu as pltpu
from jax.sharding import PartitionSpec as P

MESH = pl.DeviceIdType.MESH
F32 = jnp.float32
BF16 = jnp.bfloat16
LANES = 128

SOFTMAX_TEMP = 0.05
EPSILON = 1e-06


def embed(states, head):
    flat_states = states.reshape(-1, states.shape[-1])
    projected = jnp.dot(flat_states, head, preferred_element_type=jnp.float32)
    norm_value = jnp.sqrt(jnp.sum(projected * projected, axis=-1, keepdims=True) + EPSILON)
    unit_rows = projected / norm_value
    embedded = unit_rows.astype(jnp.bfloat16).reshape(states.shape[0], states.shape[1], -1)
    return (embedded, unit_rows, norm_value)


def head_term(states, unit_rows, norm_value, grads):
    flat_states = states.reshape(unit_rows.shape[0], -1)
    along = grads.reshape(unit_rows.shape)
    radial = jnp.sum(along * unit_rows, axis=-1, keepdims=True)
    grad_pre = ((along - unit_rows * radial) / norm_value).astype(jnp.bfloat16)
    return lax.dot_general(
        flat_states, grad_pre, (((0,), (0,)), ((), ())), preferred_element_type=jnp.float32
    )


def length_mask(lengths, width_value):
    return (jnp.arange(width_value, dtype=jnp.int32)[None, :] < lengths[:, None]).astype(
        jnp.float32
    )


def pair_terms(query_rows, passage_rows, passage_token_mask):
    token_similarity = jnp.einsum(
        "sid,sjd->sij", query_rows, passage_rows, preferred_element_type=jnp.float32
    )
    exponent_terms = jnp.exp(token_similarity / SOFTMAX_TEMP) * passage_token_mask[:, None, :]
    return (exponent_terms, jnp.sum(exponent_terms, axis=-1))


def pair_scores(exponent_total, query_token_mask):
    return jnp.sum(query_token_mask * (SOFTMAX_TEMP * jnp.log(exponent_total)), axis=-1)


def pair_grads(exponent_terms, exponent_total, query_token_mask, weights, query_rows, passage_rows):
    share = (
        (weights[:, None] * query_token_mask / exponent_total)[:, :, None] * exponent_terms
    ).astype(jnp.bfloat16)
    query_part = jnp.einsum(
        "sij,sjd->sid", share, passage_rows, preferred_element_type=jnp.float32
    ).astype(jnp.bfloat16)
    passage_part = jnp.einsum(
        "sij,sid->sjd", share, query_rows, preferred_element_type=jnp.float32
    ).astype(jnp.bfloat16)
    return (query_part, passage_part)


def distill(scores, teacher):
    student_exp = jnp.exp(scores)
    student_sum = jnp.sum(student_exp, axis=-1, keepdims=True)
    teacher_exp = jnp.exp(teacher)
    teacher_sum = jnp.sum(teacher_exp, axis=-1, keepdims=True)
    target = teacher_exp / teacher_sum
    divergence = jnp.sum(
        target * (teacher - jnp.log(teacher_sum) - (scores - jnp.log(student_sum))), axis=-1
    )
    return (student_exp / student_sum - target, divergence)


def accumulate(parts, local_index, passages):
    onehot_rows = (local_index[:, None] == jnp.arange(passages, dtype=jnp.int32)[None, :]).astype(
        jnp.bfloat16
    )
    summed = jnp.einsum(
        "sp,sx->px",
        onehot_rows,
        parts.reshape(parts.shape[0], -1),
        preferred_element_type=jnp.float32,
    )
    return summed.reshape((passages,) + parts.shape[1:])


def slot_plan(owners, capacity, devices):
    hits = (owners[:, :, None] == jnp.arange(devices, dtype=jnp.int32)[None, None, :]).astype(
        jnp.int32
    )
    present = jnp.sum(hits, axis=1)
    earlier = jnp.cumsum(present, axis=0) - present
    rank_value = jnp.sum(hits * earlier[:, None, :], axis=2)
    return owners * capacity + rank_value


def on_device(
    query_states,
    passage_states,
    head,
    teacher,
    cand_owner,
    cand_local,
    query_lengths,
    passage_lengths,
):
    outer_size = lax.axis_size("pb")
    inner_size = lax.axis_size("pa")
    devices = outer_size * inner_size
    queries = query_states.shape[0]
    query_len = query_states.shape[1]
    passages = passage_states.shape[0]
    passage_len = passage_states.shape[1]
    candidates = cand_owner.shape[1]
    capacity = min(queries, max(2, 2 * queries * candidates // devices))
    slots = devices * capacity
    query_emb, query_unit, query_norm = embed(query_states, head)
    slot_index = slot_plan(cand_owner, capacity, devices)
    flat_slot = slot_index.reshape(-1)
    row_of = jnp.repeat(jnp.arange(queries, dtype=jnp.int32), candidates)
    slot_live = jnp.zeros((slots,), jnp.int32).at[flat_slot].set(1)
    slot_query = jnp.zeros((slots,), jnp.int32).at[flat_slot].set(row_of)
    slot_local = jnp.zeros((slots,), jnp.int32).at[flat_slot].set(cand_local.reshape(-1))
    passage_emb, passage_unit, passage_norm = embed(passage_states, head)
    sent_emb = query_emb.reshape(queries, -1)[slot_query]
    sent_len = query_lengths[slot_query] * slot_live
    got_emb, got_local, got_len = (
        lax.all_to_all(
            sent_emb.reshape(devices, capacity, -1),
            ("pb", "pa"),
            split_axis=0,
            concat_axis=0,
            tiled=True,
        ),
        lax.all_to_all(
            slot_local.reshape(devices, capacity),
            ("pb", "pa"),
            split_axis=0,
            concat_axis=0,
            tiled=True,
        ),
        lax.all_to_all(
            sent_len.reshape(devices, capacity),
            ("pb", "pa"),
            split_axis=0,
            concat_axis=0,
            tiled=True,
        ),
    )
    recv_emb = got_emb.reshape(slots, query_len, -1)
    recv_local = got_local.reshape(slots)
    recv_mask = length_mask(got_len.reshape(slots), query_len)
    passage_rows = passage_emb[recv_local]
    passage_token_mask = length_mask(passage_lengths[recv_local], passage_len)
    exponent_terms, exponent_total = pair_terms(recv_emb, passage_rows, passage_token_mask)
    slot_scores = pair_scores(exponent_total, recv_mask)
    returned_scores = lax.all_to_all(
        slot_scores.reshape(devices, capacity),
        ("pb", "pa"),
        split_axis=0,
        concat_axis=0,
        tiled=True,
    )
    scores = returned_scores.reshape(slots)[slot_index]
    weights, divergence = distill(scores, teacher)
    sent_weight = jnp.zeros((slots,), jnp.float32).at[flat_slot].set(weights.reshape(-1))
    recv_weight = lax.all_to_all(
        sent_weight.reshape(devices, capacity),
        ("pb", "pa"),
        split_axis=0,
        concat_axis=0,
        tiled=True,
    ).reshape(slots)
    query_part, passage_part = pair_grads(
        exponent_terms, exponent_total, recv_mask, recv_weight, recv_emb, passage_rows
    )
    passage_grad = accumulate(passage_part, recv_local, passages)
    returned_grads = lax.all_to_all(
        query_part.reshape(devices, capacity, -1),
        ("pb", "pa"),
        split_axis=0,
        concat_axis=0,
        tiled=True,
    )
    query_terms = returned_grads.reshape(slots, query_len, -1)[slot_index]
    query_grad = jnp.sum(query_terms.astype(jnp.float32), axis=1)
    local_grad = head_term(query_states, query_unit, query_norm, query_grad) + head_term(
        passage_states, passage_unit, passage_norm, passage_grad
    )
    head_grad, divergence_total = lax.psum((local_grad, jnp.sum(divergence)), ("pb", "pa"))
    loss = divergence_total / (queries * devices)
    return (scores, loss, head_grad)


def radices(size):
    found = []
    if (size.bit_length() - 1) % 2:
        found.append(2)
        size //= 2
    while size > 1:
        found.append(4)
        size //= 4
    return found


def exchange_stages(outer, inner):
    stages = []
    held = 1
    stride = 1
    for radix in radices(outer):
        stages.append(("pb", stride, radix, held))
        stride *= radix
        held *= radix
    inner_radices = radices(inner)
    strides = []
    stride = 1
    for radix in inner_radices:
        strides.append(stride)
        stride *= radix
    for radix, stride in zip(inner_radices[::-1], strides[::-1]):
        stages.append(("pa", stride, radix, held))
        held *= radix
    return stages


def rank_of(stages, coordinates):
    rank = 0
    for axis, stride, radix, held in stages:
        rank = rank + (coordinates[axis] // stride) % radix * held
    return rank


def here():
    return {"pb": lax.axis_index("pb"), "pa": lax.axis_index("pa")}


class Stage:
    def __init__(self, stage, at):
        self.axis, self.stride, self.radix, self.held = stage
        self.at = at
        self.digit = (at[self.axis] // self.stride) % self.radix

    def peers(self):
        found = []
        for step in range(1, self.radix):
            other = (self.digit + step) % self.radix
            place = dict(self.at)
            place[self.axis] = self.at[self.axis] + (other - self.digit) * self.stride
            found.append((step - 1, other, (place["pb"], place["pa"])))
        return found


class Plane:
    def __init__(self, at, outer, inner):
        self.at = at
        self.held = outer
        self.radix = inner
        self.digit = at["pa"]

    def peers(self):
        found = []
        for step in range(1, self.radix):
            other = (self.digit + step) % self.radix
            found.append((step - 1, other, (self.at["pb"], other)))
        return found


def greet(stages):
    barrier = pltpu.get_barrier_semaphore()
    count = 0
    for stage in stages:
        for _, _, device in stage.peers():
            pl.semaphore_signal(barrier, inc=1, device_id=device, device_id_type=MESH)
            count += 1
    return barrier, count


def send(source, target, send_sem, recv_sem, device):
    copy = pltpu.make_async_remote_copy(
        src_ref=source,
        dst_ref=target,
        send_sem=send_sem,
        recv_sem=recv_sem,
        device_id=device,
        device_id_type=MESH,
    )
    copy.start()
    return copy


def gather_step(stage, rank, ref, unit, send_sems, recv_sems, base):
    first = rank // stage.held * stage.held * unit
    block = ref.at[pl.ds(first, stage.held * unit)]
    return [
        send(block, block, send_sems.at[base + slot], recv_sems.at[base + slot], device)
        for slot, _, device in stage.peers()
    ]


def reduce_step(stage, rank, ref, landing, unit, send_sems, recv_sems, base):
    span = stage.held * unit
    first = rank // (stage.held * stage.radix) * (stage.radix * span)
    return [
        send(
            ref.at[pl.ds(first + other * span, span)],
            landing.at[slot],
            send_sems.at[base + slot],
            recv_sems.at[base + slot],
            device,
        )
        for slot, other, device in stage.peers()
    ]


def finish(copies):
    for copy in copies:
        copy.wait()


def normal(pre):
    return lax.rsqrt(jnp.sum(pre * pre, axis=-1, keepdims=True) + EPSILON)


def spread(values, lanes, columns):
    total = jnp.zeros((values.shape[0], LANES), values.dtype)
    for index in range(values.shape[1]):
        here_lane = lanes == columns[:, index : index + 1]
        total = total + jnp.where(here_lane, values[:, index : index + 1], 0)
    return total


def vector_rank(layout, owner, inner):
    bits = inner.bit_length() - 1
    parts = {"pb": owner >> bits, "pa": owner & (inner - 1)}
    rank = 0
    for axis, stride, radix, held in layout:
        digit = (parts[axis] >> (stride.bit_length() - 1)) & (radix - 1)
        rank = rank + digit * held
    return rank


def pair_row(pair, queries):
    return pair // queries * (2 * queries) + pair % queries


def step_kernel(
    layout,
    sizes,
    length_ref,
    query_length_ref,
    query_ref,
    head_ref,
    teacher_ref,
    owner_ref,
    local_ref,
    states_ref,
    score_ref,
    loss_ref,
    whole_ref,
    held_ref,
    pre_ref,
    query_pre_ref,
    passage_emb_ref,
    unit_ref,
    inverse_ref,
    upright_ref,
    emb_ref,
    meta_ref,
    all_score_ref,
    turned_ref,
    table_ref,
    scalar_ref,
    ratio_ref,
    column_ref,
    query_part_ref,
    sent_ref,
    running_ref,
    head_part_ref,
    head_sum_ref,
    cross_ref,
    *rest,
):
    outer, inner, parts = sizes
    count = len(layout)
    landings = rest[:count]
    head_landing = rest[count]
    load_sems, table_sem, send_sems, recv_sems = rest[-4:]
    at = here()
    stages = [Stage(stage, at) for stage in layout]
    rank = rank_of(layout, at)
    length, passages, hidden = states_ref.shape
    queries, tokens, _ = query_ref.shape
    pairs = emb_ref.shape[0]
    width = head_ref.shape[1]
    rows = 2 * queries
    devices = pairs // queries
    step = length // parts
    span = step * passages

    loads = []
    for index in range(parts):
        part = pl.ds(index * step, step)
        load = pltpu.make_async_copy(states_ref.at[part], held_ref.at[part], load_sems.at[index])
        load.start()
        loads.append(load)
    plane = Plane(at, outer, inner)
    outer_stages = [stage for stage in stages if stage.axis == "pb"]
    short_stages = outer_stages + [plane]
    barrier, greeted = greet(short_stages)

    for index in range(queries):
        pre = jnp.dot(query_ref[index], head_ref[...], preferred_element_type=F32)
        query_pre_ref[index] = pre
        emb_ref[rank * queries + index] = (pre * normal(pre)).astype(BF16)
    teacher = teacher_ref[...]
    target = teacher - jnp.log(jnp.sum(jnp.exp(teacher), axis=-1, keepdims=True))
    owner_rank = vector_rank(layout, owner_ref[...], inner)
    lanes = lax.broadcasted_iota(jnp.int32, (queries, LANES), 1)
    slot = lax.broadcasted_iota(jnp.int32, local_ref.shape, 0)
    code = local_ref[...]
    for index in range(queries):
        code = code + jnp.where(slot == index, query_length_ref[index] * passages, 0)
    meta_ref[rank, 0:queries, :] = spread(target, lanes, owner_rank)
    meta_ref[rank, queries:rows, :] = spread(code.astype(F32), lanes, owner_rank)
    pl.semaphore_wait(barrier, greeted)

    def project(index, carry):
        flat = held_ref[pl.ds(index * step, step)].reshape(span, hidden)
        pre_ref[pl.ds(pl.multiple_of(index * span, 8), span), :] = jnp.dot(
            flat, head_ref[...], preferred_element_type=F32
        )
        return carry

    def passage_pre(index):
        return pre_ref[pl.ds(index, length, stride=passages), :]

    def unit_rows(group, carry):
        for index in range(4):
            pre = passage_pre(group * 4 + index)
            inverse = normal(pre)
            unit = pre * inverse
            passage_emb_ref[group * 4 + index] = unit.astype(BF16)
            unit_ref[group * 4 + index] = unit
            inverse_ref[group * 4 + index] = jnp.broadcast_to(inverse, unit.shape)
        return carry

    emb_bases = []
    base = 0
    for stage in stages:
        emb_bases.append(base)
        base += stage.radix - 1

    def gather_emb(number):
        return gather_step(
            stages[number], rank, emb_ref, queries, send_sems, recv_sems, emb_bases[number]
        )

    def project_until(first, until):
        for index in range(first, until):
            loads[index].wait()
            project(index, 0)

    done = 0
    flight = gather_emb(0)
    for number, stage in enumerate(short_stages):
        meta_flight = gather_step(stage, rank, meta_ref, 1, send_sems, recv_sems, base)
        base += stage.radix - 1
        until = parts * 2 * (number + 1) // (5 * len(short_stages))
        project_until(done, until)
        done = until
        finish(meta_flight)
    for number in range(1, count - 1):
        finish(flight)
        flight = gather_emb(number)
        until = parts * (number + 1) // (count - 1) if number < count - 2 else parts
        project_until(done, until)
        done = until
    project_until(done, parts)
    lax.fori_loop(0, passages // 4, unit_rows, 0, unroll=2)

    wide = devices * rows
    table = meta_ref[...].reshape(wide, LANES)
    turned = jnp.transpose(table)
    target = turned[:devices]
    column_code = jnp.sum(
        jnp.where(lax.broadcasted_iota(jnp.int32, table.shape, 1) == rank, table, 0.0),
        axis=1,
        keepdims=True,
    ).astype(jnp.int32)
    row_code = jnp.sum(
        jnp.where(lax.broadcasted_iota(jnp.int32, turned.shape, 0) == rank, turned, 0.0),
        axis=0,
        keepdims=True,
    ).astype(jnp.int32)
    low = passages.bit_length() - 1
    column_place = lax.broadcasted_iota(jnp.int32, (wide, 1), 0)
    row_place = lax.broadcasted_iota(jnp.int32, (1, wide), 1)
    column_valid = (column_place & (rows - 1)) >= queries
    row_valid = (row_place & (rows - 1)) >= queries
    column_local = jnp.where(column_valid, column_code & (passages - 1), passages)
    row_local = jnp.where(row_valid, row_code & (passages - 1), passages)
    column_key = column_local * wide + column_place
    row_key = row_local * wide + row_place
    place = jnp.sum((row_key < column_key).astype(jnp.int32), axis=1, keepdims=True)
    chosen = place == row_place
    pair_name = (column_place >> (rows.bit_length() - 1)) * queries + (
        column_place & (queries - 1)
    )
    table_ref[0:1, :] = row_code & (passages - 1)
    table_ref[1:2, :] = row_code >> low
    table_ref[2:3, :] = jnp.clip(
        jnp.sum(jnp.where(chosen, pair_name, 0), axis=0, keepdims=True), 0, pairs - 1
    )
    table_ref[3:4, :] = jnp.clip(
        jnp.sum((column_local <= row_place).astype(jnp.int32), axis=0, keepdims=True) - 1,
        0,
        pairs - 1,
    )
    table_ref[4:5, :] = jnp.sum(jnp.where(chosen, column_local, 0), axis=0, keepdims=True)
    to_scalar = pltpu.make_async_copy(table_ref, scalar_ref, table_sem)
    to_scalar.start()
    column_ref[...] = jnp.zeros_like(column_ref)
    to_scalar.wait()

    def local_of(pair):
        return scalar_ref[0, pair_row(pair, queries) + queries]

    def forward(group, carry):
        names = [group * queries + index for index in range(queries)]
        places = [local_of(name) for name in names]
        sim = jnp.concatenate(
            [
                lax.dot_general(
                    emb_ref[name],
                    passage_emb_ref[place],
                    (((1,), (1,)), ((), ())),
                    preferred_element_type=F32,
                )
                for name, place in zip(names, places)
            ],
            axis=0,
        )
        until = jnp.concatenate(
            [jnp.full((tokens, 1), length_ref[place], jnp.int32) for place in places], axis=0
        )
        alive = jnp.concatenate(
            [
                jnp.full((tokens, 1), scalar_ref[1, pair_row(name, queries) + queries], jnp.int32)
                for name in names
            ],
            axis=0,
        )
        exponent = jnp.where(
            lax.broadcasted_iota(jnp.int32, sim.shape, 1) < until, jnp.exp(sim * (1.0 / SOFTMAX_TEMP)), 0.0
        )
        whole = jnp.sum(exponent, axis=-1, keepdims=True)
        live = (lax.broadcasted_iota(jnp.int32, whole.shape, 0) & (tokens - 1)) < alive
        ratio = (exponent * jnp.where(live, 1.0 / whole, 0.0)).astype(BF16)
        logs = jnp.where(live, SOFTMAX_TEMP * jnp.log(whole), 0.0)
        for index, name in enumerate(names):
            ratio_ref[name] = ratio[index * tokens : (index + 1) * tokens]
            column_ref[pl.ds(group * rows + index, 1), :] = jnp.broadcast_to(
                jnp.sum(logs[index * tokens : (index + 1) * tokens], axis=0, keepdims=True),
                (1, LANES),
            )
        return carry

    top = stages[count - 1]
    near = rank // top.held * top.held
    first_held = stages[count - 2].held
    nearest = rank // first_held * first_held

    def forward_nearest(group, carry):
        return forward(nearest + group, carry)

    def forward_near(group, carry):
        return forward(near + (nearest - near + first_held + group) % top.held, carry)

    def forward_far(group, carry):
        return forward((near + top.held + group) % devices, carry)

    lax.fori_loop(0, first_held, forward_nearest, 0, unroll=4)
    finish(flight)
    flight = gather_emb(count - 1)
    lax.fori_loop(0, top.held - first_held, forward_near, 0, unroll=4)
    finish(flight)
    lax.fori_loop(0, devices - top.held, forward_far, 0, unroll=4)

    square = (LANES, LANES)
    diagonal = lax.broadcasted_iota(jnp.int32, square, 0) == lax.broadcasted_iota(
        jnp.int32, square, 1
    )
    blocks = wide // LANES
    all_score_ref[rank] = jnp.concatenate(
        [
            jnp.sum(
                jnp.where(diagonal, column_ref[block * LANES : (block + 1) * LANES], 0.0),
                axis=0,
                keepdims=True,
            )
            for block in range(blocks)
        ],
        axis=1,
    )

    def query_side(group, carry):
        names = [group * queries + index for index in range(queries)]
        found = [
            jnp.dot(ratio_ref[name], passage_emb_ref[local_of(name)], preferred_element_type=F32)
            for name in names
        ]
        turned_ratio = jnp.transpose(
            ratio_ref[pl.ds(group * queries, queries)].reshape(queries * tokens, length)
        )
        for name, value in zip(names, found):
            query_part_ref[name] = value
        upright_ref[group] = turned_ratio
        return carry

    done = 0
    for number, stage in enumerate(short_stages):
        flight = gather_step(stage, rank, all_score_ref, 1, send_sems, recv_sems, base)
        base += stage.radix - 1
        until = devices * (number + 1) // len(short_stages)
        lax.fori_loop(done, until, query_side, 0, unroll=4)
        done = until
        finish(flight)

    valid = (lax.broadcasted_iota(jnp.int32, (1, wide), 1) & (rows - 1)) < queries
    target = jnp.where(valid, target, 0.0)
    scores = jnp.where(valid, all_score_ref[...].reshape(devices, wide), 0.0)
    student = jnp.exp(scores)
    student_sum = jnp.sum(student, axis=0, keepdims=True)
    share = jnp.exp(target)
    mine = lax.broadcasted_iota(jnp.int32, scores.shape, 0) == rank
    weight = jnp.sum(
        jnp.where(mine, student / student_sum - share, 0.0), axis=0, keepdims=True
    )
    for block in range(blocks):
        upright = jnp.sum(
            jnp.where(
                diagonal,
                jnp.broadcast_to(weight[:, block * LANES : (block + 1) * LANES], square),
                0.0,
            ),
            axis=1,
            keepdims=True,
        )
        column_ref[block * LANES : (block + 1) * LANES] = jnp.broadcast_to(upright, square)

    def weight_of(pair):
        return column_ref[pl.ds(pair_row(pair, queries), 1), :]

    def scale(group, carry):
        for index in range(queries):
            pair = group * queries + index
            sent_ref[pair] = (query_part_ref[pair] * weight_of(pair)).astype(BF16)
        return carry

    def scale_far(group, carry):
        return scale((near + top.held + group) % devices, carry)

    def scale_near(group, carry):
        return scale(near + group, carry)

    lax.fori_loop(0, devices - top.held, scale_far, 0, unroll=4)

    bases = []
    for stage in stages:
        bases.append(base)
        base += stage.radix - 1

    def reduce_start(number):
        stage = stages[number]
        return reduce_step(
            stage, rank, sent_ref, landings[number], queries, send_sems, recv_sems, bases[number]
        )

    def reduce_end(number, flight):
        finish(flight)
        stage = stages[number]
        landing = landings[number]
        first = rank // stage.held * stage.held * queries

        def add(group, carry):
            for inner_index in range(queries):
                index = group * queries + inner_index
                value = sent_ref[first + index].astype(F32)
                for slot in range(stage.radix - 1):
                    value = value + landing[slot, index].astype(F32)
                if number:
                    sent_ref[first + index] = value.astype(BF16)
                else:
                    query_part_ref[index] = value
            return carry

        lax.fori_loop(0, stage.held, add, 0)

    def placed_rows(name):
        held = emb_ref[name].astype(F32)
        return jnp.concatenate(
            [
                held * jnp.where(name % queries == index, 1.0, 0.0)
                for index in range(queries)
            ],
            axis=0,
        ).astype(BF16)

    def passage_side(group, carry):
        places = [group * 4 + index for index in range(4)]
        names = [scalar_ref[2, place] for place in places]
        found = [
            jnp.dot(upright_ref[name // queries], placed_rows(name), preferred_element_type=F32)
            * weight_of(name)
            for name in names
        ]
        grown = carry
        for place, value in zip(places, found):
            before = scalar_ref[4, jnp.maximum(place - 1, 0)]
            grown = grown * jnp.where(scalar_ref[4, place] == before, 1.0, 0.0) + value
            running_ref[place] = grown
        return grown

    def passage_grad(group, carry):
        indices = [group * 4 + index for index in range(4)]
        found = []
        for index in indices:
            last = scalar_ref[3, index]
            along = running_ref[last] * jnp.where(scalar_ref[4, last] == index, 1.0, 0.0)
            unit = unit_ref[index]
            radial = jnp.sum(along * unit, axis=-1, keepdims=True)
            found.append((along - unit * radial) * inverse_ref[index])
        for index, value in zip(indices, found):
            pre_ref[pl.ds(index, length, stride=passages), :] = value
        return carry

    def head_term(index, carry):
        head_sum_ref[...] += lax.dot_general(
            pre_ref[pl.ds(pl.multiple_of(index * span, 8), span), :].astype(BF16),
            held_ref[pl.ds(index * step, step)].reshape(span, hidden),
            (((0,), (0,)), ((), ())),
            preferred_element_type=F32,
        )
        return carry

    flight = reduce_start(count - 1)
    lax.fori_loop(0, top.held, scale_near, 0, unroll=4)
    head_sum_ref[...] = jnp.zeros_like(head_sum_ref)
    total = lax.fori_loop(
        0, pairs // 8, passage_side, jnp.zeros((length, width), F32), unroll=4
    )
    reduce_end(count - 1, flight)
    for number in range(count - 2, -1, -1):
        flight = reduce_start(number)
        if number == count - 2:
            lax.fori_loop(pairs // 8, pairs // 4, passage_side, total, unroll=4)
            lax.fori_loop(0, passages // 4, passage_grad, 0, unroll=2)
        if number == 0:
            lax.fori_loop(0, parts, head_term, 0)
        reduce_end(number, flight)

    for index in range(queries):
        along = query_part_ref[index]
        pre = query_pre_ref[index]
        inverse = normal(pre)
        unit = pre * inverse
        radial = jnp.sum(along * unit, axis=-1, keepdims=True)
        grad = ((along - unit * radial) * inverse).astype(BF16)
        head_sum_ref[...] += lax.dot_general(
            grad, query_ref[index], (((0,), (0,)), ((), ())), preferred_element_type=F32
        )

    chunks, rows_each, _ = head_part_ref.shape
    upright = jnp.transpose(head_sum_ref[...])
    for index in range(chunks):
        head_part_ref[index] = upright[index * rows_each : (index + 1) * rows_each].astype(BF16)

    chunk = at["pa"]
    flight = [
        send(
            head_part_ref.at[other],
            head_landing.at[slot],
            send_sems.at[base + slot],
            recv_sems.at[base + slot],
            device,
        )
        for slot, other, device in plane.peers()
    ]
    base += inner - 1

    turned_ref[...] = jnp.zeros_like(turned_ref)
    turned_ref[:, 0:devices] = jnp.transpose(scores)
    own = turned_ref[pl.ds(pl.multiple_of(rank * rows, rows), rows), :][:queries]
    picked = jnp.zeros(owner_rank.shape, F32)
    for device in range(devices):
        picked = picked + jnp.where(owner_rank == device, own[:, device : device + 1], 0.0)
    score_ref[...] = picked
    loss = jnp.sum(
        jnp.sum(
            jnp.where(valid, share * (target - scores + jnp.log(student_sum)), 0.0),
            axis=0,
            keepdims=True,
        ),
        axis=1,
        keepdims=True,
    )
    loss_ref[0, 0] = (loss / pairs)[0, 0]

    finish(flight)
    value = head_part_ref[chunk].astype(F32)
    for slot in range(inner - 1):
        value = value + head_landing[slot].astype(F32)

    place = 0
    for stage in outer_stages:
        cross_ref[place + stage.digit] = value.astype(BF16)
        part = cross_ref.at[place + stage.digit]
        flight = [
            send(part, part, send_sems.at[base + slot], recv_sems.at[base + slot], device)
            for slot, _, device in stage.peers()
        ]
        base += stage.radix - 1
        finish(flight)
        value = cross_ref[place].astype(F32)
        for digit in range(1, stage.radix):
            value = value + cross_ref[place + digit].astype(F32)
        place += stage.radix

    whole_ref[chunk] = value.astype(BF16)
    part = whole_ref.at[chunk]
    flight = [
        send(part, part, send_sems.at[base + slot], recv_sems.at[base + slot], device)
        for slot, _, device in plane.peers()
    ]
    finish(flight)


def widen_kernel(narrow_ref, picked_ref, sum_ref, wide_ref, score_ref, loss_ref):
    rows_each = narrow_ref.shape[1]
    for index in range(narrow_ref.shape[0]):
        wide_ref[index * rows_each : (index + 1) * rows_each, :] = narrow_ref[index].astype(F32)
    score_ref[...] = picked_ref[...]
    loss_ref[0, 0] = sum_ref[0, 0]


def on_device_dense(
    query_states,
    passage_states,
    head,
    teacher,
    cand_owner,
    cand_local,
    query_lengths,
    passage_lengths,
):
    outer = lax.axis_size("pb")
    inner = lax.axis_size("pa")
    devices = outer * inner
    queries, tokens, hidden = query_states.shape
    passages, length, _ = passage_states.shape
    width = head.shape[1]
    pairs = queries * devices
    wide = 2 * pairs
    layout = exchange_stages(outer, inner)
    peers = outer + inner
    parts = 10 if length % 10 == 0 else 1

    vmem = pl.BlockSpec(memory_space=pltpu.VMEM)
    smem = pl.BlockSpec(memory_space=pltpu.SMEM)
    anywhere = pl.BlockSpec(memory_space=pl.ANY)
    landings = [
        pltpu.VMEM((radix - 1, held * queries, tokens, width), BF16)
        for _, _, radix, held in layout
    ]
    chunks = inner
    rows_each = hidden // chunks
    cross = sum(stage[2] for stage in layout if stage[0] == "pb")
    scores, loss, head_grad = pl.pallas_call(
        functools.partial(step_kernel, layout, (outer, inner, parts)),
        out_shape=[
            jax.ShapeDtypeStruct(teacher.shape, F32),
            jax.ShapeDtypeStruct((1, 1), F32),
            jax.ShapeDtypeStruct((chunks, rows_each, width), BF16),
        ],
        in_specs=[smem, smem, vmem, vmem, vmem, vmem, vmem, anywhere],
        out_specs=[vmem, smem, vmem],
        scratch_shapes=[
            pltpu.VMEM((length, passages, hidden), BF16),
            pltpu.VMEM(((length + 1) * passages, width), F32),
            pltpu.VMEM((queries, tokens, width), F32),
            pltpu.VMEM((passages, length, width), BF16),
            pltpu.VMEM((passages, length, width), F32),
            pltpu.VMEM((passages, length, width), F32),
            pltpu.VMEM((devices, length, queries * tokens), BF16),
            pltpu.VMEM((pairs, tokens, width), BF16),
            pltpu.VMEM((devices, 2 * queries, LANES), F32),
            pltpu.VMEM((devices, 1, wide), F32),
            pltpu.VMEM((wide, LANES), F32),
            pltpu.VMEM((8, wide), jnp.int32),
            pltpu.SMEM((8, wide), jnp.int32),
            pltpu.VMEM((pairs, tokens, length), BF16),
            pltpu.VMEM((wide, LANES), F32),
            pltpu.VMEM((pairs, tokens, width), F32),
            pltpu.VMEM((pairs, tokens, width), BF16),
            pltpu.VMEM((pairs, length, width), F32),
            pltpu.VMEM((chunks, rows_each, width), BF16),
            pltpu.VMEM((width, hidden), F32),
            pltpu.VMEM((cross, rows_each, width), BF16),
            *landings,
            pltpu.VMEM((inner - 1, rows_each, width), BF16),
            pltpu.SemaphoreType.DMA((parts,)),
            pltpu.SemaphoreType.DMA,
            pltpu.SemaphoreType.DMA((6 * peers,)),
            pltpu.SemaphoreType.DMA((6 * peers,)),
        ],
        compiler_params=pltpu.CompilerParams(
            collective_id=0, has_side_effects=True, vmem_limit_bytes=56 * 2**20
        ),
    )(
        passage_lengths,
        query_lengths,
        query_states,
        head,
        teacher,
        cand_owner,
        cand_local,
        jnp.transpose(passage_states, (1, 0, 2)),
    )
    head_grad, scores, loss = pl.pallas_call(
        widen_kernel,
        out_shape=[
            jax.ShapeDtypeStruct((hidden, width), F32),
            jax.ShapeDtypeStruct(teacher.shape, F32),
            jax.ShapeDtypeStruct((1, 1), F32),
        ],
        in_specs=[vmem, vmem, smem],
        out_specs=[vmem, vmem, smem],
    )(head_grad, scores, loss)
    return (scores, loss.reshape(()), head_grad)


def suits_dense(mesh, arguments):
    outer, inner = mesh.shape["pb"], mesh.shape["pa"]
    devices = outer * inner
    queries = arguments[0].shape[0]
    hidden = arguments[0].shape[2]
    return (
        arguments[4].shape[1] == devices
        and queries == LANES
        and queries // devices == 4
        and outer & (outer - 1) == 0
        and inner & (inner - 1) == 0
        and hidden % (16 * inner) == 0
        and arguments[0].shape[1] == 32
        and arguments[1].shape[0] // devices in (16, 32, 64)
        and arguments[1].shape[1] * (arguments[1].shape[0] // devices) % 8 == 0
        and arguments[2].shape[1] == LANES
    )


def solution(mesh):
    def run(*arguments):
        body = on_device_dense if suits_dense(mesh, arguments) else on_device
        return placed(mesh, body)(*arguments)

    return run


def placed(mesh, body):
    return jax.shard_map(
        body,
        mesh=mesh,
        in_specs=(
            P(("pb", "pa"), None, None),
            P(("pb", "pa"), None, None),
            P(),
            P(("pb", "pa"), None),
            P(("pb", "pa"), None),
            P(("pb", "pa"), None),
            P(("pb", "pa")),
            P(("pb", "pa")),
        ),
        out_specs=(P(("pb", "pa"), None), P(), P()),
        check_vma=False,
    )
```

```python
import functools

import jax
import jax.numpy as jnp
from jax import lax
from jax.experimental import pallas as pl
from jax.experimental.pallas import tpu as pltpu
from jax.sharding import PartitionSpec as P

MESH = pl.DeviceIdType.MESH
F32 = jnp.float32
BF16 = jnp.bfloat16
LANES = 128

SOFTMAX_TEMP = 0.05
EPSILON = 1e-06


def embed(states, head):
    flat_states = states.reshape(-1, states.shape[-1])
    projected = jnp.dot(flat_states, head, preferred_element_type=jnp.float32)
    norm_value = jnp.sqrt(jnp.sum(projected * projected, axis=-1, keepdims=True) + EPSILON)
    unit_rows = projected / norm_value
    embedded = unit_rows.astype(jnp.bfloat16).reshape(states.shape[0], states.shape[1], -1)
    return (embedded, unit_rows, norm_value)


def head_term(states, unit_rows, norm_value, grads):
    flat_states = states.reshape(unit_rows.shape[0], -1)
    along = grads.reshape(unit_rows.shape)
    radial = jnp.sum(along * unit_rows, axis=-1, keepdims=True)
    grad_pre = ((along - unit_rows * radial) / norm_value).astype(jnp.bfloat16)
    return lax.dot_general(
        flat_states, grad_pre, (((0,), (0,)), ((), ())), preferred_element_type=jnp.float32
    )


def length_mask(lengths, width_value):
    return (jnp.arange(width_value, dtype=jnp.int32)[None, :] < lengths[:, None]).astype(
        jnp.float32
    )


def pair_terms(query_rows, passage_rows, passage_token_mask):
    token_similarity = jnp.einsum(
        "sid,sjd->sij", query_rows, passage_rows, preferred_element_type=jnp.float32
    )
    exponent_terms = jnp.exp(token_similarity / SOFTMAX_TEMP) * passage_token_mask[:, None, :]
    return (exponent_terms, jnp.sum(exponent_terms, axis=-1))


def pair_scores(exponent_total, query_token_mask):
    return jnp.sum(query_token_mask * (SOFTMAX_TEMP * jnp.log(exponent_total)), axis=-1)


def pair_grads(exponent_terms, exponent_total, query_token_mask, weights, query_rows, passage_rows):
    share = (
        (weights[:, None] * query_token_mask / exponent_total)[:, :, None] * exponent_terms
    ).astype(jnp.bfloat16)
    query_part = jnp.einsum(
        "sij,sjd->sid", share, passage_rows, preferred_element_type=jnp.float32
    ).astype(jnp.bfloat16)
    passage_part = jnp.einsum(
        "sij,sid->sjd", share, query_rows, preferred_element_type=jnp.float32
    ).astype(jnp.bfloat16)
    return (query_part, passage_part)


def distill(scores, teacher):
    student_exp = jnp.exp(scores)
    student_sum = jnp.sum(student_exp, axis=-1, keepdims=True)
    teacher_exp = jnp.exp(teacher)
    teacher_sum = jnp.sum(teacher_exp, axis=-1, keepdims=True)
    target = teacher_exp / teacher_sum
    divergence = jnp.sum(
        target * (teacher - jnp.log(teacher_sum) - (scores - jnp.log(student_sum))), axis=-1
    )
    return (student_exp / student_sum - target, divergence)


def accumulate(parts, local_index, passages):
    onehot_rows = (local_index[:, None] == jnp.arange(passages, dtype=jnp.int32)[None, :]).astype(
        jnp.bfloat16
    )
    summed = jnp.einsum(
        "sp,sx->px",
        onehot_rows,
        parts.reshape(parts.shape[0], -1),
        preferred_element_type=jnp.float32,
    )
    return summed.reshape((passages,) + parts.shape[1:])


def slot_plan(owners, capacity, devices):
    hits = (owners[:, :, None] == jnp.arange(devices, dtype=jnp.int32)[None, None, :]).astype(
        jnp.int32
    )
    present = jnp.sum(hits, axis=1)
    earlier = jnp.cumsum(present, axis=0) - present
    rank_value = jnp.sum(hits * earlier[:, None, :], axis=2)
    return owners * capacity + rank_value


def on_device(
    query_states,
    passage_states,
    head,
    teacher,
    cand_owner,
    cand_local,
    query_lengths,
    passage_lengths,
):
    outer_size = lax.axis_size("pb")
    inner_size = lax.axis_size("pa")
    devices = outer_size * inner_size
    queries = query_states.shape[0]
    query_len = query_states.shape[1]
    passages = passage_states.shape[0]
    passage_len = passage_states.shape[1]
    candidates = cand_owner.shape[1]
    capacity = min(queries, max(2, 2 * queries * candidates // devices))
    slots = devices * capacity
    query_emb, query_unit, query_norm = embed(query_states, head)
    slot_index = slot_plan(cand_owner, capacity, devices)
    flat_slot = slot_index.reshape(-1)
    row_of = jnp.repeat(jnp.arange(queries, dtype=jnp.int32), candidates)
    slot_live = jnp.zeros((slots,), jnp.int32).at[flat_slot].set(1)
    slot_query = jnp.zeros((slots,), jnp.int32).at[flat_slot].set(row_of)
    slot_local = jnp.zeros((slots,), jnp.int32).at[flat_slot].set(cand_local.reshape(-1))
    passage_emb, passage_unit, passage_norm = embed(passage_states, head)
    sent_emb = query_emb.reshape(queries, -1)[slot_query]
    sent_len = query_lengths[slot_query] * slot_live
    got_emb, got_local, got_len = (
        lax.all_to_all(
            sent_emb.reshape(devices, capacity, -1),
            ("pb", "pa"),
            split_axis=0,
            concat_axis=0,
            tiled=True,
        ),
        lax.all_to_all(
            slot_local.reshape(devices, capacity),
            ("pb", "pa"),
            split_axis=0,
            concat_axis=0,
            tiled=True,
        ),
        lax.all_to_all(
            sent_len.reshape(devices, capacity),
            ("pb", "pa"),
            split_axis=0,
            concat_axis=0,
            tiled=True,
        ),
    )
    recv_emb = got_emb.reshape(slots, query_len, -1)
    recv_local = got_local.reshape(slots)
    recv_mask = length_mask(got_len.reshape(slots), query_len)
    passage_rows = passage_emb[recv_local]
    passage_token_mask = length_mask(passage_lengths[recv_local], passage_len)
    exponent_terms, exponent_total = pair_terms(recv_emb, passage_rows, passage_token_mask)
    slot_scores = pair_scores(exponent_total, recv_mask)
    returned_scores = lax.all_to_all(
        slot_scores.reshape(devices, capacity),
        ("pb", "pa"),
        split_axis=0,
        concat_axis=0,
        tiled=True,
    )
    scores = returned_scores.reshape(slots)[slot_index]
    weights, divergence = distill(scores, teacher)
    sent_weight = jnp.zeros((slots,), jnp.float32).at[flat_slot].set(weights.reshape(-1))
    recv_weight = lax.all_to_all(
        sent_weight.reshape(devices, capacity),
        ("pb", "pa"),
        split_axis=0,
        concat_axis=0,
        tiled=True,
    ).reshape(slots)
    query_part, passage_part = pair_grads(
        exponent_terms, exponent_total, recv_mask, recv_weight, recv_emb, passage_rows
    )
    passage_grad = accumulate(passage_part, recv_local, passages)
    returned_grads = lax.all_to_all(
        query_part.reshape(devices, capacity, -1),
        ("pb", "pa"),
        split_axis=0,
        concat_axis=0,
        tiled=True,
    )
    query_terms = returned_grads.reshape(slots, query_len, -1)[slot_index]
    query_grad = jnp.sum(query_terms.astype(jnp.float32), axis=1)
    local_grad = head_term(query_states, query_unit, query_norm, query_grad) + head_term(
        passage_states, passage_unit, passage_norm, passage_grad
    )
    head_grad, divergence_total = lax.psum((local_grad, jnp.sum(divergence)), ("pb", "pa"))
    loss = divergence_total / (queries * devices)
    return (scores, loss, head_grad)


def radices(size):
    found = []
    if (size.bit_length() - 1) % 2:
        found.append(2)
        size //= 2
    while size > 1:
        found.append(4)
        size //= 4
    return found


def exchange_stages(outer, inner):
    stages = []
    held = 1
    stride = 1
    for radix in radices(outer):
        stages.append(("pb", stride, radix, held))
        stride *= radix
        held *= radix
    inner_radices = radices(inner)
    strides = []
    stride = 1
    for radix in inner_radices:
        strides.append(stride)
        stride *= radix
    for radix, stride in zip(inner_radices[::-1], strides[::-1]):
        stages.append(("pa", stride, radix, held))
        held *= radix
    return stages


def rank_of(stages, coordinates):
    rank = 0
    for axis, stride, radix, held in stages:
        rank = rank + (coordinates[axis] // stride) % radix * held
    return rank


def here():
    return {"pb": lax.axis_index("pb"), "pa": lax.axis_index("pa")}


class Stage:
    def __init__(self, stage, at):
        self.axis, self.stride, self.radix, self.held = stage
        self.at = at
        self.digit = (at[self.axis] // self.stride) % self.radix

    def peers(self):
        found = []
        for step in range(1, self.radix):
            other = (self.digit + step) % self.radix
            place = dict(self.at)
            place[self.axis] = self.at[self.axis] + (other - self.digit) * self.stride
            found.append((step - 1, other, (place["pb"], place["pa"])))
        return found


class Plane:
    def __init__(self, at, outer, inner):
        self.at = at
        self.held = outer
        self.radix = inner
        self.digit = at["pa"]

    def peers(self):
        found = []
        for step in range(1, self.radix):
            other = (self.digit + step) % self.radix
            found.append((step - 1, other, (self.at["pb"], other)))
        return found


def greet(stages):
    barrier = pltpu.get_barrier_semaphore()
    count = 0
    for stage in stages:
        for _, _, device in stage.peers():
            pl.semaphore_signal(barrier, inc=1, device_id=device, device_id_type=MESH)
            count += 1
    return barrier, count


def send(source, target, send_sem, recv_sem, device):
    copy = pltpu.make_async_remote_copy(
        src_ref=source,
        dst_ref=target,
        send_sem=send_sem,
        recv_sem=recv_sem,
        device_id=device,
        device_id_type=MESH,
    )
    copy.start()
    return copy


def gather_step(stage, rank, ref, unit, send_sems, recv_sems, base):
    first = rank // stage.held * stage.held * unit
    block = ref.at[pl.ds(first, stage.held * unit)]
    return [
        send(block, block, send_sems.at[base + slot], recv_sems.at[base + slot], device)
        for slot, _, device in stage.peers()
    ]


def reduce_step(stage, rank, ref, landing, unit, send_sems, recv_sems, base):
    span = stage.held * unit
    first = rank // (stage.held * stage.radix) * (stage.radix * span)
    return [
        send(
            ref.at[pl.ds(first + other * span, span)],
            landing.at[slot],
            send_sems.at[base + slot],
            recv_sems.at[base + slot],
            device,
        )
        for slot, other, device in stage.peers()
    ]


def finish(copies):
    for copy in copies:
        copy.wait()


def normal(pre):
    return lax.rsqrt(jnp.sum(pre * pre, axis=-1, keepdims=True) + EPSILON)


def spread(values, lanes, columns):
    total = jnp.zeros((values.shape[0], LANES), values.dtype)
    for index in range(values.shape[1]):
        here_lane = lanes == columns[:, index : index + 1]
        total = total + jnp.where(here_lane, values[:, index : index + 1], 0)
    return total


def vector_rank(layout, owner, inner):
    bits = inner.bit_length() - 1
    parts = {"pb": owner >> bits, "pa": owner & (inner - 1)}
    rank = 0
    for axis, stride, radix, held in layout:
        digit = (parts[axis] >> (stride.bit_length() - 1)) & (radix - 1)
        rank = rank + digit * held
    return rank


def pair_row(pair, queries):
    return pair // queries * (2 * queries) + pair % queries


def step_kernel(
    layout,
    sizes,
    length_ref,
    query_length_ref,
    query_ref,
    head_ref,
    teacher_ref,
    owner_ref,
    local_ref,
    states_ref,
    score_ref,
    loss_ref,
    whole_ref,
    held_ref,
    pre_ref,
    query_pre_ref,
    passage_emb_ref,
    unit_ref,
    inverse_ref,
    upright_ref,
    emb_ref,
    meta_ref,
    all_score_ref,
    turned_ref,
    table_ref,
    scalar_ref,
    ratio_ref,
    column_ref,
    query_part_ref,
    sent_ref,
    running_ref,
    head_part_ref,
    head_sum_ref,
    cross_ref,
    *rest,
):
    outer, inner, parts = sizes
    count = len(layout)
    landings = rest[:count]
    head_landing = rest[count]
    load_sems, table_sem, send_sems, recv_sems = rest[-4:]
    at = here()
    stages = [Stage(stage, at) for stage in layout]
    rank = rank_of(layout, at)
    length, passages, hidden = states_ref.shape
    queries, tokens, _ = query_ref.shape
    pairs = emb_ref.shape[0]
    width = head_ref.shape[1]
    rows = 2 * queries
    devices = pairs // queries
    step = length // parts
    span = step * passages

    loads = []
    for index in range(parts):
        part = pl.ds(index * step, step)
        load = pltpu.make_async_copy(states_ref.at[part], held_ref.at[part], load_sems.at[index])
        load.start()
        loads.append(load)
    plane = Plane(at, outer, inner)
    outer_stages = [stage for stage in stages if stage.axis == "pb"]
    short_stages = outer_stages + [plane]
    barrier, greeted = greet(short_stages)

    for index in range(queries):
        pre = jnp.dot(query_ref[index], head_ref[...], preferred_element_type=F32)
        query_pre_ref[index] = pre
        emb_ref[rank * queries + index] = (pre * normal(pre)).astype(BF16)
    teacher = teacher_ref[...]
    target = teacher - jnp.log(jnp.sum(jnp.exp(teacher), axis=-1, keepdims=True))
    owner_rank = vector_rank(layout, owner_ref[...], inner)
    lanes = lax.broadcasted_iota(jnp.int32, (queries, LANES), 1)
    slot = lax.broadcasted_iota(jnp.int32, local_ref.shape, 0)
    code = local_ref[...]
    for index in range(queries):
        code = code + jnp.where(slot == index, query_length_ref[index] * passages, 0)
    meta_ref[rank, 0:queries, :] = spread(target, lanes, owner_rank)
    meta_ref[rank, queries:rows, :] = spread(code.astype(F32), lanes, owner_rank)
    pl.semaphore_wait(barrier, greeted)

    def project(index, carry):
        flat = held_ref[pl.ds(index * step, step)].reshape(span, hidden)
        pre_ref[pl.ds(pl.multiple_of(index * span, 8), span), :] = jnp.dot(
            flat, head_ref[...], preferred_element_type=F32
        )
        return carry

    def passage_pre(index):
        return pre_ref[pl.ds(index, length, stride=passages), :]

    def unit_rows(group, carry):
        for index in range(4):
            pre = passage_pre(group * 4 + index)
            inverse = normal(pre)
            unit = pre * inverse
            passage_emb_ref[group * 4 + index] = unit.astype(BF16)
            unit_ref[group * 4 + index] = unit
            inverse_ref[group * 4 + index] = jnp.broadcast_to(inverse, unit.shape)
        return carry

    emb_bases = []
    base = 0
    for stage in stages:
        emb_bases.append(base)
        base += stage.radix - 1

    def gather_emb(number):
        return gather_step(
            stages[number], rank, emb_ref, queries, send_sems, recv_sems, emb_bases[number]
        )

    def project_until(first, until):
        for index in range(first, until):
            loads[index].wait()
            project(index, 0)

    done = 0
    flight = gather_emb(0)
    for number, stage in enumerate(short_stages):
        meta_flight = gather_step(stage, rank, meta_ref, 1, send_sems, recv_sems, base)
        base += stage.radix - 1
        until = parts * 2 * (number + 1) // (5 * len(short_stages))
        project_until(done, until)
        done = until
        finish(meta_flight)
    for number in range(1, count - 1):
        finish(flight)
        flight = gather_emb(number)
        until = parts * (number + 1) // (count - 1) if number < count - 2 else parts
        project_until(done, until)
        done = until
    project_until(done, parts)
    lax.fori_loop(0, passages // 4, unit_rows, 0, unroll=2)

    wide = devices * rows
    table = meta_ref[...].reshape(wide, LANES)
    turned = jnp.transpose(table)
    target = turned[:devices]
    column_code = jnp.sum(
        jnp.where(lax.broadcasted_iota(jnp.int32, table.shape, 1) == rank, table, 0.0),
        axis=1,
        keepdims=True,
    ).astype(jnp.int32)
    row_code = jnp.sum(
        jnp.where(lax.broadcasted_iota(jnp.int32, turned.shape, 0) == rank, turned, 0.0),
        axis=0,
        keepdims=True,
    ).astype(jnp.int32)
    low = passages.bit_length() - 1
    column_place = lax.broadcasted_iota(jnp.int32, (wide, 1), 0)
    row_place = lax.broadcasted_iota(jnp.int32, (1, wide), 1)
    column_valid = (column_place & (rows - 1)) >= queries
    row_valid = (row_place & (rows - 1)) >= queries
    column_local = jnp.where(column_valid, column_code & (passages - 1), passages)
    row_local = jnp.where(row_valid, row_code & (passages - 1), passages)
    column_key = column_local * wide + column_place
    row_key = row_local * wide + row_place
    place = jnp.sum((row_key < column_key).astype(jnp.int32), axis=1, keepdims=True)
    chosen = place == row_place
    pair_name = (column_place >> (rows.bit_length() - 1)) * queries + (
        column_place & (queries - 1)
    )
    table_ref[0:1, :] = row_code & (passages - 1)
    table_ref[1:2, :] = row_code >> low
    table_ref[2:3, :] = jnp.clip(
        jnp.sum(jnp.where(chosen, pair_name, 0), axis=0, keepdims=True), 0, pairs - 1
    )
    table_ref[3:4, :] = jnp.clip(
        jnp.sum((column_local <= row_place).astype(jnp.int32), axis=0, keepdims=True) - 1,
        0,
        pairs - 1,
    )
    table_ref[4:5, :] = jnp.sum(jnp.where(chosen, column_local, 0), axis=0, keepdims=True)
    to_scalar = pltpu.make_async_copy(table_ref, scalar_ref, table_sem)
    to_scalar.start()
    column_ref[...] = jnp.zeros_like(column_ref)
    to_scalar.wait()

    def local_of(pair):
        return scalar_ref[0, pair_row(pair, queries) + queries]

    def forward(group, carry):
        names = [group * queries + index for index in range(queries)]
        places = [local_of(name) for name in names]
        sim = jnp.concatenate(
            [
                lax.dot_general(
                    emb_ref[name],
                    passage_emb_ref[place],
                    (((1,), (1,)), ((), ())),
                    preferred_element_type=F32,
                )
                for name, place in zip(names, places)
            ],
            axis=0,
        )
        until = jnp.concatenate(
            [jnp.full((tokens, length), length_ref[place], jnp.int32) for place in places],
            axis=0,
        )
        alive = jnp.concatenate(
            [
                jnp.full((tokens, 1), scalar_ref[1, pair_row(name, queries) + queries], jnp.int32)
                for name in names
            ],
            axis=0,
        )
        exponent = jnp.where(
            lax.broadcasted_iota(jnp.int32, sim.shape, 1) < until, jnp.exp(sim * (1.0 / SOFTMAX_TEMP)), 0.0
        )
        whole = jnp.sum(exponent, axis=-1, keepdims=True)
        live = (lax.broadcasted_iota(jnp.int32, whole.shape, 0) & (tokens - 1)) < alive
        ratio = (exponent * jnp.where(live, 1.0 / whole, 0.0)).astype(BF16)
        logs = jnp.where(live, SOFTMAX_TEMP * jnp.log(whole), 0.0)
        for index, name in enumerate(names):
            ratio_ref[name] = ratio[index * tokens : (index + 1) * tokens]
            column_ref[pl.ds(group * rows + index, 1), :] = jnp.broadcast_to(
                jnp.sum(logs[index * tokens : (index + 1) * tokens], axis=0, keepdims=True),
                (1, LANES),
            )
        return carry

    top = stages[count - 1]
    near = rank // top.held * top.held
    first_held = stages[count - 2].held
    nearest = rank // first_held * first_held

    def forward_nearest(group, carry):
        return forward(nearest + group, carry)

    def forward_near(group, carry):
        return forward(near + (nearest - near + first_held + group) % top.held, carry)

    def forward_far(group, carry):
        return forward((near + top.held + group) % devices, carry)

    lax.fori_loop(0, first_held, forward_nearest, 0, unroll=4)
    finish(flight)
    flight = gather_emb(count - 1)
    lax.fori_loop(0, top.held - first_held, forward_near, 0, unroll=4)
    finish(flight)
    lax.fori_loop(0, devices - top.held, forward_far, 0, unroll=4)

    square = (LANES, LANES)
    diagonal = lax.broadcasted_iota(jnp.int32, square, 0) == lax.broadcasted_iota(
        jnp.int32, square, 1
    )
    blocks = wide // LANES
    all_score_ref[rank] = jnp.concatenate(
        [
            jnp.sum(
                jnp.where(diagonal, column_ref[block * LANES : (block + 1) * LANES], 0.0),
                axis=0,
                keepdims=True,
            )
            for block in range(blocks)
        ],
        axis=1,
    )

    def query_side(group, carry):
        names = [group * queries + index for index in range(queries)]
        found = [
            jnp.dot(ratio_ref[name], passage_emb_ref[local_of(name)], preferred_element_type=F32)
            for name in names
        ]
        turned_ratio = jnp.transpose(
            ratio_ref[pl.ds(group * queries, queries)].reshape(queries * tokens, length)
        )
        for name, value in zip(names, found):
            query_part_ref[name] = value
        upright_ref[group] = turned_ratio
        return carry

    done = 0
    for number, stage in enumerate(short_stages):
        flight = gather_step(stage, rank, all_score_ref, 1, send_sems, recv_sems, base)
        base += stage.radix - 1
        until = devices * (number + 1) // len(short_stages)
        lax.fori_loop(done, until, query_side, 0, unroll=4)
        done = until
        finish(flight)

    valid = (lax.broadcasted_iota(jnp.int32, (1, wide), 1) & (rows - 1)) < queries
    target = jnp.where(valid, target, 0.0)
    scores = jnp.where(valid, all_score_ref[...].reshape(devices, wide), 0.0)
    student = jnp.exp(scores)
    student_sum = jnp.sum(student, axis=0, keepdims=True)
    share = jnp.exp(target)
    mine = lax.broadcasted_iota(jnp.int32, scores.shape, 0) == rank
    weight = jnp.sum(
        jnp.where(mine, student / student_sum - share, 0.0), axis=0, keepdims=True
    )
    for block in range(blocks):
        upright = jnp.sum(
            jnp.where(
                diagonal,
                jnp.broadcast_to(weight[:, block * LANES : (block + 1) * LANES], square),
                0.0,
            ),
            axis=1,
            keepdims=True,
        )
        column_ref[block * LANES : (block + 1) * LANES] = jnp.broadcast_to(upright, square)

    def weight_of(pair):
        return column_ref[pl.ds(pair_row(pair, queries), 1), :]

    def scale(group, carry):
        found = []
        for index in range(queries):
            pair = group * queries + index
            found.append((query_part_ref[pair] * weight_of(pair)).astype(BF16))
        for index in range(queries):
            sent_ref[group * queries + index] = found[index]
        return carry

    def scale_far(group, carry):
        return scale((near + top.held + group) % devices, carry)

    def scale_near(group, carry):
        return scale(near + group, carry)

    lax.fori_loop(0, devices - top.held, scale_far, 0, unroll=4)

    bases = []
    for stage in stages:
        bases.append(base)
        base += stage.radix - 1

    def reduce_start(number):
        stage = stages[number]
        return reduce_step(
            stage, rank, sent_ref, landings[number], queries, send_sems, recv_sems, bases[number]
        )

    def reduce_end(number, flight):
        finish(flight)
        stage = stages[number]
        landing = landings[number]
        first = rank // stage.held * stage.held * queries

        def add(group, carry):
            names = pl.ds(group * queries, queries)
            value = sent_ref[pl.ds(first + group * queries, queries)].astype(F32)
            for slot in range(stage.radix - 1):
                value = value + landing[slot, names].astype(F32)
            if number:
                sent_ref[pl.ds(first + group * queries, queries)] = value.astype(BF16)
            else:
                query_part_ref[names] = value
            return carry

        lax.fori_loop(0, stage.held, add, 0, unroll=min(stage.held, 4))

    def placed_rows(name):
        held = emb_ref[name].astype(F32)
        return jnp.concatenate(
            [
                held * jnp.where(name % queries == index, 1.0, 0.0)
                for index in range(queries)
            ],
            axis=0,
        ).astype(BF16)

    def passage_side(group, carry):
        places = [group * 4 + index for index in range(4)]
        names = [scalar_ref[2, place] for place in places]
        found = [
            jnp.dot(upright_ref[name // queries], placed_rows(name), preferred_element_type=F32)
            * weight_of(name)
            for name in names
        ]
        grown = carry
        for place, value in zip(places, found):
            before = scalar_ref[4, jnp.maximum(place - 1, 0)]
            grown = grown * jnp.where(scalar_ref[4, place] == before, 1.0, 0.0) + value
            running_ref[place] = grown
        return grown

    def passage_grad(group, carry):
        indices = [group * 4 + index for index in range(4)]
        found = []
        for index in indices:
            last = scalar_ref[3, index]
            along = running_ref[last] * jnp.where(scalar_ref[4, last] == index, 1.0, 0.0)
            unit = unit_ref[index]
            radial = jnp.sum(along * unit, axis=-1, keepdims=True)
            found.append((along - unit * radial) * inverse_ref[index])
        for index, value in zip(indices, found):
            pre_ref[pl.ds(index, length, stride=passages), :] = value
        return carry

    joined = 2 if parts % 2 == 0 else 1

    def head_term(index, carry):
        head_sum_ref[...] += lax.dot_general(
            pre_ref[pl.ds(pl.multiple_of(index * joined * span, 8), joined * span), :].astype(BF16),
            held_ref[pl.ds(index * joined * step, joined * step)].reshape(joined * span, hidden),
            (((0,), (0,)), ((), ())),
            preferred_element_type=F32,
        )
        return carry

    flight = reduce_start(count - 1)
    lax.fori_loop(0, top.held, scale_near, 0, unroll=4)
    head_sum_ref[...] = jnp.zeros_like(head_sum_ref)
    total = lax.fori_loop(
        0, pairs // 8, passage_side, jnp.zeros((length, width), F32), unroll=4
    )
    reduce_end(count - 1, flight)
    for number in range(count - 2, -1, -1):
        flight = reduce_start(number)
        if number == count - 2:
            lax.fori_loop(pairs // 8, pairs // 4, passage_side, total, unroll=4)
            lax.fori_loop(0, passages // 4, passage_grad, 0, unroll=2)
        if number == 0:
            lax.fori_loop(0, parts // joined, head_term, 0)
        reduce_end(number, flight)

    flat = (queries * tokens, width)
    along = query_part_ref[0:queries].reshape(flat)
    pre = query_pre_ref[...].reshape(flat)
    inverse = normal(pre)
    unit = pre * inverse
    radial = jnp.sum(along * unit, axis=-1, keepdims=True)
    grad = ((along - unit * radial) * inverse).astype(BF16)
    head_sum_ref[...] += lax.dot_general(
        grad,
        query_ref[...].reshape(queries * tokens, hidden),
        (((0,), (0,)), ((), ())),
        preferred_element_type=F32,
    )

    chunks, rows_each, _ = head_part_ref.shape
    upright = jnp.transpose(head_sum_ref[...])
    for index in range(chunks):
        head_part_ref[index] = upright[index * rows_each : (index + 1) * rows_each].astype(BF16)

    chunk = at["pa"]
    flight = [
        send(
            head_part_ref.at[other],
            head_landing.at[slot],
            send_sems.at[base + slot],
            recv_sems.at[base + slot],
            device,
        )
        for slot, other, device in plane.peers()
    ]
    base += inner - 1

    turned_ref[...] = jnp.zeros_like(turned_ref)
    turned_ref[:, 0:devices] = jnp.transpose(scores)
    own = turned_ref[pl.ds(pl.multiple_of(rank * rows, rows), rows), :][:queries]
    picked = jnp.zeros(owner_rank.shape, F32)
    for device in range(devices):
        picked = picked + jnp.where(owner_rank == device, own[:, device : device + 1], 0.0)
    score_ref[...] = picked
    loss = jnp.sum(
        jnp.sum(
            jnp.where(valid, share * (target - scores + jnp.log(student_sum)), 0.0),
            axis=0,
            keepdims=True,
        ),
        axis=1,
        keepdims=True,
    )
    loss_ref[0, 0] = (loss / pairs)[0, 0]

    finish(flight)
    value = head_part_ref[chunk].astype(F32)
    for slot in range(inner - 1):
        value = value + head_landing[slot].astype(F32)

    place = 0
    for stage in outer_stages:
        cross_ref[place + stage.digit] = value.astype(BF16)
        part = cross_ref.at[place + stage.digit]
        flight = [
            send(part, part, send_sems.at[base + slot], recv_sems.at[base + slot], device)
            for slot, _, device in stage.peers()
        ]
        base += stage.radix - 1
        finish(flight)
        value = cross_ref[place].astype(F32)
        for digit in range(1, stage.radix):
            value = value + cross_ref[place + digit].astype(F32)
        place += stage.radix

    whole_ref[chunk] = value.astype(BF16)
    part = whole_ref.at[chunk]
    flight = [
        send(part, part, send_sems.at[base + slot], recv_sems.at[base + slot], device)
        for slot, _, device in plane.peers()
    ]
    finish(flight)


def widen_kernel(narrow_ref, picked_ref, sum_ref, wide_ref, score_ref, loss_ref):
    rows_each = narrow_ref.shape[1]
    for index in range(narrow_ref.shape[0]):
        wide_ref[index * rows_each : (index + 1) * rows_each, :] = narrow_ref[index].astype(F32)
    score_ref[...] = picked_ref[...]
    loss_ref[0, 0] = sum_ref[0, 0]


def on_device_dense(
    query_states,
    passage_states,
    head,
    teacher,
    cand_owner,
    cand_local,
    query_lengths,
    passage_lengths,
):
    outer = lax.axis_size("pb")
    inner = lax.axis_size("pa")
    devices = outer * inner
    queries, tokens, hidden = query_states.shape
    passages, length, _ = passage_states.shape
    width = head.shape[1]
    pairs = queries * devices
    wide = 2 * pairs
    layout = exchange_stages(outer, inner)
    peers = outer + inner
    parts = 10 if length % 10 == 0 else 1

    vmem = pl.BlockSpec(memory_space=pltpu.VMEM)
    smem = pl.BlockSpec(memory_space=pltpu.SMEM)
    anywhere = pl.BlockSpec(memory_space=pl.ANY)
    landings = [
        pltpu.VMEM((radix - 1, held * queries, tokens, width), BF16)
        for _, _, radix, held in layout
    ]
    chunks = inner
    rows_each = hidden // chunks
    cross = sum(stage[2] for stage in layout if stage[0] == "pb")
    scores, loss, head_grad = pl.pallas_call(
        functools.partial(step_kernel, layout, (outer, inner, parts)),
        out_shape=[
            jax.ShapeDtypeStruct(teacher.shape, F32),
            jax.ShapeDtypeStruct((1, 1), F32),
            jax.ShapeDtypeStruct((chunks, rows_each, width), BF16),
        ],
        in_specs=[smem, smem, vmem, vmem, vmem, vmem, vmem, anywhere],
        out_specs=[vmem, smem, vmem],
        scratch_shapes=[
            pltpu.VMEM((length, passages, hidden), BF16),
            pltpu.VMEM(((length + 1) * passages, width), F32),
            pltpu.VMEM((queries, tokens, width), F32),
            pltpu.VMEM((passages, length, width), BF16),
            pltpu.VMEM((passages, length, width), F32),
            pltpu.VMEM((passages, length, width), F32),
            pltpu.VMEM((devices, length, queries * tokens), BF16),
            pltpu.VMEM((pairs, tokens, width), BF16),
            pltpu.VMEM((devices, 2 * queries, LANES), F32),
            pltpu.VMEM((devices, 1, wide), F32),
            pltpu.VMEM((wide, LANES), F32),
            pltpu.VMEM((8, wide), jnp.int32),
            pltpu.SMEM((8, wide), jnp.int32),
            pltpu.VMEM((pairs, tokens, length), BF16),
            pltpu.VMEM((wide, LANES), F32),
            pltpu.VMEM((pairs, tokens, width), F32),
            pltpu.VMEM((pairs, tokens, width), BF16),
            pltpu.VMEM((pairs, length, width), F32),
            pltpu.VMEM((chunks, rows_each, width), BF16),
            pltpu.VMEM((width, hidden), F32),
            pltpu.VMEM((cross, rows_each, width), BF16),
            *landings,
            pltpu.VMEM((inner - 1, rows_each, width), BF16),
            pltpu.SemaphoreType.DMA((parts,)),
            pltpu.SemaphoreType.DMA,
            pltpu.SemaphoreType.DMA((6 * peers,)),
            pltpu.SemaphoreType.DMA((6 * peers,)),
        ],
        compiler_params=pltpu.CompilerParams(
            collective_id=0, has_side_effects=True, vmem_limit_bytes=56 * 2**20
        ),
    )(
        passage_lengths,
        query_lengths,
        query_states,
        head,
        teacher,
        cand_owner,
        cand_local,
        jnp.transpose(passage_states, (1, 0, 2)),
    )
    head_grad, scores, loss = pl.pallas_call(
        widen_kernel,
        out_shape=[
            jax.ShapeDtypeStruct((hidden, width), F32),
            jax.ShapeDtypeStruct(teacher.shape, F32),
            jax.ShapeDtypeStruct((1, 1), F32),
        ],
        in_specs=[vmem, vmem, smem],
        out_specs=[vmem, vmem, smem],
    )(head_grad, scores, loss)
    return (scores, loss.reshape(()), head_grad)


def suits_dense(mesh, arguments):
    outer, inner = mesh.shape["pb"], mesh.shape["pa"]
    devices = outer * inner
    queries = arguments[0].shape[0]
    hidden = arguments[0].shape[2]
    return (
        arguments[4].shape[1] == devices
        and queries == LANES
        and queries // devices == 4
        and outer & (outer - 1) == 0
        and inner & (inner - 1) == 0
        and hidden % (16 * inner) == 0
        and arguments[0].shape[1] == 32
        and arguments[1].shape[0] // devices in (16, 32, 64)
        and arguments[1].shape[1] * (arguments[1].shape[0] // devices) % 8 == 0
        and arguments[2].shape[1] == LANES
    )


def solution(mesh):
    def run(*arguments):
        body = on_device_dense if suits_dense(mesh, arguments) else on_device
        return placed(mesh, body)(*arguments)

    return run


def placed(mesh, body):
    return jax.shard_map(
        body,
        mesh=mesh,
        in_specs=(
            P(("pb", "pa"), None, None),
            P(("pb", "pa"), None, None),
            P(),
            P(("pb", "pa"), None),
            P(("pb", "pa"), None),
            P(("pb", "pa"), None),
            P(("pb", "pa")),
            P(("pb", "pa")),
        ),
        out_specs=(P(("pb", "pa"), None), P(), P()),
        check_vma=False,
    )
```

```python
import functools

import jax
import jax.numpy as jnp
from jax import lax
from jax.experimental import pallas as pl
from jax.experimental.pallas import tpu as pltpu
from jax.sharding import PartitionSpec as P

MESH = pl.DeviceIdType.MESH
F32 = jnp.float32
BF16 = jnp.bfloat16
LANES = 128

SOFTMAX_TEMP = 0.05
EPSILON = 1e-06


def embed(states, head):
    flat_states = states.reshape(-1, states.shape[-1])
    projected = jnp.dot(flat_states, head, preferred_element_type=jnp.float32)
    norm_value = jnp.sqrt(jnp.sum(projected * projected, axis=-1, keepdims=True) + EPSILON)
    unit_rows = projected / norm_value
    embedded = unit_rows.astype(jnp.bfloat16).reshape(states.shape[0], states.shape[1], -1)
    return (embedded, unit_rows, norm_value)


def head_term(states, unit_rows, norm_value, grads):
    flat_states = states.reshape(unit_rows.shape[0], -1)
    along = grads.reshape(unit_rows.shape)
    radial = jnp.sum(along * unit_rows, axis=-1, keepdims=True)
    grad_pre = ((along - unit_rows * radial) / norm_value).astype(jnp.bfloat16)
    return lax.dot_general(
        flat_states, grad_pre, (((0,), (0,)), ((), ())), preferred_element_type=jnp.float32
    )


def length_mask(lengths, width_value):
    return (jnp.arange(width_value, dtype=jnp.int32)[None, :] < lengths[:, None]).astype(
        jnp.float32
    )


def pair_terms(query_rows, passage_rows, passage_token_mask):
    token_similarity = jnp.einsum(
        "sid,sjd->sij", query_rows, passage_rows, preferred_element_type=jnp.float32
    )
    exponent_terms = jnp.exp(token_similarity / SOFTMAX_TEMP) * passage_token_mask[:, None, :]
    return (exponent_terms, jnp.sum(exponent_terms, axis=-1))


def pair_scores(exponent_total, query_token_mask):
    return jnp.sum(query_token_mask * (SOFTMAX_TEMP * jnp.log(exponent_total)), axis=-1)


def pair_grads(exponent_terms, exponent_total, query_token_mask, weights, query_rows, passage_rows):
    share = (
        (weights[:, None] * query_token_mask / exponent_total)[:, :, None] * exponent_terms
    ).astype(jnp.bfloat16)
    query_part = jnp.einsum(
        "sij,sjd->sid", share, passage_rows, preferred_element_type=jnp.float32
    ).astype(jnp.bfloat16)
    passage_part = jnp.einsum(
        "sij,sid->sjd", share, query_rows, preferred_element_type=jnp.float32
    ).astype(jnp.bfloat16)
    return (query_part, passage_part)


def distill(scores, teacher):
    student_exp = jnp.exp(scores)
    student_sum = jnp.sum(student_exp, axis=-1, keepdims=True)
    teacher_exp = jnp.exp(teacher)
    teacher_sum = jnp.sum(teacher_exp, axis=-1, keepdims=True)
    target = teacher_exp / teacher_sum
    divergence = jnp.sum(
        target * (teacher - jnp.log(teacher_sum) - (scores - jnp.log(student_sum))), axis=-1
    )
    return (student_exp / student_sum - target, divergence)


def accumulate(parts, local_index, passages):
    onehot_rows = (local_index[:, None] == jnp.arange(passages, dtype=jnp.int32)[None, :]).astype(
        jnp.bfloat16
    )
    summed = jnp.einsum(
        "sp,sx->px",
        onehot_rows,
        parts.reshape(parts.shape[0], -1),
        preferred_element_type=jnp.float32,
    )
    return summed.reshape((passages,) + parts.shape[1:])


def slot_plan(owners, capacity, devices):
    hits = (owners[:, :, None] == jnp.arange(devices, dtype=jnp.int32)[None, None, :]).astype(
        jnp.int32
    )
    present = jnp.sum(hits, axis=1)
    earlier = jnp.cumsum(present, axis=0) - present
    rank_value = jnp.sum(hits * earlier[:, None, :], axis=2)
    return owners * capacity + rank_value


def on_device(
    query_states,
    passage_states,
    head,
    teacher,
    cand_owner,
    cand_local,
    query_lengths,
    passage_lengths,
):
    outer_size = lax.axis_size("pb")
    inner_size = lax.axis_size("pa")
    devices = outer_size * inner_size
    queries = query_states.shape[0]
    query_len = query_states.shape[1]
    passages = passage_states.shape[0]
    passage_len = passage_states.shape[1]
    candidates = cand_owner.shape[1]
    capacity = min(queries, max(2, 2 * queries * candidates // devices))
    slots = devices * capacity
    query_emb, query_unit, query_norm = embed(query_states, head)
    slot_index = slot_plan(cand_owner, capacity, devices)
    flat_slot = slot_index.reshape(-1)
    row_of = jnp.repeat(jnp.arange(queries, dtype=jnp.int32), candidates)
    slot_live = jnp.zeros((slots,), jnp.int32).at[flat_slot].set(1)
    slot_query = jnp.zeros((slots,), jnp.int32).at[flat_slot].set(row_of)
    slot_local = jnp.zeros((slots,), jnp.int32).at[flat_slot].set(cand_local.reshape(-1))
    passage_emb, passage_unit, passage_norm = embed(passage_states, head)
    sent_emb = query_emb.reshape(queries, -1)[slot_query]
    sent_len = query_lengths[slot_query] * slot_live
    got_emb, got_local, got_len = (
        lax.all_to_all(
            sent_emb.reshape(devices, capacity, -1),
            ("pb", "pa"),
            split_axis=0,
            concat_axis=0,
            tiled=True,
        ),
        lax.all_to_all(
            slot_local.reshape(devices, capacity),
            ("pb", "pa"),
            split_axis=0,
            concat_axis=0,
            tiled=True,
        ),
        lax.all_to_all(
            sent_len.reshape(devices, capacity),
            ("pb", "pa"),
            split_axis=0,
            concat_axis=0,
            tiled=True,
        ),
    )
    recv_emb = got_emb.reshape(slots, query_len, -1)
    recv_local = got_local.reshape(slots)
    recv_mask = length_mask(got_len.reshape(slots), query_len)
    passage_rows = passage_emb[recv_local]
    passage_token_mask = length_mask(passage_lengths[recv_local], passage_len)
    exponent_terms, exponent_total = pair_terms(recv_emb, passage_rows, passage_token_mask)
    slot_scores = pair_scores(exponent_total, recv_mask)
    returned_scores = lax.all_to_all(
        slot_scores.reshape(devices, capacity),
        ("pb", "pa"),
        split_axis=0,
        concat_axis=0,
        tiled=True,
    )
    scores = returned_scores.reshape(slots)[slot_index]
    weights, divergence = distill(scores, teacher)
    sent_weight = jnp.zeros((slots,), jnp.float32).at[flat_slot].set(weights.reshape(-1))
    recv_weight = lax.all_to_all(
        sent_weight.reshape(devices, capacity),
        ("pb", "pa"),
        split_axis=0,
        concat_axis=0,
        tiled=True,
    ).reshape(slots)
    query_part, passage_part = pair_grads(
        exponent_terms, exponent_total, recv_mask, recv_weight, recv_emb, passage_rows
    )
    passage_grad = accumulate(passage_part, recv_local, passages)
    returned_grads = lax.all_to_all(
        query_part.reshape(devices, capacity, -1),
        ("pb", "pa"),
        split_axis=0,
        concat_axis=0,
        tiled=True,
    )
    query_terms = returned_grads.reshape(slots, query_len, -1)[slot_index]
    query_grad = jnp.sum(query_terms.astype(jnp.float32), axis=1)
    local_grad = head_term(query_states, query_unit, query_norm, query_grad) + head_term(
        passage_states, passage_unit, passage_norm, passage_grad
    )
    head_grad, divergence_total = lax.psum((local_grad, jnp.sum(divergence)), ("pb", "pa"))
    loss = divergence_total / (queries * devices)
    return (scores, loss, head_grad)


def radices(size):
    found = []
    if (size.bit_length() - 1) % 2:
        found.append(2)
        size //= 2
    while size > 1:
        found.append(4)
        size //= 4
    return found


def exchange_stages(outer, inner):
    stages = []
    held = 1
    stride = 1
    for radix in radices(outer):
        stages.append(("pb", stride, radix, held))
        stride *= radix
        held *= radix
    inner_radices = radices(inner)
    strides = []
    stride = 1
    for radix in inner_radices:
        strides.append(stride)
        stride *= radix
    for radix, stride in zip(inner_radices[::-1], strides[::-1]):
        stages.append(("pa", stride, radix, held))
        held *= radix
    return stages


def rank_of(stages, coordinates):
    rank = 0
    for axis, stride, radix, held in stages:
        rank = rank + (coordinates[axis] // stride) % radix * held
    return rank


def here():
    return {"pb": lax.axis_index("pb"), "pa": lax.axis_index("pa")}


class Stage:
    def __init__(self, stage, at):
        self.axis, self.stride, self.radix, self.held = stage
        self.at = at
        self.digit = (at[self.axis] // self.stride) % self.radix

    def peers(self):
        found = []
        for step in range(1, self.radix):
            other = (self.digit + step) % self.radix
            place = dict(self.at)
            place[self.axis] = self.at[self.axis] + (other - self.digit) * self.stride
            found.append((step - 1, other, (place["pb"], place["pa"])))
        return found


class Plane:
    def __init__(self, at, outer, inner):
        self.at = at
        self.held = outer
        self.radix = inner
        self.digit = at["pa"]

    def peers(self):
        found = []
        for step in range(1, self.radix):
            other = (self.digit + step) % self.radix
            found.append((step - 1, other, (self.at["pb"], other)))
        return found


def greet(stages):
    barrier = pltpu.get_barrier_semaphore()
    count = 0
    for stage in stages:
        for _, _, device in stage.peers():
            pl.semaphore_signal(barrier, inc=1, device_id=device, device_id_type=MESH)
            count += 1
    return barrier, count


def send(source, target, send_sem, recv_sem, device):
    copy = pltpu.make_async_remote_copy(
        src_ref=source,
        dst_ref=target,
        send_sem=send_sem,
        recv_sem=recv_sem,
        device_id=device,
        device_id_type=MESH,
    )
    copy.start()
    return copy


def gather_step(stage, rank, ref, unit, send_sems, recv_sems, base):
    first = rank // stage.held * stage.held * unit
    block = ref.at[pl.ds(first, stage.held * unit)]
    return [
        send(block, block, send_sems.at[base + slot], recv_sems.at[base + slot], device)
        for slot, _, device in stage.peers()
    ]


def reduce_step(stage, rank, ref, landing, unit, send_sems, recv_sems, base):
    span = stage.held * unit
    first = rank // (stage.held * stage.radix) * (stage.radix * span)
    return [
        send(
            ref.at[pl.ds(first + other * span, span)],
            landing.at[slot],
            send_sems.at[base + slot],
            recv_sems.at[base + slot],
            device,
        )
        for slot, other, device in stage.peers()
    ]


def finish(copies):
    for copy in copies:
        copy.wait()


def normal(pre):
    return lax.rsqrt(jnp.sum(pre * pre, axis=-1, keepdims=True) + EPSILON)


def spread(values, lanes, columns):
    total = jnp.zeros((values.shape[0], LANES), values.dtype)
    for index in range(values.shape[1]):
        here_lane = lanes == columns[:, index : index + 1]
        total = total + jnp.where(here_lane, values[:, index : index + 1], 0)
    return total


def vector_rank(layout, owner, inner):
    bits = inner.bit_length() - 1
    parts = {"pb": owner >> bits, "pa": owner & (inner - 1)}
    rank = 0
    for axis, stride, radix, held in layout:
        digit = (parts[axis] >> (stride.bit_length() - 1)) & (radix - 1)
        rank = rank + digit * held
    return rank


def pair_row(pair, queries):
    return pair // queries * (2 * queries) + pair % queries


def step_kernel(
    layout,
    sizes,
    length_ref,
    query_length_ref,
    query_ref,
    head_ref,
    teacher_ref,
    owner_ref,
    local_ref,
    states_ref,
    score_ref,
    loss_ref,
    whole_ref,
    held_ref,
    pre_ref,
    query_pre_ref,
    passage_emb_ref,
    unit_ref,
    inverse_ref,
    upright_ref,
    emb_ref,
    meta_ref,
    all_score_ref,
    turned_ref,
    table_ref,
    scalar_ref,
    ratio_ref,
    column_ref,
    query_part_ref,
    sent_ref,
    running_ref,
    head_part_ref,
    head_sum_ref,
    cross_ref,
    *rest,
):
    outer, inner, parts = sizes
    count = len(layout)
    landings = rest[:count]
    head_landing = rest[count]
    load_sems, table_sem, send_sems, recv_sems = rest[-4:]
    at = here()
    stages = [Stage(stage, at) for stage in layout]
    rank = rank_of(layout, at)
    length, passages, hidden = states_ref.shape
    queries, tokens, _ = query_ref.shape
    pairs = emb_ref.shape[0]
    width = head_ref.shape[1]
    rows = 2 * queries
    devices = pairs // queries
    step = length // parts
    span = step * passages

    loads = []
    for index in range(parts):
        part = pl.ds(index * step, step)
        load = pltpu.make_async_copy(states_ref.at[part], held_ref.at[part], load_sems.at[index])
        load.start()
        loads.append(load)
    plane = Plane(at, outer, inner)
    outer_stages = [stage for stage in stages if stage.axis == "pb"]
    short_stages = outer_stages + [plane]
    barrier, greeted = greet(short_stages)

    for index in range(queries):
        pre = jnp.dot(query_ref[index], head_ref[...], preferred_element_type=F32)
        query_pre_ref[index] = pre
        emb_ref[rank * queries + index] = (pre * normal(pre)).astype(BF16)
    teacher = teacher_ref[...]
    target = teacher - jnp.log(jnp.sum(jnp.exp(teacher), axis=-1, keepdims=True))
    owner_rank = vector_rank(layout, owner_ref[...], inner)
    lanes = lax.broadcasted_iota(jnp.int32, (queries, LANES), 1)
    slot = lax.broadcasted_iota(jnp.int32, local_ref.shape, 0)
    code = local_ref[...]
    for index in range(queries):
        code = code + jnp.where(slot == index, query_length_ref[index] * passages, 0)
    meta_ref[rank, 0:queries, :] = spread(target, lanes, owner_rank)
    meta_ref[rank, queries:rows, :] = spread(code.astype(F32), lanes, owner_rank)
    pl.semaphore_wait(barrier, greeted)

    def project(index, carry):
        flat = held_ref[pl.ds(index * step, step)].reshape(span, hidden)
        pre_ref[pl.ds(pl.multiple_of(index * span, 8), span), :] = jnp.dot(
            flat, head_ref[...], preferred_element_type=F32
        )
        return carry

    def passage_pre(index):
        return pre_ref[pl.ds(index, length, stride=passages), :]

    def unit_rows(group, carry):
        for index in range(4):
            pre = passage_pre(group * 4 + index)
            inverse = normal(pre)
            unit = pre * inverse
            passage_emb_ref[group * 4 + index] = unit.astype(BF16)
            unit_ref[group * 4 + index] = unit
            inverse_ref[group * 4 + index] = jnp.broadcast_to(inverse, unit.shape)
        return carry

    emb_bases = []
    base = 0
    for stage in stages:
        emb_bases.append(base)
        base += stage.radix - 1

    def gather_emb(number):
        return gather_step(
            stages[number], rank, emb_ref, queries, send_sems, recv_sems, emb_bases[number]
        )

    def project_until(first, until):
        for index in range(first, until):
            loads[index].wait()
            project(index, 0)

    early = stages[0]
    relay_base = base
    base += early.radix * (stages[1].radix - 1)

    def relay(digit, turn):
        block = emb_ref.at[pl.ds((rank + digit - early.digit) * queries, queries)]
        sems = relay_base + turn * (stages[1].radix - 1)
        return [
            send(block, block, send_sems.at[sems + slot], recv_sems.at[sems + slot], device)
            for slot, _, device in stages[1].peers()
        ]

    done = 0
    flight = gather_emb(0)
    relayed = relay(early.digit, 0)
    for number, stage in enumerate(short_stages):
        meta_flight = gather_step(stage, rank, meta_ref, 1, send_sems, recv_sems, base)
        base += stage.radix - 1
        until = parts * 2 * (number + 1) // (5 * len(short_stages))
        project_until(done, until)
        done = until
        finish(meta_flight)
    for number in range(1, count - 1):
        if number == 1:
            for turn, copy in enumerate(flight):
                copy.wait()
                relayed += relay((early.digit + early.radix - turn - 1) % early.radix, turn + 1)
            flight = relayed
        else:
            finish(flight)
            flight = gather_emb(number)
        until = parts * (number + 1) // (count - 1) if number < count - 2 else parts
        project_until(done, until)
        done = until
    project_until(done, parts)
    lax.fori_loop(0, passages // 4, unit_rows, 0, unroll=2)

    wide = devices * rows
    table = meta_ref[...].reshape(wide, LANES)
    turned = jnp.transpose(table)
    target = turned[:devices]
    column_code = jnp.sum(
        jnp.where(lax.broadcasted_iota(jnp.int32, table.shape, 1) == rank, table, 0.0),
        axis=1,
        keepdims=True,
    ).astype(jnp.int32)
    row_code = jnp.sum(
        jnp.where(lax.broadcasted_iota(jnp.int32, turned.shape, 0) == rank, turned, 0.0),
        axis=0,
        keepdims=True,
    ).astype(jnp.int32)
    low = passages.bit_length() - 1
    column_place = lax.broadcasted_iota(jnp.int32, (wide, 1), 0)
    row_place = lax.broadcasted_iota(jnp.int32, (1, wide), 1)
    column_valid = (column_place & (rows - 1)) >= queries
    row_valid = (row_place & (rows - 1)) >= queries
    column_local = jnp.where(column_valid, column_code & (passages - 1), passages)
    row_local = jnp.where(row_valid, row_code & (passages - 1), passages)
    column_key = column_local * wide + column_place
    row_key = row_local * wide + row_place
    place = jnp.sum((row_key < column_key).astype(jnp.int32), axis=1, keepdims=True)
    chosen = place == row_place
    pair_name = (column_place >> (rows.bit_length() - 1)) * queries + (
        column_place & (queries - 1)
    )
    table_ref[0:1, :] = row_code & (passages - 1)
    table_ref[1:2, :] = row_code >> low
    table_ref[2:3, :] = jnp.clip(
        jnp.sum(jnp.where(chosen, pair_name, 0), axis=0, keepdims=True), 0, pairs - 1
    )
    table_ref[3:4, :] = jnp.clip(
        jnp.sum((column_local <= row_place).astype(jnp.int32), axis=0, keepdims=True) - 1,
        0,
        pairs - 1,
    )
    table_ref[4:5, :] = jnp.sum(jnp.where(chosen, column_local, 0), axis=0, keepdims=True)
    to_scalar = pltpu.make_async_copy(table_ref, scalar_ref, table_sem)
    to_scalar.start()
    column_ref[...] = jnp.zeros_like(column_ref)
    to_scalar.wait()

    def local_of(pair):
        return scalar_ref[0, pair_row(pair, queries) + queries]

    def forward(group, carry):
        names = [group * queries + index for index in range(queries)]
        places = [local_of(name) for name in names]
        sim = jnp.concatenate(
            [
                lax.dot_general(
                    emb_ref[name],
                    passage_emb_ref[place],
                    (((1,), (1,)), ((), ())),
                    preferred_element_type=F32,
                )
                for name, place in zip(names, places)
            ],
            axis=0,
        )
        until = jnp.concatenate(
            [jnp.full((tokens, length), length_ref[place], jnp.int32) for place in places],
            axis=0,
        )
        alive = jnp.concatenate(
            [
                jnp.full((tokens, 1), scalar_ref[1, pair_row(name, queries) + queries], jnp.int32)
                for name in names
            ],
            axis=0,
        )
        exponent = jnp.where(
            lax.broadcasted_iota(jnp.int32, sim.shape, 1) < until, jnp.exp(sim * (1.0 / SOFTMAX_TEMP)), 0.0
        )
        whole = jnp.sum(exponent, axis=-1, keepdims=True)
        live = (lax.broadcasted_iota(jnp.int32, whole.shape, 0) & (tokens - 1)) < alive
        ratio = (exponent * jnp.where(live, 1.0 / whole, 0.0)).astype(BF16)
        logs = jnp.where(live, SOFTMAX_TEMP * jnp.log(whole), 0.0)
        for index, name in enumerate(names):
            ratio_ref[name] = ratio[index * tokens : (index + 1) * tokens]
            column_ref[pl.ds(group * rows + index, 1), :] = jnp.broadcast_to(
                jnp.sum(logs[index * tokens : (index + 1) * tokens], axis=0, keepdims=True),
                (1, LANES),
            )
        return carry

    top = stages[count - 1]
    near = rank // top.held * top.held
    first_held = stages[count - 2].held
    nearest = rank // first_held * first_held

    def forward_nearest(group, carry):
        return forward(nearest + group, carry)

    def forward_near(group, carry):
        return forward(near + (nearest - near + first_held + group) % top.held, carry)

    def forward_far(group, carry):
        return forward((near + top.held + group) % devices, carry)

    lax.fori_loop(0, first_held, forward_nearest, 0, unroll=4)
    finish(flight)
    flight = gather_emb(count - 1)
    lax.fori_loop(0, top.held - first_held, forward_near, 0, unroll=4)
    finish(flight)
    lax.fori_loop(0, devices - top.held, forward_far, 0, unroll=4)

    square = (LANES, LANES)
    diagonal = lax.broadcasted_iota(jnp.int32, square, 0) == lax.broadcasted_iota(
        jnp.int32, square, 1
    )
    blocks = wide // LANES
    all_score_ref[rank] = jnp.concatenate(
        [
            jnp.sum(
                jnp.where(diagonal, column_ref[block * LANES : (block + 1) * LANES], 0.0),
                axis=0,
                keepdims=True,
            )
            for block in range(blocks)
        ],
        axis=1,
    )

    def query_side(group, carry):
        names = [group * queries + index for index in range(queries)]
        found = [
            jnp.dot(ratio_ref[name], passage_emb_ref[local_of(name)], preferred_element_type=F32)
            for name in names
        ]
        turned_ratio = jnp.transpose(
            ratio_ref[pl.ds(group * queries, queries)].reshape(queries * tokens, length)
        )
        for name, value in zip(names, found):
            query_part_ref[name] = value
        upright_ref[group] = turned_ratio
        return carry

    done = 0
    for number, stage in enumerate(short_stages):
        flight = gather_step(stage, rank, all_score_ref, 1, send_sems, recv_sems, base)
        base += stage.radix - 1
        until = devices * (number + 1) // len(short_stages)
        lax.fori_loop(done, until, query_side, 0, unroll=4)
        done = until
        finish(flight)

    valid = (lax.broadcasted_iota(jnp.int32, (1, wide), 1) & (rows - 1)) < queries
    target = jnp.where(valid, target, 0.0)
    scores = jnp.where(valid, all_score_ref[...].reshape(devices, wide), 0.0)
    student = jnp.exp(scores)
    student_sum = jnp.sum(student, axis=0, keepdims=True)
    share = jnp.exp(target)
    mine = lax.broadcasted_iota(jnp.int32, scores.shape, 0) == rank
    weight = jnp.sum(
        jnp.where(mine, student / student_sum - share, 0.0), axis=0, keepdims=True
    )
    for block in range(blocks):
        upright = jnp.sum(
            jnp.where(
                diagonal,
                jnp.broadcast_to(weight[:, block * LANES : (block + 1) * LANES], square),
                0.0,
            ),
            axis=1,
            keepdims=True,
        )
        column_ref[block * LANES : (block + 1) * LANES] = jnp.broadcast_to(upright, square)

    def weight_of(pair):
        return column_ref[pl.ds(pair_row(pair, queries), 1), :]

    def scale(group, carry):
        found = []
        for index in range(queries):
            pair = group * queries + index
            found.append((query_part_ref[pair] * weight_of(pair)).astype(BF16))
        for index in range(queries):
            sent_ref[group * queries + index] = found[index]
        return carry

    def scale_far(group, carry):
        return scale((near + top.held + group) % devices, carry)

    def scale_near(group, carry):
        return scale(near + group, carry)

    lax.fori_loop(0, devices - top.held, scale_far, 0, unroll=4)

    bases = []
    for stage in stages:
        bases.append(base)
        base += stage.radix - 1

    def reduce_start(number):
        stage = stages[number]
        return reduce_step(
            stage, rank, sent_ref, landings[number], queries, send_sems, recv_sems, bases[number]
        )

    def reduce_end(number, flight):
        finish(flight)
        stage = stages[number]
        landing = landings[number]
        first = rank // stage.held * stage.held * queries

        def add(group, carry):
            names = pl.ds(group * queries, queries)
            value = sent_ref[pl.ds(first + group * queries, queries)].astype(F32)
            for slot in range(stage.radix - 1):
                value = value + landing[slot, names].astype(F32)
            if number:
                sent_ref[pl.ds(first + group * queries, queries)] = value.astype(BF16)
            else:
                query_part_ref[names] = value
            return carry

        lax.fori_loop(0, stage.held, add, 0, unroll=min(stage.held, 4))

    def placed_rows(name):
        held = emb_ref[name].astype(F32)
        return jnp.concatenate(
            [
                held * jnp.where(name % queries == index, 1.0, 0.0)
                for index in range(queries)
            ],
            axis=0,
        ).astype(BF16)

    def passage_side(group, carry):
        places = [group * 4 + index for index in range(4)]
        names = [scalar_ref[2, place] for place in places]
        found = [
            jnp.dot(upright_ref[name // queries], placed_rows(name), preferred_element_type=F32)
            * weight_of(name)
            for name in names
        ]
        grown = carry
        for place, value in zip(places, found):
            before = scalar_ref[4, jnp.maximum(place - 1, 0)]
            grown = grown * jnp.where(scalar_ref[4, place] == before, 1.0, 0.0) + value
            running_ref[place] = grown
        return grown

    def passage_grad(group, carry):
        indices = [group * 4 + index for index in range(4)]
        found = []
        for index in indices:
            last = scalar_ref[3, index]
            along = running_ref[last] * jnp.where(scalar_ref[4, last] == index, 1.0, 0.0)
            unit = unit_ref[index]
            radial = jnp.sum(along * unit, axis=-1, keepdims=True)
            found.append((along - unit * radial) * inverse_ref[index])
        for index, value in zip(indices, found):
            pre_ref[pl.ds(index, length, stride=passages), :] = value
        return carry

    joined = 2 if parts % 2 == 0 else 1

    def head_term(index, carry):
        head_sum_ref[...] += lax.dot_general(
            pre_ref[pl.ds(pl.multiple_of(index * joined * span, 8), joined * span), :].astype(BF16),
            held_ref[pl.ds(index * joined * step, joined * step)].reshape(joined * span, hidden),
            (((0,), (0,)), ((), ())),
            preferred_element_type=F32,
        )
        return carry

    flight = reduce_start(count - 1)
    lax.fori_loop(0, top.held, scale_near, 0, unroll=4)
    head_sum_ref[...] = jnp.zeros_like(head_sum_ref)
    total = lax.fori_loop(
        0, pairs // 8, passage_side, jnp.zeros((length, width), F32), unroll=4
    )
    reduce_end(count - 1, flight)
    for number in range(count - 2, -1, -1):
        flight = reduce_start(number)
        if number == count - 2:
            lax.fori_loop(pairs // 8, pairs // 4, passage_side, total, unroll=4)
            lax.fori_loop(0, passages // 4, passage_grad, 0, unroll=2)
        if number == 0:
            lax.fori_loop(0, parts // joined, head_term, 0)
        reduce_end(number, flight)

    flat = (queries * tokens, width)
    along = query_part_ref[0:queries].reshape(flat)
    pre = query_pre_ref[...].reshape(flat)
    inverse = normal(pre)
    unit = pre * inverse
    radial = jnp.sum(along * unit, axis=-1, keepdims=True)
    grad = ((along - unit * radial) * inverse).astype(BF16)
    head_sum_ref[...] += lax.dot_general(
        grad,
        query_ref[...].reshape(queries * tokens, hidden),
        (((0,), (0,)), ((), ())),
        preferred_element_type=F32,
    )

    chunks, rows_each, _ = head_part_ref.shape
    upright = jnp.transpose(head_sum_ref[...])
    for index in range(chunks):
        head_part_ref[index] = upright[index * rows_each : (index + 1) * rows_each].astype(BF16)

    chunk = at["pa"]
    flight = [
        send(
            head_part_ref.at[other],
            head_landing.at[slot],
            send_sems.at[base + slot],
            recv_sems.at[base + slot],
            device,
        )
        for slot, other, device in plane.peers()
    ]
    base += inner - 1

    turned_ref[...] = jnp.zeros_like(turned_ref)
    turned_ref[:, 0:devices] = jnp.transpose(scores)
    own = turned_ref[pl.ds(pl.multiple_of(rank * rows, rows), rows), :][:queries]
    picked = jnp.zeros(owner_rank.shape, F32)
    for device in range(devices):
        picked = picked + jnp.where(owner_rank == device, own[:, device : device + 1], 0.0)
    score_ref[...] = picked
    loss = jnp.sum(
        jnp.sum(
            jnp.where(valid, share * (target - scores + jnp.log(student_sum)), 0.0),
            axis=0,
            keepdims=True,
        ),
        axis=1,
        keepdims=True,
    )
    loss_ref[0, 0] = (loss / pairs)[0, 0]

    finish(flight)
    value = head_part_ref[chunk].astype(F32)
    for slot in range(inner - 1):
        value = value + head_landing[slot].astype(F32)

    place = 0
    for stage in outer_stages:
        cross_ref[place + stage.digit] = value.astype(BF16)
        part = cross_ref.at[place + stage.digit]
        flight = [
            send(part, part, send_sems.at[base + slot], recv_sems.at[base + slot], device)
            for slot, _, device in stage.peers()
        ]
        base += stage.radix - 1
        finish(flight)
        value = cross_ref[place].astype(F32)
        for digit in range(1, stage.radix):
            value = value + cross_ref[place + digit].astype(F32)
        place += stage.radix

    whole_ref[chunk] = value.astype(BF16)
    part = whole_ref.at[chunk]
    flight = [
        send(part, part, send_sems.at[base + slot], recv_sems.at[base + slot], device)
        for slot, _, device in plane.peers()
    ]
    finish(flight)


def widen_kernel(narrow_ref, picked_ref, sum_ref, wide_ref, score_ref, loss_ref):
    rows_each = narrow_ref.shape[1]
    for index in range(narrow_ref.shape[0]):
        wide_ref[index * rows_each : (index + 1) * rows_each, :] = narrow_ref[index].astype(F32)
    score_ref[...] = picked_ref[...]
    loss_ref[0, 0] = sum_ref[0, 0]


def on_device_dense(
    query_states,
    passage_states,
    head,
    teacher,
    cand_owner,
    cand_local,
    query_lengths,
    passage_lengths,
):
    outer = lax.axis_size("pb")
    inner = lax.axis_size("pa")
    devices = outer * inner
    queries, tokens, hidden = query_states.shape
    passages, length, _ = passage_states.shape
    width = head.shape[1]
    pairs = queries * devices
    wide = 2 * pairs
    layout = exchange_stages(outer, inner)
    peers = outer + inner
    parts = 10 if length % 10 == 0 else 1

    vmem = pl.BlockSpec(memory_space=pltpu.VMEM)
    smem = pl.BlockSpec(memory_space=pltpu.SMEM)
    anywhere = pl.BlockSpec(memory_space=pl.ANY)
    landings = [
        pltpu.VMEM((radix - 1, held * queries, tokens, width), BF16)
        for _, _, radix, held in layout
    ]
    chunks = inner
    rows_each = hidden // chunks
    cross = sum(stage[2] for stage in layout if stage[0] == "pb")
    scores, loss, head_grad = pl.pallas_call(
        functools.partial(step_kernel, layout, (outer, inner, parts)),
        out_shape=[
            jax.ShapeDtypeStruct(teacher.shape, F32),
            jax.ShapeDtypeStruct((1, 1), F32),
            jax.ShapeDtypeStruct((chunks, rows_each, width), BF16),
        ],
        in_specs=[smem, smem, vmem, vmem, vmem, vmem, vmem, anywhere],
        out_specs=[vmem, smem, vmem],
        scratch_shapes=[
            pltpu.VMEM((length, passages, hidden), BF16),
            pltpu.VMEM(((length + 1) * passages, width), F32),
            pltpu.VMEM((queries, tokens, width), F32),
            pltpu.VMEM((passages, length, width), BF16),
            pltpu.VMEM((passages, length, width), F32),
            pltpu.VMEM((passages, length, width), F32),
            pltpu.VMEM((devices, length, queries * tokens), BF16),
            pltpu.VMEM((pairs, tokens, width), BF16),
            pltpu.VMEM((devices, 2 * queries, LANES), F32),
            pltpu.VMEM((devices, 1, wide), F32),
            pltpu.VMEM((wide, LANES), F32),
            pltpu.VMEM((8, wide), jnp.int32),
            pltpu.SMEM((8, wide), jnp.int32),
            pltpu.VMEM((pairs, tokens, length), BF16),
            pltpu.VMEM((wide, LANES), F32),
            pltpu.VMEM((pairs, tokens, width), F32),
            pltpu.VMEM((pairs, tokens, width), BF16),
            pltpu.VMEM((pairs, length, width), F32),
            pltpu.VMEM((chunks, rows_each, width), BF16),
            pltpu.VMEM((width, hidden), F32),
            pltpu.VMEM((cross, rows_each, width), BF16),
            *landings,
            pltpu.VMEM((inner - 1, rows_each, width), BF16),
            pltpu.SemaphoreType.DMA((parts,)),
            pltpu.SemaphoreType.DMA,
            pltpu.SemaphoreType.DMA((6 * peers,)),
            pltpu.SemaphoreType.DMA((6 * peers,)),
        ],
        compiler_params=pltpu.CompilerParams(
            collective_id=0, has_side_effects=True, vmem_limit_bytes=56 * 2**20
        ),
    )(
        passage_lengths,
        query_lengths,
        query_states,
        head,
        teacher,
        cand_owner,
        cand_local,
        jnp.transpose(passage_states, (1, 0, 2)),
    )
    head_grad, scores, loss = pl.pallas_call(
        widen_kernel,
        out_shape=[
            jax.ShapeDtypeStruct((hidden, width), F32),
            jax.ShapeDtypeStruct(teacher.shape, F32),
            jax.ShapeDtypeStruct((1, 1), F32),
        ],
        in_specs=[vmem, vmem, smem],
        out_specs=[vmem, vmem, smem],
    )(head_grad, scores, loss)
    return (scores, loss.reshape(()), head_grad)


def suits_dense(mesh, arguments):
    outer, inner = mesh.shape["pb"], mesh.shape["pa"]
    devices = outer * inner
    queries = arguments[0].shape[0]
    hidden = arguments[0].shape[2]
    return (
        arguments[4].shape[1] == devices
        and queries == LANES
        and queries // devices == 4
        and outer & (outer - 1) == 0
        and inner & (inner - 1) == 0
        and hidden % (16 * inner) == 0
        and arguments[0].shape[1] == 32
        and arguments[1].shape[0] // devices in (16, 32, 64)
        and arguments[1].shape[1] * (arguments[1].shape[0] // devices) % 8 == 0
        and arguments[2].shape[1] == LANES
    )


def solution(mesh):
    def run(*arguments):
        body = on_device_dense if suits_dense(mesh, arguments) else on_device
        return placed(mesh, body)(*arguments)

    return run


def placed(mesh, body):
    return jax.shard_map(
        body,
        mesh=mesh,
        in_specs=(
            P(("pb", "pa"), None, None),
            P(("pb", "pa"), None, None),
            P(),
            P(("pb", "pa"), None),
            P(("pb", "pa"), None),
            P(("pb", "pa"), None),
            P(("pb", "pa")),
            P(("pb", "pa")),
        ),
        out_specs=(P(("pb", "pa"), None), P(), P()),
        check_vma=False,
    )
```
